128 devices in a mesh: dp: 32 (over z, x, core), tensor: 4 (over y).
Axes of the slice: x: 4, y: 4, z: 4, core: 2. Of those that a mesh axis runs over, the one named last changes fastest.
Arguments:
- hidden_in: float32 [8192, 1152], P('dp'), may hold values from -6 to 6
- out_grad: float32 [8192, 1152], P('dp'), may hold values from -6 to 6
- segment_ids: int32 [8192], P('dp'), may hold values from 0 to 19, never falling along the last dimension, each value on 1 to 800 neighbouring positions
- w_query: float32 [1152, 1024], P('dp', 'tensor'), may hold values from -0.1875 to 0.1875
- w_keyval: float32 [2, 1152, 256], P(None, 'dp', 'tensor'), may hold values from -0.1875 to 0.1875
- w_output: float32 [1024, 1152], P('tensor', 'dp'), may hold values from -0.1875 to 0.1875
- w_gateup: float32 [2, 1152, 6912], P(None, 'dp', 'tensor'), may hold values from -0.1875 to 0.1875
- w_down: float32 [6912, 1152], P('tensor', 'dp'), may hold values from -0.078125 to 0.078125
- norm_gains: float32 [4, 1152], P(None, 'dp'), may hold values from 0.34 to 2.3
- qk_gains: float32 [2, 256], P(None, ('dp', 'tensor')), may hold values from 0.5 to 1.5
- mom_query: float32 [1152, 1024], P('dp', 'tensor'), may hold values from -217.2232 to 217.2232
- mom_keyval: float32 [2, 1152, 256], P(None, 'dp', 'tensor'), may hold values from -217.2232 to 217.2232
- mom_output: float32 [1024, 1152], P('tensor', 'dp'), may hold values from -217.2232 to 217.2232
- mom_gateup: float32 [2, 1152, 6912], P(None, 'dp', 'tensor'), may hold values from -217.2232 to 217.2232
- mom_down: float32 [6912, 1152], P('tensor', 'dp'), may hold values from -217.2232 to 217.2232
- gain_moms: float32 [4, 1152], P(None, 'dp'), may hold values from -64 to 64
- qk_moms: float32 [2, 256], P(None, ('dp', 'tensor')), may hold values from -128 to 128
Outputs:
- block_out: float32 [8192, 1152], P('dp')
- input_grad: float32 [8192, 1152], P('dp')
- new_query: float32 [1152, 1024], P('dp', 'tensor')
- new_keyval: float32 [2, 1152, 256], P(None, 'dp', 'tensor')
- new_output: float32 [1024, 1152], P('tensor', 'dp')
- new_gateup: float32 [2, 1152, 6912], P(None, 'dp', 'tensor')
- new_down: float32 [6912, 1152], P('tensor', 'dp')
- next_mom_query: float32 [1152, 1024], P('dp', 'tensor')
- next_mom_keyval: float32 [2, 1152, 256], P(None, 'dp', 'tensor')
- next_mom_output: float32 [1024, 1152], P('tensor', 'dp')
- next_mom_gateup: float32 [2, 1152, 6912], P(None, 'dp', 'tensor')
- next_mom_down: float32 [6912, 1152], P('tensor', 'dp')
- new_norm_gains: float32 [4, 1152], P(None, 'dp')
- next_gain_moms: float32 [4, 1152], P(None, 'dp')
- new_qk_gains: float32 [2, 256], P(None, ('dp', 'tensor'))
- next_qk_moms: float32 [2, 256], P(None, ('dp', 'tensor'))
The draws below stay inside these ranges and needn't reach their ends.
Inputs may be any that keep to these rules, and one draw needn't show every extreme that they name: `segment_ids`: segment numbers never fall along the sequence; each document holds 1 to 800 tokens and one holds exactly 800.
All inputs are finite; a program needn't handle non-finite values.
Results may differ from the reference program's by a relative error of at most 0.04.
Values may be sent and summed in bfloat16 or wider, within the bound.
A program may use at most 128 MiB of HBM per device.

```python
import math
import jax
import jax.numpy as jnp
import numpy as np
from jax import lax

D = 1152
H = 4
HD = 256
FF = 6912
WINDOW = 512
DOC_MOST = 800
NS_STEPS = 3
TOKENS = 8192


def ramped_normal(key, shape, axis, scales, low_end, high_end):
    length = shape[axis]
    fraction = jnp.arange(length, dtype=jnp.float32) / length
    ramp_line = low_end + (high_end - low_end) * fraction
    layout = tuple((length if position == axis else 1 for position in range(len(shape))))
    normal_draw = jnp.clip(jax.random.normal(key, shape, jnp.float32), -4.0, 4.0)
    return normal_draw * scales * ramp_line.reshape(layout)


def draw_norm_gains(key, part):
    key = jax.random.fold_in(key, 6)
    low_end, high_end = (0.6, 1.8)
    fraction = jnp.arange(D, dtype=jnp.float32) / D
    ramp_line = low_end + (high_end - low_end) * fraction
    jitter = jax.random.uniform(key, (4, D), jnp.float32, 0.85, 1.15)
    return jitter * ramp_line[None, :]


def draw_mom_query(key, part):
    key = jax.random.fold_in(key, 11)
    low_end, high_end = (0.6, 1.8)
    return ramped_normal(key, (D, H * HD), 0, 0.3 * TOKENS ** 0.5, low_end, high_end)


def draw_mom_keyval(key, part):
    key = jax.random.fold_in(key, 12)
    low_end, high_end = (0.6, 1.8)
    return ramped_normal(key, (2, D, HD), 1, 0.3 * TOKENS ** 0.5, low_end, high_end)


def draw_mom_output(key, part):
    key = jax.random.fold_in(key, 13)
    low_end, high_end = (0.6, 1.8)
    return ramped_normal(key, (H * HD, D), 1, 0.3 * TOKENS ** 0.5, low_end, high_end)


def draw_mom_gateup(key, part):
    key = jax.random.fold_in(key, 14)
    low_end, high_end = (0.6, 1.8)
    return ramped_normal(key, (2, D, FF), 1, 0.3 * TOKENS ** 0.5, low_end, high_end)


def draw_mom_down(key, part):
    key = jax.random.fold_in(key, 15)
    low_end, high_end = (0.6, 1.8)
    return ramped_normal(key, (FF, D), 1, 0.3 * TOKENS ** 0.5, low_end, high_end)


def levels(stream_key, extent, split, least, high):
    level, own = 1.0, jax.random.fold_in(stream_key, 6)
    for dim, blocks in split:
        heights = jnp.exp(jax.random.uniform(jax.random.fold_in(own, dim), (blocks,), jnp.float32, least / len(split), high / len(split)))
        level = level * jnp.repeat(heights, extent[dim] // blocks).reshape([-1 if axis == dim else 1 for axis in range(len(extent))])
    return level


def split_up(amount, total, reach, slope):
    loads = [(1 << 20) // math.isqrt(standing ** slope) + 1 for standing in range(2, amount + 1)]
    spare, holding = total - reach - (amount - 1), [1] * (amount - 1)
    while spare > 0:
        free = [i for i in range(amount - 1) if holding[i] < reach]
        whole, left = sum([loads[i] for i in free]), spare
        for i in free:
            addition = min(reach - holding[i], max(1, left * loads[i] // whole), spare)
            holding[i] = holding[i] + addition
            spare = spare - addition
    return np.array([reach] + holding)


def uneven(key, count, total, limit, slope):
    if count == 2:
        one = jax.random.randint(key, (), max(1, total - limit), min(limit, total - 1) + 1)
        return jnp.stack([one, total - one])
    tallies = jnp.asarray(split_up(count, total, limit, slope), jnp.int32)
    pairs = (count - 1) // 2
    giver, sink = tallies[1:1 + 2 * pairs:2], tallies[2:2 + 2 * pairs:2]
    margin = jnp.minimum(giver - 1, limit - sink)
    passed = jax.random.randint(jax.random.fold_in(key, 1), (pairs,), 0, 1 << 20) % (margin + 1)
    tallies = tallies.at[1:1 + 2 * pairs:2].set(giver - passed).at[2:2 + 2 * pairs:2].set(sink + passed)
    return tallies[jax.random.permutation(jax.random.fold_in(key, 2), count)]


def gaussian(key, dims, spread, limit, pieces=(), kind=jnp.bfloat16):
    result = spread * jax.random.normal(key, dims, jnp.float32)
    if pieces:
        result = result * levels(key, dims, pieces, -0.22, 0.18)
    return jnp.clip(result, -limit, limit).astype(kind)


def setup_inputs(seed: int = 0) -> dict:
    streams_of = jax.random.split(jax.random.key(seed), 18)
    hidden_in = gaussian(streams_of[0], (TOKENS, D), 1.0, 6.0, ((0, 32),), jnp.float32)
    out_grad = gaussian(streams_of[1], (TOKENS, D), 1.0, 6.0, ((0, 32),), jnp.float32)
    segment_ids = jnp.searchsorted(jnp.cumsum(uneven(streams_of[2], 2 * TOKENS // DOC_MOST, TOKENS, DOC_MOST, 2)), jnp.arange(TOKENS), side="right").astype(jnp.int32)
    w_query = gaussian(streams_of[3], (D, H * HD), D ** -0.5, 0.1875, ((0, 32), (1, 4)), jnp.float32)
    w_keyval = gaussian(streams_of[4], (2, D, HD), D ** -0.5, 0.1875, ((1, 32), (2, 4)), jnp.float32)
    w_output = gaussian(streams_of[5], (H * HD, D), (H * HD) ** -0.5, 0.1875, ((0, 4), (1, 32)), jnp.float32)
    w_gateup = gaussian(streams_of[6], (2, D, FF), D ** -0.5, 0.1875, ((1, 32), (2, 4)), jnp.float32)
    w_down = gaussian(streams_of[7], (FF, D), FF ** -0.5, 0.078125, ((0, 4), (1, 32)), jnp.float32)
    norm_gains = draw_norm_gains(jax.random.fold_in(streams_of[17], 71), 0)
    qk_gains = jnp.clip(1.0 + 0.1 * jax.random.normal(streams_of[9], (2, HD), jnp.float32), 0.5, 1.5)
    mom_query = draw_mom_query(jax.random.fold_in(streams_of[17], 71), 0)
    mom_keyval = draw_mom_keyval(jax.random.fold_in(streams_of[17], 71), 0)
    mom_output = draw_mom_output(jax.random.fold_in(streams_of[17], 71), 0)
    mom_gateup = draw_mom_gateup(jax.random.fold_in(streams_of[17], 71), 0)
    mom_down = draw_mom_down(jax.random.fold_in(streams_of[17], 71), 0)
    gain_moms = gaussian(streams_of[15], (4, D), (0.11 * TOKENS ** 0.5), 64.0, ((1, 32),), jnp.float32)
    qk_moms = gaussian(streams_of[16], (2, HD), (0.11 * (TOKENS * H) ** 0.5), 128.0, ((1, 128),), jnp.float32)
    return dict(hidden_in=hidden_in, out_grad=out_grad, segment_ids=segment_ids, w_query=w_query, w_keyval=w_keyval, w_output=w_output, w_gateup=w_gateup, w_down=w_down, norm_gains=norm_gains, qk_gains=qk_gains, mom_query=mom_query, mom_keyval=mom_keyval, mom_output=mom_output, mom_gateup=mom_gateup, mom_down=mom_down, gain_moms=gain_moms, qk_moms=qk_moms)


EPSILON = 1e-06
COEF_ONE = 3.4445
COEF_TWO = -4.775
COEF_THREE = 2.0315

@jax.custom_vjp
def low(v):
    return lax.optimization_barrier(v.astype(jnp.bfloat16)).astype(jnp.float32)

@jax.custom_vjp
def low_back(v):
    return v

def low_keep(v):
    return (low(v), None)

def low_pass(kept, grad):
    return (grad,)

def back_keep(v):
    return (v, None)

def back_low(kept, grad):
    return (low(grad),)
low.defvjp(low_keep, low_pass)
low_back.defvjp(back_keep, back_low)

def rms_norm(values, scales):
    return values * lax.rsqrt(lax.optimization_barrier(jnp.mean(values * values, axis=-1, keepdims=True)) + EPSILON) * scales

def rotate(values, cosine, sine_wave):
    middle = values.shape[-1] // 2
    front_part = values[..., :middle]
    back_part = values[..., middle:]
    return jnp.concatenate([front_part * cosine - back_part * sine_wave, back_part * cosine + front_part * sine_wave], axis=-1)

def angles(positions, width):
    freqs = 10000.0 ** (-jnp.arange(width // 2, dtype=jnp.float32) * 2.0 / width)
    turned = positions.astype(jnp.float32)[:, None] * freqs[None, :]
    return (jnp.cos(turned), jnp.sin(turned))

def gated_gelu(gate_in, up_in):
    return jax.nn.gelu(gate_in, approximate=True) * up_in

def matmul(left, right):
    return jnp.dot(left, right, precision=lax.Precision.HIGHEST)

def attention(query_rot, key_rot, value_low, segments):
    block = min(512, TOKENS)
    blocks = TOKENS // block
    attn_scale = HD ** (-0.5)
    padded_keys = jnp.pad(key_rot, ((WINDOW, 0), (0, 0)))
    padded_values = jnp.pad(value_low, ((WINDOW, 0), (0, 0)))
    padded_segments = jnp.pad(segments, (WINDOW, 0), constant_values=-1)
    query_blocks = query_rot.reshape(blocks, block, H, HD)
    segment_blocks = segments.reshape(blocks, block)

    def one_block(inputs):
        query_rows, query_segs, number = inputs
        start = number * block
        key_rows = lax.dynamic_slice_in_dim(padded_keys, start, block + WINDOW, 0)
        value_rows = lax.dynamic_slice_in_dim(padded_values, start, block + WINDOW, 0)
        key_segs = lax.dynamic_slice_in_dim(padded_segments, start, block + WINDOW, 0)
        query_pos = start + jnp.arange(block, dtype=jnp.int32)
        key_pos = start - WINDOW + jnp.arange(block + WINDOW, dtype=jnp.int32)
        key_gap = query_pos[:, None] - key_pos[None, :]
        allowed = (query_segs[:, None] == key_segs[None, :]) & (key_gap >= 0) & (key_gap < WINDOW)
        scores = low_back(jnp.einsum('qhd,kd->hqk', query_rows, key_rows, precision=lax.Precision.HIGHEST) * attn_scale)
        scores = jnp.where(allowed[None], scores, -1e+30)
        biggest = lax.optimization_barrier(jnp.max(scores, axis=-1, keepdims=True))
        exps = jnp.exp(scores - biggest)
        softmax_out = low(exps / lax.optimization_barrier(jnp.sum(exps, axis=-1, keepdims=True)))
        return jnp.einsum('hqk,kd->qhd', softmax_out, value_rows, precision=lax.Precision.HIGHEST)
    mapped = lax.map(jax.checkpoint(one_block), (query_blocks, segment_blocks, jnp.arange(blocks, dtype=jnp.int32)))
    return mapped.reshape(TOKENS, H, HD)

def forward(params, hidden, segments):
    w_query, w_keyval, w_output, w_gateup, w_down, norm_gains, qk_gains = params
    query_w = low(w_query)
    keyval_w = low(w_keyval)
    output_w = low(w_output)
    gateup_w = low(w_gateup)
    down_w = low(w_down)
    gain_low = low(norm_gains)
    qk_low = low(qk_gains)
    positions = jnp.arange(TOKENS, dtype=jnp.int32)
    cosine, sine_wave = angles(positions, HD)
    normed = low(rms_norm(hidden, gain_low[0]))
    queries = low_back(matmul(normed, query_w)).reshape(TOKENS, H, HD)
    key_proj = low_back(matmul(normed, keyval_w[0]))
    values = low_back(matmul(normed, keyval_w[1]))
    query_rot = low(rotate(rms_norm(queries, qk_low[0]), cosine[:, None, :], sine_wave[:, None, :]))
    key_rot = low(rotate(rms_norm(key_proj, qk_low[1]), cosine, sine_wave))
    attended = attention(query_rot, key_rot, low(values), segments)
    attended = low(low_back(attended)).reshape(TOKENS, H * HD)
    attn_out = low_back(matmul(attended, output_w))
    middle = hidden + rms_norm(attn_out, gain_low[1])
    ffn_in = low(rms_norm(middle, gain_low[2]))
    gate_proj = low_back(matmul(ffn_in, gateup_w[0]))
    up_proj = low_back(matmul(ffn_in, gateup_w[1]))
    mixed_low = low(gated_gelu(gate_proj, up_proj))
    ffn_out = low_back(matmul(mixed_low, down_w))
    return middle + rms_norm(ffn_out, gain_low[3])

def orthogonalize(matrix):
    current = matrix / (jnp.sqrt(jnp.sum(matrix * matrix)) + 1e-07)
    for repeat in range(NS_STEPS):
        rounded = low(current)
        gram_low = low(jnp.dot(rounded, rounded.T, precision=lax.Precision.HIGHEST))
        image = jnp.dot(gram_low, rounded, precision=lax.Precision.HIGHEST)
        squared = jnp.dot(gram_low, low(image), precision=lax.Precision.HIGHEST)
        current = COEF_ONE * current + COEF_TWO * image + COEF_THREE * squared
    return current

def step_scale(matrix):
    return 0.15 * 0.2 * math.sqrt(max(matrix.shape[0], matrix.shape[1]))

def reference(hidden_in, out_grad, segment_ids, w_query, w_keyval, w_output, w_gateup, w_down, norm_gains, qk_gains, mom_query, mom_keyval, mom_output, mom_gateup, mom_down, gain_moms, qk_moms):
    params = (w_query, w_keyval, w_output, w_gateup, w_down, norm_gains, qk_gains)

    def apply_layer(weights, hidden):
        return forward(weights, hidden, segment_ids)
    block_out, pull_back = jax.vjp(apply_layer, params, hidden_in)
    grads, input_grad = pull_back(out_grad)
    query_grad, keyval_grad, output_grad, gateup_grad, down_grad, gains_grad, qk_grad = grads
    next_query = 0.95 * mom_query + query_grad
    next_keyval = 0.95 * mom_keyval + keyval_grad
    next_output = 0.95 * mom_output + output_grad
    next_gateup = 0.95 * mom_gateup + gateup_grad
    next_down = 0.95 * mom_down + down_grad
    matrices = [next_query, next_keyval[0], next_keyval[1], next_output.T, next_gateup[0], next_gateup[1], next_down.T]
    ortho = [orthogonalize(matrix) for matrix in matrices]
    new_query = w_query - step_scale(ortho[0]) * ortho[0]
    new_keyval = w_keyval - jnp.stack([step_scale(ortho[1]) * ortho[1], step_scale(ortho[2]) * ortho[2]])
    new_output = w_output - step_scale(ortho[3]) * ortho[3].T
    new_gateup = w_gateup - jnp.stack([step_scale(ortho[4]) * ortho[4], step_scale(ortho[5]) * ortho[5]])
    new_down = w_down - step_scale(ortho[6]) * ortho[6].T
    gain_rate = 2.0 / math.sqrt(TOKENS)
    next_gain_moms = 0.9 * gain_moms + 0.1 * gains_grad
    new_norm_gains = norm_gains - gain_rate * next_gain_moms
    next_qk_moms = 0.9 * qk_moms + 0.1 * qk_grad
    new_qk_gains = qk_gains - gain_rate * next_qk_moms
    return (block_out, input_grad, new_query, new_keyval, new_output, new_gateup, new_down, next_query, next_keyval, next_output, next_gateup, next_down, new_norm_gains, next_gain_moms, new_qk_gains, next_qk_moms)
```

```python
import functools
import math

import jax
import jax.numpy as jnp
import numpy as np
from jax import lax
from jax.experimental import pallas as pl
from jax.experimental.pallas import tpu as pltpu
from jax.sharding import PartitionSpec as P

WINDOW = 512
EPSILON = 1e-06
COEF_ONE = 3.4445
COEF_TWO = -4.775
COEF_THREE = 2.0315

D = 1152
HD = 256
TOK = 256
QTOK = 64
ROWS = 36
FFT = 1728
FFP = 1792
HALF = 896
BLK = 224
BF = jnp.bfloat16
F32 = jnp.float32
MESH = pl.DeviceIdType.MESH

SIZES = {"z": 4, "x": 4, "c": 2, "y": 4}


def place():
    dp = lax.axis_index("dp")
    return {"z": dp // 8, "x": (dp // 2) % 4, "c": dp % 2, "y": lax.axis_index("tensor")}


def rank(at, axes):
    r = 0
    for a in axes:
        r = r * SIZES[a] + at[a]
    return r


def count(axes):
    return math.prod(SIZES[a] for a in axes)


def decode(p, axes):
    out = {}
    for a in reversed(axes):
        out[a] = p % SIZES[a]
        p = p // SIZES[a]
    return out


def moved(at, off, sign):
    return {a: (at[a] + (off[a] if sign > 0 else SIZES[a] - off[a])) % SIZES[a] if a in off else at[a] for a in at}


def device(at):
    return {"dp": at["z"] * 8 + at["x"] * 2 + at["c"], "tensor": at["y"]}


def slot(ref, mode, axes, target):
    if mode == "ag":
        return ref
    if mode == "a2a":
        return ref.at[rank(target, axes)]
    return ref.at[rank(target, mode[1])]


def exchange_body(axes, modes, *refs):
    k = len(modes)
    n = count(axes)
    ins, outs = refs[:k], refs[k : 2 * k]
    send_sem, recv_sem, local_sem = refs[2 * k :]
    me = place()
    barrier = pltpu.get_barrier_semaphore()

    def greet(p, carry):
        pl.semaphore_signal(barrier, inc=1, device_id=device(moved(me, decode(p, axes), -1)), device_id_type=MESH)
        return carry

    def copies(p):
        off = decode(p, axes)
        target = moved(me, off, 1)
        return [
            pltpu.make_async_remote_copy(
                src_ref=slot(ins[i], modes[i], axes, target),
                dst_ref=outs[i].at[rank(me, axes)],
                send_sem=send_sem.at[i, p],
                recv_sem=recv_sem.at[i, p],
                device_id=device(target),
                device_id_type=MESH,
            )
            for i in range(k)
        ]

    def arrivals(p):
        off = decode(p, axes)
        target = moved(me, off, 1)
        source = moved(me, off, -1)
        return [
            pltpu.make_async_remote_copy(
                src_ref=slot(ins[i], modes[i], axes, target),
                dst_ref=outs[i].at[rank(source, axes)],
                send_sem=send_sem.at[i, p],
                recv_sem=recv_sem.at[i, p],
                device_id=device(target),
                device_id_type=MESH,
            )
            for i in range(k)
        ]

    def launch(p, carry):
        for copy in copies(p):
            copy.start()
        return carry

    def finish(p, carry):
        for copy in arrivals(p):
            copy.wait()
        return carry

    own = [
        pltpu.make_async_copy(slot(ins[i], modes[i], axes, me), outs[i].at[rank(me, axes)], local_sem.at[i])
        for i in range(k)
    ]
    lax.fori_loop(1, n, greet, 0)
    for copy in own:
        copy.start()
    pl.semaphore_wait(barrier, n - 1)
    lax.fori_loop(1, n, launch, 0)
    for copy in own:
        copy.wait()
    lax.fori_loop(1, n, finish, 0)


def exchange(items, axes, cid):
    arrays = [a for a, _ in items]
    modes = [m for _, m in items]
    n = count(axes)
    shapes = [a.shape if m == "ag" else a.shape[1:] for a, m in items]
    k = len(items)
    out = pl.pallas_call(
        functools.partial(exchange_body, axes, modes),
        out_shape=[jax.ShapeDtypeStruct((n,) + s, a.dtype) for s, a in zip(shapes, arrays)],
        in_specs=[pl.BlockSpec(memory_space=pl.ANY)] * k,
        out_specs=[pl.BlockSpec(memory_space=pl.ANY)] * k,
        scratch_shapes=[
            pltpu.SemaphoreType.DMA((k, n)),
            pltpu.SemaphoreType.DMA((k, n)),
            pltpu.SemaphoreType.DMA((k,)),
        ],
        compiler_params=pltpu.CompilerParams(collective_id=cid, has_side_effects=True),
    )(*arrays)
    return out


def halo_body(sign, kinds, *refs):
    k = len(kinds)
    ins, outs = refs[:k], refs[k : 2 * k]
    send_sem, recv_sem, local_sem = refs[2 * k :]
    dp = lax.axis_index("dp")
    y = lax.axis_index("tensor")
    barrier = pltpu.get_barrier_semaphore()
    offs = [(d, t) for d in range(3) for t in range(4)]

    def dev(d, t, way):
        shift = d if way > 0 else 32 - d
        return {"dp": (dp + shift) % 32, "tensor": (y + (t if way > 0 else 4 - t)) % 4}

    for d, t in offs[1:]:
        back = dev(d, t, -1) if sign > 0 else {"dp": (dp + d) % 32, "tensor": (y + 4 - t) % 4}
        pl.semaphore_signal(barrier, inc=1, device_id=back, device_id_type=MESH)
    own = []
    copies = []
    for i, kind in enumerate(kinds):
        for p, (d, t) in enumerate(offs):
            if kind == "near" and d > 0:
                continue
            ty = (y + t) % 4
            sy = (y + 4 - t) % 4
            src = ins[i].at[d, ty] if kind == "split" else ins[i]
            tdp = (dp + d) % 32 if sign > 0 else (dp + 32 - d) % 32
            if kind == "near":
                to, frm = outs[i].at[y], outs[i].at[sy]
            else:
                to, frm = outs[i].at[d, y], outs[i].at[d, sy]
            if p == 0:
                own.append(pltpu.make_async_copy(src, to, local_sem.at[i]))
                continue
            args = dict(send_sem=send_sem.at[i, p], recv_sem=recv_sem.at[i, p], device_id={"dp": tdp, "tensor": ty}, device_id_type=MESH)
            copies.append(
                (
                    pltpu.make_async_remote_copy(src_ref=src, dst_ref=to, **args),
                    pltpu.make_async_remote_copy(src_ref=src, dst_ref=frm, **args),
                )
            )
    for copy in own:
        copy.start()
    pl.semaphore_wait(barrier, len(offs) - 1)
    for out_copy, _ in copies:
        out_copy.start()
    for copy in own:
        copy.wait()
    for _, in_copy in copies:
        in_copy.wait()


def halo(items, sign, cid):
    arrays = [a for a, _ in items]
    kinds = [m for _, m in items]
    shapes = []
    for a, m in items:
        shapes.append((4,) + a.shape if m == "near" else (3, 4) + (a.shape[2:] if m == "split" else a.shape))
    k = len(items)
    return pl.pallas_call(
        functools.partial(halo_body, sign, kinds),
        out_shape=[jax.ShapeDtypeStruct(s, a.dtype) for s, a in zip(shapes, arrays)],
        in_specs=[pl.BlockSpec(memory_space=pl.ANY)] * k,
        out_specs=[pl.BlockSpec(memory_space=pl.ANY)] * k,
        scratch_shapes=[
            pltpu.SemaphoreType.DMA((k, 12)),
            pltpu.SemaphoreType.DMA((k, 12)),
            pltpu.SemaphoreType.DMA((k,)),
        ],
        compiler_params=pltpu.CompilerParams(collective_id=cid, has_side_effects=True),
    )(*arrays)


def sum_body(fn, rs_axes, ag_axes, n_extra, n_local, n_ag, *refs):
    parts = refs[0]
    extras = refs[1 : 1 + n_extra]
    locals_ = refs[1 + n_extra : 1 + n_extra + n_local]
    gathers = refs[1 + n_extra + n_local : 1 + n_extra + n_local + n_ag]
    recv, agbuf, rs_send, rs_recv, ag_send, ag_recv, local_sem = refs[1 + n_extra + n_local + n_ag :]
    me = place()
    union = rs_axes if len(rs_axes) >= len(ag_axes) else ag_axes
    barrier = pltpu.get_barrier_semaphore()
    for p in range(1, count(union)):
        pl.semaphore_signal(barrier, inc=1, device_id=device(moved(me, decode(p, union), -1)), device_id_type=MESH)
    own = pltpu.make_async_copy(parts.at[rank(me, rs_axes)], recv.at[rank(me, rs_axes)], local_sem.at[0])
    own.start()
    pl.semaphore_wait(barrier, count(union) - 1)

    def send(p, axes, src, dst, send_sem, recv_sem):
        off = decode(p, axes)
        target, source = moved(me, off, 1), moved(me, off, -1)
        source_ref = src(target)
        args = dict(send_sem=send_sem, recv_sem=recv_sem, device_id=device(target), device_id_type=MESH)
        out_copy = pltpu.make_async_remote_copy(src_ref=source_ref, dst_ref=dst.at[rank(me, axes)], **args)
        in_copy = pltpu.make_async_remote_copy(src_ref=source_ref, dst_ref=dst.at[rank(source, axes)], **args)
        return out_copy, in_copy

    moves = [
        send(p, rs_axes, lambda t: parts.at[rank(t, rs_axes)], recv, rs_send.at[p], rs_recv.at[p])
        for p in range(1, count(rs_axes))
    ]
    for out_copy, _ in moves:
        out_copy.start()
    own.wait()
    for _, in_copy in moves:
        in_copy.wait()
    total = recv[0].astype(F32)
    for i in range(1, count(rs_axes)):
        total = total + recv[i].astype(F32)
    local_vals, ag_vals = fn(total, *[e[...] for e in extras])
    for i, value in enumerate(ag_vals):
        agbuf[i] = value.astype(BF)
    moves = []
    own = []
    for i in range(n_ag):
        own.append(pltpu.make_async_copy(agbuf.at[i], gathers[i].at[rank(me, ag_axes)], local_sem.at[1 + i]))
        for p in range(1, count(ag_axes)):
            moves.append(send(p, ag_axes, lambda t, i=i: agbuf.at[i], gathers[i], ag_send.at[i, p], ag_recv.at[i, p]))
    for out_copy, _ in moves:
        out_copy.start()
    for copy in own:
        copy.start()
    for ref, value in zip(locals_, local_vals):
        ref[...] = value
    for copy in own:
        copy.wait()
    for _, in_copy in moves:
        in_copy.wait()


def sum_then_gather(fn, parts, extras, local_shapes, n_ag, rs_axes, ag_axes, cid):
    n_rs, n_g = count(rs_axes), count(ag_axes)
    rows = parts.shape[1:]
    vmem = pl.BlockSpec(memory_space=pltpu.VMEM)
    hbm = pl.BlockSpec(memory_space=pl.ANY)
    return pl.pallas_call(
        functools.partial(sum_body, fn, rs_axes, ag_axes, len(extras), len(local_shapes), n_ag),
        out_shape=[jax.ShapeDtypeStruct(s, F32) for s in local_shapes]
        + [jax.ShapeDtypeStruct((n_g,) + rows, BF)] * n_ag,
        in_specs=[hbm] + [vmem] * len(extras),
        out_specs=[vmem] * len(local_shapes) + [hbm] * n_ag,
        scratch_shapes=[
            pltpu.VMEM((n_rs,) + rows, BF),
            pltpu.VMEM((n_ag,) + rows, BF),
            pltpu.SemaphoreType.DMA((n_rs,)),
            pltpu.SemaphoreType.DMA((n_rs,)),
            pltpu.SemaphoreType.DMA((n_ag, n_g)),
            pltpu.SemaphoreType.DMA((n_ag, n_g)),
            pltpu.SemaphoreType.DMA((1 + n_ag,)),
        ],
        compiler_params=pltpu.CompilerParams(
            collective_id=cid, has_side_effects=True, vmem_limit_bytes=32 * 1024 * 1024
        ),
    )(parts, *extras)


def inv_rms(values):
    return lax.rsqrt(jnp.mean(values * values, axis=-1, keepdims=True) + EPSILON)


def rms_back(values, gain, s, grad):
    scaled = gain * grad
    dv = s * scaled - values * (s * s * s * jnp.mean(scaled * values, axis=-1, keepdims=True))
    return dv, jnp.sum(grad * values * s, axis=0, keepdims=True)


def rot(values, cosine, sine):
    front, back = values[:, :128], values[:, 128:]
    return jnp.concatenate([front * cosine - back * sine, back * cosine + front * sine], axis=-1)


def unrot(values, cosine, sine):
    return rot(values, cosine, -sine)


def mid_fn(u, hidden, g1, g2):
    hmid = hidden + u * inv_rms(u) * g1
    return [u, hmid], [hmid * inv_rms(hmid) * g2]


def ffn_out_fn(f, hmid, out_grad, g3):
    s = inv_rms(f)
    block = hmid + f * s * g3
    df, dg3 = rms_back(f, g3, s, out_grad)
    return [block, dg3], [df]


def ffn_in_fn(dbin, hmid, u, out_grad, g1, g2):
    dm, dg2 = rms_back(hmid, g2, inv_rms(hmid), dbin)
    dhmid = out_grad + dm
    du, dg1 = rms_back(u, g1, inv_rms(u), dhmid)
    return [dhmid, dg1, dg2], [du]


def last_fn(da, hidden, dhmid, block, g0):
    dh, dg0 = rms_back(hidden, g0, inv_rms(hidden), da)
    return [dg0], [dhmid + dh, block]


def dot(a, b, dims):
    return lax.dot_general(a, b, (dims, ((), ())), preferred_element_type=F32)


NN = ((1,), (0,))
NT = ((1,), (1,))
TN = ((0,), (0,))


def rope_tables():
    freqs = 10000.0 ** (-np.arange(128, dtype=np.float64) * 2.0 / 256)
    base = (np.arange(32, dtype=np.float64) - 2)[:, None] * 256 * freqs[None]
    step = np.arange(768, dtype=np.float64)[:, None] * freqs[None]
    return [t.astype(np.float32) for t in (np.cos(base), np.sin(base), np.cos(step), np.sin(step))]


def to_columns(ffn, attn):
    big = jnp.pad(ffn, ((0, 0), (0, 0), (0, FFP - FFT))).reshape(3, ROWS, 2, 4, BLK)
    big = big.transpose(0, 3, 2, 1, 4).reshape(24, ROWS, BLK)
    small = []
    for piece in attn:
        half = piece.shape[1] // 2
        piece = piece.reshape(ROWS, 2, half).transpose(1, 0, 2)
        small.append(jnp.pad(piece, ((0, 0), (0, 0), (0, BLK - half))))
    return jnp.concatenate([big] + small, axis=0)


def from_columns(blocks):
    big = blocks[:24].reshape(3, 4, 2, ROWS, BLK).transpose(0, 3, 2, 1, 4).reshape(3, ROWS, FFP)[:, :, :FFT]
    small = []
    for i, half in enumerate((128, 128, 32, 32)):
        piece = blocks[24 + 2 * i : 26 + 2 * i, :, :half]
        small.append(piece.transpose(1, 0, 2).reshape(ROWS, 2 * half))
    return big, small


def orthogonal(gram, columns):
    diag = jnp.sum(jnp.where(jnp.eye(D, dtype=bool), gram.astype(F32), 0.0))
    inv = 1.0 / (jnp.sqrt(diag) + 1e-07)
    a = (gram.astype(F32) * inv * inv).astype(BF)
    x = columns * inv
    for i in range(3):
        r = (COEF_TWO * a.astype(F32) + COEF_THREE * dot(a, a, NN)).astype(BF)
        x = COEF_ONE * x + dot(x.astype(BF), r, NN)
        if i < 2:
            t = (COEF_ONE * a.astype(F32) + dot(a, r, NN)).astype(BF)
            a = (COEF_ONE * t.astype(F32) + dot(t, r, NN)).astype(BF)
    return x


def local(
    hidden_in,
    out_grad,
    segment_ids,
    w_query,
    w_keyval,
    w_output,
    w_gateup,
    w_down,
    norm_gains,
    qk_gains,
    mom_query,
    mom_keyval,
    mom_output,
    mom_gateup,
    mom_down,
    gain_moms,
    qk_moms,
):
    dp = lax.axis_index("dp")
    y = lax.axis_index("tensor")
    z, x, c = dp // 8, (dp // 2) % 4, dp % 2

    attn_w = jnp.concatenate(
        [
            w_query,
            w_output.T,
            w_keyval[0],
            w_keyval[1],
            norm_gains.T,
            jnp.broadcast_to(qk_gains.reshape(1, 4), (ROWS, 4)),
            jnp.zeros((ROWS, 120), F32),
        ],
        axis=1,
    ).astype(BF)
    segs = segment_ids.reshape(2, 128)
    attn_all, segs_all = exchange([(attn_w, "ag"), (segs, "ag")], ("z", "x", "c"), 1)
    weights = attn_all.reshape(D, 768)
    wq, woT, wkv = weights[:, :256], weights[:, 256:512], weights[:, 512:640]
    gains = weights[:, 640:644].T.astype(F32)
    g0, g1, g2, g3 = (gains[i : i + 1] for i in range(4))
    qk_mine = jnp.pad(attn_all[:, 0, 644:648].reshape(32, 2, 2).transpose(1, 0, 2).reshape(2, 64), ((0, 14), (0, 64)))

    ffn_w = jnp.concatenate([w_gateup, w_down.T[None]], axis=0).astype(BF)
    ffn_w = jnp.pad(ffn_w, ((0, 0), (0, 0), (0, FFP - FFT))).reshape(3, ROWS, 2, HALF).transpose(2, 0, 1, 3)
    moms = to_columns(
        jnp.concatenate([mom_gateup, mom_down.T[None]], axis=0).astype(BF),
        [m.astype(BF) for m in (mom_query, mom_output.T, mom_keyval[0], mom_keyval[1])],
    )

    cos_b, sin_b, cos_s, sin_s = (jnp.asarray(t) for t in rope_tables())
    cb = lax.dynamic_slice_in_dim(cos_b, dp, 1, 0)
    sb = lax.dynamic_slice_in_dim(sin_b, dp, 1, 0)
    cosine = cb * cos_s - sb * sin_s
    sine = sb * cos_s + cb * sin_s
    cos_q, sin_q = cosine[512:], sine[512:]

    normed = (hidden_in * inv_rms(hidden_in) * g0).astype(BF)
    proj = dot(normed, jnp.concatenate([wq, wkv], axis=1), NN)
    q_raw = proj[:, :256]
    kv_all, qk_all = halo([(proj[:, 256:].astype(BF), "all"), (qk_mine, "near")], 1, 2)
    qk_full = qk_all[:, :2, :64].reshape(4, 2, 32, 2).transpose(1, 2, 0, 3).reshape(2, HD).astype(F32)
    gq, gk = qk_full[0:1], qk_full[1:2]
    kv_all = kv_all[::-1].reshape(3, 4, TOK, 2, 64).transpose(3, 0, 2, 1, 4).reshape(2, 3 * TOK, HD)
    k_raw = kv_all[0].astype(F32)
    vb = kv_all[1]
    q_s = inv_rms(q_raw)
    qr = rot(q_raw * q_s * gq, cos_q, sin_q).astype(BF)
    kr = rot(k_raw * inv_rms(k_raw) * gk, cosine, sine).astype(BF)
    first = jnp.maximum(dp - 2, 0)
    seg_rows = lax.dynamic_slice_in_dim(segs_all.reshape(32, TOK), first, 3, 0)
    seg_keys = jnp.where(
        dp >= 2, seg_rows, jnp.where(dp == 1, jnp.roll(seg_rows, 1, axis=0), jnp.roll(seg_rows, 2, axis=0))
    ).reshape(3 * TOK)
    key_no = jnp.arange(3 * TOK, dtype=jnp.int32)
    gap = (jnp.arange(TOK, dtype=jnp.int32) + 2 * TOK)[:, None] - key_no[None, :]
    allowed = (
        (segment_ids[:, None] == seg_keys[None, :])
        & (gap >= 0)
        & (gap < WINDOW)
        & (key_no + (dp - 2) * TOK >= 0)[None, :]
    )
    scale = HD ** (-0.5)
    scores = jnp.where(allowed, dot(qr, kr, NT) * scale, -1e30)
    top = jnp.max(scores, axis=-1, keepdims=True)
    exps = jnp.exp(scores - top)
    probs = exps / jnp.sum(exps, axis=-1, keepdims=True)
    pb = probs.astype(BF)
    ob = dot(pb, vb, NN).astype(BF)
    u_part = dot(ob, woT, NT).astype(BF).reshape(4, QTOK, D)
    hidden_q = lax.dynamic_slice_in_dim(hidden_in, y * QTOK, QTOK, 0)
    grad_q = lax.dynamic_slice_in_dim(out_grad, y * QTOK, QTOK, 0)
    u, hmid, bin_all = sum_then_gather(
        mid_fn, u_part, [hidden_q, g1, g2], [(QTOK, D)] * 2, 1, ("y",), ("c", "y"), 3
    )

    ffn_all, moms_all = exchange([(ffn_w, ("by", ("c",))), (moms, "a2a")], ("z", "x", "c"), 4)
    ffn_full = ffn_all.transpose(1, 0, 2, 3).reshape(3, D, HALF)
    wg, wu, wdT = ffn_full[0], ffn_full[1], ffn_full[2]
    bin_low = bin_all.reshape(512, D)
    gate = dot(bin_low, wg, NN)
    up = dot(bin_low, wu, NN)
    inner = math.sqrt(2.0 / math.pi)
    th = jnp.tanh(inner * (gate + 0.044715 * gate * gate * gate))
    gelu = 0.5 * gate * (1.0 + th)
    gelu_d = 0.5 * (1.0 + th) + 0.5 * gate * (1.0 - th * th) * inner * (1.0 + 3 * 0.044715 * gate * gate)
    mixed = (gelu * up).astype(BF)
    f_part = dot(mixed, wdT, NT).astype(BF).reshape(8, QTOK, D)
    block, dg3, df_all = sum_then_gather(
        ffn_out_fn, f_part, [hmid, grad_q, g3], [(QTOK, D), (1, D)], 1, ("c", "y"), ("c", "y"), 5
    )
    dfb = df_all.reshape(512, D)
    dz = dot(dfb, wdT, NN)
    dgate = (dz * up * gelu_d).astype(BF)
    dup = (dz * gelu).astype(BF)
    dbin_part = (dot(dgate, wg, NT) + dot(dup, wu, NT)).astype(BF).reshape(8, QTOK, D)
    dhmid, dg1, dg2, du_all = sum_then_gather(
        ffn_in_fn,
        dbin_part,
        [hmid, u, grad_q, g1, g2],
        [(QTOK, D), (1, D), (1, D)],
        1,
        ("c", "y"),
        ("c", "y"),
        6,
    )

    dub_all = du_all.reshape(512, D)
    dub = lax.dynamic_slice_in_dim(dub_all, c * TOK, TOK, 0)
    dob = dot(dub, woT, NN).astype(BF)
    dP = dot(dob, vb, NT)
    ds = (probs * (dP - jnp.sum(probs * dP, axis=-1, keepdims=True))).astype(BF)
    dqr = dot(ds, kr, NN) * scale
    dkr = dot(ds, qr, TN) * scale
    dv = dot(pb, dob, TN)
    dkv_part = jnp.concatenate([dkr, dv], axis=1).astype(BF).reshape(3, 4, QTOK, 512)[::-1]
    (dkv_got,) = halo([(dkv_part, "split")], -1, 7)
    dkv_sum = jnp.sum(dkv_got.reshape(12, QTOK, 512).astype(F32), axis=0)
    k_own = lax.dynamic_slice_in_dim(k_raw, 2 * TOK + y * QTOK, QTOK, 0)
    cos_k = lax.dynamic_slice_in_dim(cos_q, y * QTOK, QTOK, 0)
    sin_k = lax.dynamic_slice_in_dim(sin_q, y * QTOK, QTOK, 0)
    dk, dgk = rms_back(k_own, gk, inv_rms(k_own), unrot(dkv_sum[:, :256], cos_k, sin_k))
    dq, dgq = rms_back(q_raw, gq, q_s, unrot(dqr, cos_q, sin_q))
    dkvb = jnp.concatenate([dk, dkv_sum[:, 256:]], axis=1).astype(BF)
    dqb = dq.astype(BF)
    (dkv_all,) = exchange([(dkvb, "ag")], ("c", "y"), 8)
    pair, = exchange([(jnp.concatenate([normed, ob, dqb], axis=1), "ag")], ("c",), 9)
    pair = pair.reshape(512, D + 512)
    dkv_all = dkv_all.reshape(512, 2, 4, 64)
    dkv_cols = lax.dynamic_slice_in_dim(dkv_all, y, 1, 2).reshape(512, 128)
    da_part = (
        dot(
            jnp.concatenate([dqb, lax.dynamic_slice_in_dim(dkv_cols, c * TOK, TOK, 0)], axis=1),
            jnp.concatenate([wq, wkv], axis=1),
            NT,
        )
        .astype(BF)
        .reshape(4, QTOK, D)
    )
    dg0, last_in, last_out = sum_then_gather(
        last_fn, da_part, [hidden_q, dhmid, block, g0], [(1, D)], 2, ("y",), ("y",), 10
    )
    input_grad = last_in.reshape(TOK, D).astype(F32)
    block_out = last_out.reshape(TOK, D).astype(F32)

    qk_row = jnp.concatenate([dgq, dgk, jnp.zeros((1, D - 2 * HD), F32)], axis=1)
    gain_sum = lax.psum(jnp.concatenate([dg0, dg1, dg2, dg3, qk_row], axis=0), ("dp", "tensor"))
    gains_red = lax.dynamic_slice(gain_sum, (0, dp * ROWS), (4, ROWS))
    qk_red = lax.dynamic_slice_in_dim(gain_sum[4, : 2 * HD].reshape(2, HD), (dp * 4 + y) * 2, 2, 1)
    gain_rate = 2.0 / math.sqrt(8192)
    next_gain_moms = 0.9 * gain_moms + 0.1 * gains_red
    new_norm_gains = norm_gains - gain_rate * next_gain_moms
    next_qk_moms = 0.9 * qk_moms + 0.1 * qk_red
    new_qk_gains = qk_gains - gain_rate * next_qk_moms

    a_all, ob_all, dq_all = pair[:, :D], pair[:, D : D + 256], pair[:, D + 256 :]
    ob_cols = lax.dynamic_slice_in_dim(ob_all, c * 128, 128, 1)
    dq_cols = lax.dynamic_slice_in_dim(dq_all, c * 128, 128, 1)
    dk_cols = lax.dynamic_slice_in_dim(dkv_cols, c * 32, 32, 1)
    dv_cols = lax.dynamic_slice_in_dim(dkv_cols, 64 + c * 32, 32, 1)
    d_gate = dot(dgate, bin_low, TN).astype(BF)
    d_up = dot(dup, bin_low, TN).astype(BF)
    d_down = dot(mixed, dfb, TN).astype(BF)
    d_q = dot(dq_cols, a_all, TN).astype(BF)
    d_kv = dot(jnp.concatenate([dk_cols, dv_cols], axis=1), a_all, TN).astype(BF)
    d_o = dot(ob_cols, dub_all, TN).astype(BF)
    wgrads = jnp.concatenate(
        [
            d_gate.reshape(4, BLK, D),
            d_up.reshape(4, BLK, D),
            d_down.reshape(4, BLK, D),
            jnp.pad(d_q, ((0, BLK - 128), (0, 0)))[None],
            jnp.pad(d_o, ((0, BLK - 128), (0, 0)))[None],
            jnp.pad(d_kv[:32], ((0, BLK - 32), (0, 0)))[None],
            jnp.pad(d_kv[32:], ((0, BLK - 32), (0, 0)))[None],
        ],
        axis=0,
    )
    (wgrads_got,) = exchange([(wgrads, "a2a")], ("z", "x"), 11)
    wgrad = jnp.sum(wgrads_got.astype(F32), axis=0)

    mom = 0.95 * moms_all.reshape(D, BLK).T.astype(F32) + wgrad
    mom_low = mom.astype(BF)
    gram_part = dot(mom_low, mom_low, TN).astype(BF).reshape(32, ROWS, D)
    (gram_got,) = exchange([(gram_part, "a2a")], ("x", "y", "c"), 12)
    by_x = jnp.sum(gram_got.reshape(4, 8, ROWS, D).astype(F32), axis=1)
    by_x = jnp.where(z < 3, jnp.sum(by_x, axis=0, keepdims=True), by_x).astype(BF)
    (gram,) = exchange([(by_x, ("by", ("x",)))], ("x", "y", "c"), 13)
    ortho = orthogonal(gram.reshape(D, D), mom)
    back = jnp.concatenate([ortho.astype(BF), wgrad.astype(BF)], axis=0).T.reshape(32, ROWS, 2 * BLK)
    (back_got,) = exchange([(back, "a2a")], ("z", "x", "c"), 14)
    o_big, o_small = from_columns(back_got[:, :, :BLK].astype(F32))
    w_big, w_small = from_columns(back_got[:, :, BLK:].astype(F32))

    def step(columns):
        return 0.15 * 0.2 * math.sqrt(max(D, columns))

    new_query = w_query - step(1024) * o_small[0]
    new_output = w_output - step(1024) * o_small[1].T
    new_keyval = w_keyval - step(256) * jnp.stack(o_small[2:])
    new_gateup = w_gateup - step(6912) * o_big[:2]
    new_down = w_down - step(6912) * o_big[2].T
    next_query = 0.95 * mom_query + w_small[0]
    next_output = 0.95 * mom_output + w_small[1].T
    next_keyval = 0.95 * mom_keyval + jnp.stack(w_small[2:])
    next_gateup = 0.95 * mom_gateup + w_big[:2]
    next_down = 0.95 * mom_down + w_big[2].T
    return (
        block_out,
        input_grad,
        new_query,
        new_keyval,
        new_output,
        new_gateup,
        new_down,
        next_query,
        next_keyval,
        next_output,
        next_gateup,
        next_down,
        new_norm_gains,
        next_gain_moms,
        new_qk_gains,
        next_qk_moms,
    )


def solution(mesh):
    return jax.shard_map(
        local,
        mesh=mesh,
        in_specs=(
            P("dp", None),
            P("dp", None),
            P("dp"),
            P("dp", "tensor"),
            P(None, "dp", "tensor"),
            P("tensor", "dp"),
            P(None, "dp", "tensor"),
            P("tensor", "dp"),
            P(None, "dp"),
            P(None, ("dp", "tensor")),
            P("dp", "tensor"),
            P(None, "dp", "tensor"),
            P("tensor", "dp"),
            P(None, "dp", "tensor"),
            P("tensor", "dp"),
            P(None, "dp"),
            P(None, ("dp", "tensor")),
        ),
        out_specs=(
            P("dp", None),
            P("dp", None),
            P("dp", "tensor"),
            P(None, "dp", "tensor"),
            P("tensor", "dp"),
            P(None, "dp", "tensor"),
            P("tensor", "dp"),
            P("dp", "tensor"),
            P(None, "dp", "tensor"),
            P("tensor", "dp"),
            P(None, "dp", "tensor"),
            P("tensor", "dp"),
            P(None, "dp"),
            P(None, "dp"),
            P(None, ("dp", "tensor")),
            P(None, ("dp", "tensor")),
        ),
        check_vma=False,
    )
```

```python
import functools
import math

import jax
import jax.numpy as jnp
import numpy as np
from jax import lax
from jax.experimental import pallas as pl
from jax.experimental.pallas import tpu as pltpu
from jax.sharding import PartitionSpec as P

WINDOW = 512
EPSILON = 1e-06
COEF_ONE = 3.4445
COEF_TWO = -4.775
COEF_THREE = 2.0315

D = 1152
HD = 256
TOK = 256
QTOK = 64
ROWS = 36
FFT = 1728
FFP = 1792
HALF = 896
BLK = 224
BF = jnp.bfloat16
F32 = jnp.float32
MESH = pl.DeviceIdType.MESH

SIZES = {"z": 4, "x": 4, "c": 2, "y": 4}


def place():
    dp = lax.axis_index("dp")
    return {"z": dp // 8, "x": (dp // 2) % 4, "c": dp % 2, "y": lax.axis_index("tensor")}


def rank(at, axes):
    r = 0
    for a in axes:
        r = r * SIZES[a] + at[a]
    return r


def count(axes):
    return math.prod(SIZES[a] for a in axes)


def decode(p, axes):
    out = {}
    for a in reversed(axes):
        out[a] = p % SIZES[a]
        p = p // SIZES[a]
    return out


def moved(at, off, sign):
    return {a: (at[a] + (off[a] if sign > 0 else SIZES[a] - off[a])) % SIZES[a] if a in off else at[a] for a in at}


def device(at):
    return {"dp": at["z"] * 8 + at["x"] * 2 + at["c"], "tensor": at["y"]}


def slot(ref, mode, axes, target):
    if mode == "ag":
        return ref
    if mode == "a2a":
        return ref.at[rank(target, axes)]
    return ref.at[rank(target, mode[1])]


def exchange_body(axes, modes, subs, *refs):
    k = len(modes)
    n = count(axes)
    ins, outs = refs[:k], refs[k : 2 * k]
    send_sem, recv_sem, local_sem = refs[2 * k :]
    me = place()
    barrier = pltpu.get_barrier_semaphore()

    def greet(p, carry):
        pl.semaphore_signal(barrier, inc=1, device_id=device(moved(me, decode(p, axes), -1)), device_id_type=MESH)
        return carry

    def copies(p, arriving, items):
        off = decode(p, axes)
        target = moved(me, off, 1)
        place_of = moved(me, off, -1) if arriving else me
        return [
            pltpu.make_async_remote_copy(
                src_ref=slot(ins[i], modes[i], axes, target),
                dst_ref=outs[i].at[rank(place_of, subs[i])],
                send_sem=send_sem.at[i, p],
                recv_sem=recv_sem.at[i, p],
                device_id=device(target),
                device_id_type=MESH,
            )
            for i in items
        ]

    own = [
        pltpu.make_async_copy(slot(ins[i], modes[i], axes, me), outs[i].at[rank(me, subs[i])], local_sem.at[i])
        for i in range(k)
    ]
    lax.fori_loop(1, n, greet, 0)
    for copy in own:
        copy.start()
    pl.semaphore_wait(barrier, n - 1)
    if all(s == axes for s in subs):

        def launch(p, carry):
            for copy in copies(p, False, range(k)):
                copy.start()
            return carry

        def finish(p, carry):
            for copy in copies(p, True, range(k)):
                copy.wait()
            return carry

        lax.fori_loop(1, n, launch, 0)
        for copy in own:
            copy.wait()
        lax.fori_loop(1, n, finish, 0)
        return
    items = []
    for p in range(1, n):
        off = decode(p, axes)
        items.append((p, [i for i in range(k) if all(off[ax] == 0 for ax in axes if ax not in subs[i])]))
    for p, mine in items:
        for copy in copies(p, False, mine):
            copy.start()
    for copy in own:
        copy.wait()
    for p, mine in items:
        for copy in copies(p, True, mine):
            copy.wait()


def exchange(items, axes, cid):
    arrays = [i[0] for i in items]
    modes = [i[1] for i in items]
    subs = [i[2] if len(i) > 2 else axes for i in items]
    shapes = [
        (count(sub),) + (a.shape if m == "ag" else a.shape[1:]) for a, m, sub in zip(arrays, modes, subs)
    ]
    k, n = len(items), count(axes)
    vmem = pl.BlockSpec(memory_space=pltpu.VMEM)
    return pl.pallas_call(
        functools.partial(exchange_body, axes, modes, subs),
        out_shape=[jax.ShapeDtypeStruct(s, a.dtype) for s, a in zip(shapes, arrays)],
        in_specs=[vmem] * k,
        out_specs=[vmem] * k,
        scratch_shapes=[
            pltpu.SemaphoreType.DMA((k, n)),
            pltpu.SemaphoreType.DMA((k, n)),
            pltpu.SemaphoreType.DMA((k,)),
        ],
        compiler_params=pltpu.CompilerParams(
            collective_id=cid, has_side_effects=True, vmem_limit_bytes=32 * 1024 * 1024
        ),
    )(*arrays)


def virtual(me, p, q):
    c = me["c"]
    first = {"a": jnp.where(c == 0, me[p], me[q]), "b": jnp.where(c == 0, me[q], me[p])}

    def to(av, bv):
        return {**me, p: jnp.where(c == 0, av, bv), q: jnp.where(c == 0, bv, av)}

    return first["a"], first["b"], to


def remote(src, dst, send_sem, recv_sem, at):
    return pltpu.make_async_remote_copy(
        src_ref=src, dst_ref=dst, send_sem=send_sem, recv_sem=recv_sem, device_id=device(at), device_id_type=MESH
    )


def greet_all(places):
    barrier = pltpu.get_barrier_semaphore()
    for at in places:
        pl.semaphore_signal(barrier, inc=1, device_id=device(at), device_id_type=MESH)
    return barrier


def gather_body(block, ffn, out, near, send_sem, recv_sem, local_sem):
    me = place()
    a, b, to = virtual(me, "z", "x")
    twin = {**me, "c": 1 - me["c"]}
    a_next, a_last, a_far = (a + 1) % 4, (a + 3) % 4, (a + 2) % 4
    b_next, b_last = (b + 1) % 4, (b + 3) % 4
    barrier = greet_all([to(a_next, b), to(a_last, b), to(a, b_next), to(a, b_last)] + [twin])

    def spot(av, bv):
        at = to(av, bv)
        return out.at[me["c"], at["z"], at["x"]]

    here = spot(a, b)
    mine = near.at[a, pl.ds(me["c"] * 3, 3)]
    theirs = near.at[a, pl.ds((1 - me["c"]) * 3, 3)]
    own = pltpu.make_async_copy(block, here, local_sem.at[0])
    own.start()
    keep = pltpu.make_async_copy(ffn.at[me["c"]], mine, local_sem.at[1])
    keep.start()
    pl.semaphore_wait(barrier, 5)

    def sent(src, dst_here, sem, at):
        remote(src, src, send_sem.at[sem], recv_sem.at[sem], at).start()
        return remote(src, dst_here, send_sem.at[sem], recv_sem.at[sem], at)

    own.wait()
    up, down = to(a_next, b), to(a_last, b)
    first = [sent(here, spot(a_last, b), 1, up), sent(here, spot(a_next, b), 2, down)]
    there = near.at[b, pl.ds(me["c"] * 3, 3)]
    remote(ffn.at[1 - me["c"]], there, send_sem.at[0], recv_sem.at[0], twin).start()
    keep.wait()
    remote(ffn.at[1 - me["c"]], theirs, send_sem.at[0], recv_sem.at[0], twin).wait()
    ffn_first = [sent(near.at[a], near.at[a_last], 17, up), sent(near.at[a], near.at[a_next], 18, down)]
    for w in first:
        w.wait()
    left, right, far = spot(a_last, b), spot(a_next, b), spot(a_far, b)
    for w in [sent(left.at[0], far.at[0], 3, up), sent(right.at[1], far.at[1], 4, down)]:
        w.wait()
    up2, down2 = to(a, b_next), to(a, b_last)
    waits = [
        (sent(spot(i, b), spot(i, b_last), 5 + 2 * i, up2), sent(spot(i, b), spot(i, b_next), 6 + 2 * i, down2))
        for i in range(4)
    ]
    for w in ffn_first:
        w.wait()
    lo, hi = pl.ds(0, 3), pl.ds(3, 3)
    late = [
        sent(near.at[a_last, lo], near.at[a_far, lo], 19, up),
        sent(near.at[a_next, hi], near.at[a_far, hi], 20, down),
    ]
    for i in range(4):
        w_last, w_next = waits[i]
        far = spot(i, (b + 2) % 4)
        if i < 2:
            w_last.wait()
            late += [sent(spot(i, b_last), far, 13 + i, up2), w_next]
        else:
            w_next.wait()
            late += [sent(spot(i, b_next), far, 13 + i, down2), w_last]
    for w in late:
        w.wait()
    remote(out.at[me["c"]], out.at[me["c"]], send_sem.at[21], recv_sem.at[21], twin).start()
    remote(out.at[me["c"]], out.at[1 - me["c"]], send_sem.at[21], recv_sem.at[21], twin).wait()


def gather_plane(block, ffn, cid):
    hbm = pl.BlockSpec(memory_space=pl.ANY)
    return pl.pallas_call(
        gather_body,
        out_shape=[
            jax.ShapeDtypeStruct((2, 4, 4) + block.shape, block.dtype),
            jax.ShapeDtypeStruct((4, 6) + ffn.shape[2:], ffn.dtype),
        ],
        in_specs=[hbm, hbm],
        out_specs=[hbm, hbm],
        scratch_shapes=[
            pltpu.SemaphoreType.DMA((22,)),
            pltpu.SemaphoreType.DMA((22,)),
            pltpu.SemaphoreType.DMA((2,)),
        ],
        compiler_params=pltpu.CompilerParams(collective_id=cid, has_side_effects=True),
    )(block, ffn)


class SideGather:
    sems = 16

    def shape(self, near):
        return jax.ShapeDtypeStruct((4, 4) + near.shape[1:], near.dtype)

    def places(self, me):
        a, b, to = virtual(me, "z", "x")
        return [to(a, (b + 1) % 4), to(a, (b + 3) % 4)]

    def start(self, me, near, out, send_sem, recv_sem):
        a, b, to = virtual(me, "z", "x")
        b_next, b_last = (b + 1) % 4, (b + 3) % 4
        up, down = to(a, b_next), to(a, b_last)

        def spot(av, bv):
            at = to(av, bv)
            return out.at[at["z"], at["x"]]

        def sent(src, dst, dst_here, sem, at):
            remote(src, dst, send_sem.at[sem], recv_sem.at[sem], at).start()
            return remote(src, dst_here, send_sem.at[sem], recv_sem.at[sem], at)

        self.waits = []
        for i in range(4):
            self.waits.append(
                (
                    sent(near.at[i], spot(i, b), spot(i, b_last), 2 * i, up),
                    sent(near.at[i], spot(i, b), spot(i, b_next), 2 * i + 1, down),
                )
            )
        self.late = []
        for i in range(4):
            copy = pltpu.make_async_copy(near.at[i], spot(i, b), recv_sem.at[12 + i])
            copy.start()
            self.late.append(copy)

        def middle():
            for i in range(4):
                w_last, w_next = self.waits[i]
                far = spot(i, (b + 2) % 4)
                if i < 2:
                    w_last.wait()
                    src = spot(i, b_last)
                    self.late += [sent(src, src, far, 8 + i, up), w_next]
                else:
                    w_next.wait()
                    src = spot(i, b_next)
                    self.late += [sent(src, src, far, 8 + i, down), w_last]

        self.middle = middle

    def finish(self):
        for w in self.late:
            w.wait()


class SideSwap:
    sems = 33
    axes = ("z", "x", "c")

    def shape(self, parts):
        return jax.ShapeDtypeStruct(parts.shape, parts.dtype)

    def places(self, me):
        return [moved(me, decode(p, self.axes), -1) for p in range(1, 32)]

    def start(self, me, parts, out, send_sem, recv_sem):
        def copies(p, arriving):
            off = decode(p, self.axes)
            target = moved(me, off, 1)
            spot = moved(me, off, -1) if arriving else me
            return remote(
                parts.at[rank(target, self.axes)],
                out.at[rank(spot, self.axes)],
                send_sem.at[p],
                recv_sem.at[p],
                target,
            )

        def launch(p, carry):
            copies(p, False).start()
            return carry

        def finish(p, carry):
            copies(p, True).wait()
            return carry

        lax.fori_loop(1, 32, launch, 0)
        mine = rank(me, self.axes)
        copy = pltpu.make_async_copy(parts.at[mine], out.at[mine], recv_sem.at[32])
        copy.start()
        copy.wait()
        self.finish = lambda: lax.fori_loop(1, 32, finish, 0)
        self.middle = lambda: None


def reduce_body(parts, total, p, r1, r2, q, r3, r4, send_sem, recv_sem, local_sem):
    me = place()
    a, b, to = virtual(me, "z", "x")
    a_next, a_last, a_far = (a + 1) % 4, (a + 3) % 4, (a + 2) % 4
    b_next, b_last, b_far = (b + 1) % 4, (b + 3) % 4, (b + 2) % 4
    up, down = to(a_next, b), to(a_last, b)
    up2, down2 = to(a, b_next), to(a, b_last)
    barrier = greet_all([up, down, up2, down2])

    def at(ref, av, bv):
        w = to(av, bv)
        return ref.at[w["z"], w["x"]]

    load = pltpu.make_async_copy(parts, p, local_sem.at[0])
    load.start()
    pl.semaphore_wait(barrier, 4)
    first = []
    for i in range(4):
        first.append(remote(at(parts, a_far, i), r1.at[i], send_sem.at[i], recv_sem.at[i], up if i < 2 else down))
        first[-1].start()
    second = []

    def onward(i, way, src):
        sem = 4 + 2 * i + way
        copy = remote(src, r2.at[way, i], send_sem.at[sem], recv_sem.at[sem], down if way else up)
        copy.start()
        second.append(copy)

    for i in range(4):
        onward(i, 1 if i < 2 else 0, at(parts, a_last if i < 2 else a_next, i))
    load.wait()
    for i in range(4):
        first[i].wait()
        dest = at(p, a_next if i < 2 else a_last, i)
        dest[...] = (dest[...].astype(F32) + r1[i].astype(F32)).astype(BF)
        onward(i, 0 if i < 2 else 1, dest)
    for copy in second:
        copy.wait()
    for i in range(4):
        q[i] = (at(p, a, i)[...].astype(F32) + r2[0, i].astype(F32) + r2[1, i].astype(F32)).astype(BF)
    lo, hi = pl.ds(0, BLK // 2), pl.ds(BLK // 2, BLK // 2)
    one = remote(q.at[b_far, lo], r3.at[0], send_sem.at[12], recv_sem.at[12], up2)
    two = remote(q.at[b_far, hi], r3.at[1], send_sem.at[13], recv_sem.at[13], down2)
    one.start()
    two.start()
    three = remote(q.at[b_next, hi], r4.at[0, hi], send_sem.at[14], recv_sem.at[14], up2)
    four = remote(q.at[b_last, lo], r4.at[1, lo], send_sem.at[15], recv_sem.at[15], down2)
    three.start()
    four.start()
    one.wait()
    dest = q.at[b_next, lo]
    dest[...] = (dest[...].astype(F32) + r3[0].astype(F32)).astype(BF)
    five = remote(q.at[b_next, lo], r4.at[0, lo], send_sem.at[16], recv_sem.at[16], up2)
    five.start()
    two.wait()
    dest = q.at[b_last, hi]
    dest[...] = (dest[...].astype(F32) + r3[1].astype(F32)).astype(BF)
    six = remote(q.at[b_last, hi], r4.at[1, hi], send_sem.at[17], recv_sem.at[17], down2)
    six.start()
    for copy in (three, four, five, six):
        copy.wait()
    total[...] = q[b].astype(F32) + r4[0].astype(F32) + r4[1].astype(F32)


def reduce_plane(parts, cid):
    block = parts.shape[2:]
    return pl.pallas_call(
        reduce_body,
        out_shape=jax.ShapeDtypeStruct(block, F32),
        in_specs=[pl.BlockSpec(memory_space=pl.ANY)],
        out_specs=pl.BlockSpec(memory_space=pltpu.VMEM),
        scratch_shapes=[
            pltpu.VMEM((4, 4) + block, BF),
            pltpu.VMEM((4,) + block, BF),
            pltpu.VMEM((2, 4) + block, BF),
            pltpu.VMEM((4,) + block, BF),
            pltpu.VMEM((2, BLK // 2, D), BF),
            pltpu.VMEM((2,) + block, BF),
            pltpu.SemaphoreType.DMA((18,)),
            pltpu.SemaphoreType.DMA((18,)),
            pltpu.SemaphoreType.DMA((1,)),
        ],
        compiler_params=pltpu.CompilerParams(
            collective_id=cid, has_side_effects=True, vmem_limit_bytes=48 * 1024 * 1024
        ),
    )(parts)


def gram_body(parts, extra, gram, extras, p, got, mine, bx, send_sem, recv_sem, local_sem):
    me = place()
    c, z = me["c"], me["z"]
    axes = ("x", "y")
    twin = {**me, "c": 1 - c}
    barrier = pltpu.get_barrier_semaphore()
    for i in range(1, 16):
        pl.semaphore_signal(barrier, inc=1, device_id=device(moved(me, decode(i, axes), -1)), device_id_type=MESH)
    for i in range(4):
        pl.semaphore_signal(barrier, inc=1, device_id=device({**twin, "y": (me["y"] + i) % 4}), device_id_type=MESH)
    load = pltpu.make_async_copy(parts.at[c], p, local_sem.at[0])
    load.start()
    keep = pltpu.make_async_copy(extra, extras.at[rank(me, ("c", "y"))], local_sem.at[1])
    keep.start()
    pl.semaphore_wait(barrier, 19)
    swap = remote(parts.at[1 - c], got, send_sem.at[0, 0], recv_sem.at[0, 0], twin)
    swap.start()
    extra_waits = []
    for i in range(1, 8):
        off = decode(i, ("c", "y"))
        target, source = moved(me, off, 1), moved(me, off, -1)
        sems = (send_sem.at[3, i], recv_sem.at[3, i])
        remote(extra, extras.at[rank(me, ("c", "y"))], *sems, target).start()
        extra_waits.append(remote(extra, extras.at[rank(source, ("c", "y"))], *sems, target))
    load.wait()
    swap.wait()
    for i in range(16):
        p[i] = (p[i].astype(F32) + got[i].astype(F32)).astype(BF)
    waits = []
    for i in range(1, 16):
        off = decode(i, axes)
        target, source = moved(me, off, 1), moved(me, off, -1)
        sems = (send_sem.at[1, i], recv_sem.at[1, i])
        remote(p.at[rank(target, axes)], mine.at[rank(me, axes)], *sems, target).start()
        waits.append(remote(p.at[rank(target, axes)], mine.at[rank(source, axes)], *sems, target))
    own = pltpu.make_async_copy(p.at[rank(me, axes)], mine.at[rank(me, axes)], local_sem.at[0])
    own.start()
    own.wait()
    for w in waits:
        w.wait()
    sums = []
    for i in range(4):
        part = mine[4 * i].astype(F32)
        for j in range(1, 4):
            part = part + mine[4 * i + j].astype(F32)
        sums.append(part)
    whole = sums[0] + sums[1] + sums[2] + sums[3]
    for i in range(4):
        bx[i] = jnp.where(z < 3, whole, sums[i]).astype(BF)
    waits = []
    spot = gram.at[c]
    for i in range(1, 16):
        off = decode(i, axes)
        target, source = moved(me, off, 1), moved(me, off, -1)
        sems = (send_sem.at[2, i], recv_sem.at[2, i])
        remote(bx.at[target["x"]], spot.at[rank(me, axes)], *sems, target).start()
        waits.append(remote(bx.at[target["x"]], spot.at[rank(source, axes)], *sems, target))
    own = pltpu.make_async_copy(bx.at[me["x"]], spot.at[rank(me, axes)], local_sem.at[0])
    own.start()
    own.wait()
    for w in waits:
        w.wait()
    remote(gram.at[c], gram.at[c], send_sem.at[2, 0], recv_sem.at[2, 0], twin).start()
    remote(gram.at[c], gram.at[1 - c], send_sem.at[2, 0], recv_sem.at[2, 0], twin).wait()
    keep.wait()
    for w in extra_waits:
        w.wait()


def gram_sum(parts, extra, cid):
    vmem = pl.BlockSpec(memory_space=pltpu.VMEM)
    half = parts.shape[1:]
    return pl.pallas_call(
        gram_body,
        out_shape=[
            jax.ShapeDtypeStruct(parts.shape, BF),
            jax.ShapeDtypeStruct((8,) + extra.shape, extra.dtype),
        ],
        in_specs=[vmem, vmem],
        out_specs=[vmem, vmem],
        scratch_shapes=[
            pltpu.VMEM(half, BF),
            pltpu.VMEM(half, BF),
            pltpu.VMEM(half, BF),
            pltpu.VMEM((4,) + half[1:], BF),
            pltpu.SemaphoreType.DMA((4, 16)),
            pltpu.SemaphoreType.DMA((4, 16)),
            pltpu.SemaphoreType.DMA((2,)),
        ],
        compiler_params=pltpu.CompilerParams(
            collective_id=cid, has_side_effects=True, vmem_limit_bytes=48 * 1024 * 1024
        ),
    )(parts, extra)


def halo_body(sign, kinds, *refs):
    k = len(kinds)
    ins, outs = refs[:k], refs[k : 2 * k]
    send_sem, recv_sem, local_sem = refs[2 * k :]
    dp = lax.axis_index("dp")
    y = lax.axis_index("tensor")
    barrier = pltpu.get_barrier_semaphore()
    offs = [(d, t) for d in range(3) for t in range(4)]

    def dev(d, t, way):
        shift = d if way > 0 else 32 - d
        return {"dp": (dp + shift) % 32, "tensor": (y + (t if way > 0 else 4 - t)) % 4}

    for d, t in offs[1:]:
        back = dev(d, t, -1) if sign > 0 else {"dp": (dp + d) % 32, "tensor": (y + 4 - t) % 4}
        pl.semaphore_signal(barrier, inc=1, device_id=back, device_id_type=MESH)
    own = []
    copies = []
    for i, kind in enumerate(kinds):
        for p, (d, t) in enumerate(offs):
            if kind == "near" and d > 0:
                continue
            ty = (y + t) % 4
            sy = (y + 4 - t) % 4
            src = ins[i].at[d, ty] if kind == "split" else ins[i]
            tdp = (dp + d) % 32 if sign > 0 else (dp + 32 - d) % 32
            if kind == "near":
                to, frm = outs[i].at[y], outs[i].at[sy]
            else:
                to, frm = outs[i].at[d, y], outs[i].at[d, sy]
            if p == 0:
                own.append(pltpu.make_async_copy(src, to, local_sem.at[i]))
                continue
            args = dict(send_sem=send_sem.at[i, p], recv_sem=recv_sem.at[i, p], device_id={"dp": tdp, "tensor": ty}, device_id_type=MESH)
            copies.append(
                (
                    pltpu.make_async_remote_copy(src_ref=src, dst_ref=to, **args),
                    pltpu.make_async_remote_copy(src_ref=src, dst_ref=frm, **args),
                )
            )
    for copy in own:
        copy.start()
    pl.semaphore_wait(barrier, len(offs) - 1)
    for out_copy, _ in copies:
        out_copy.start()
    for copy in own:
        copy.wait()
    for _, in_copy in copies:
        in_copy.wait()


def halo(items, sign, cid):
    arrays = [a for a, _ in items]
    kinds = [m for _, m in items]
    shapes = []
    for a, m in items:
        shapes.append((4,) + a.shape if m == "near" else (3, 4) + (a.shape[2:] if m == "split" else a.shape))
    k = len(items)
    return pl.pallas_call(
        functools.partial(halo_body, sign, kinds),
        out_shape=[jax.ShapeDtypeStruct(s, a.dtype) for s, a in zip(shapes, arrays)],
        in_specs=[pl.BlockSpec(memory_space=pl.ANY)] * k,
        out_specs=[pl.BlockSpec(memory_space=pl.ANY)] * k,
        scratch_shapes=[
            pltpu.SemaphoreType.DMA((k, 12)),
            pltpu.SemaphoreType.DMA((k, 12)),
            pltpu.SemaphoreType.DMA((k,)),
        ],
        compiler_params=pltpu.CompilerParams(collective_id=cid, has_side_effects=True),
    )(*arrays)


def sum_body(fn, both, spread, side, n_extra, n_local, n_ag, *refs):
    if side is not None:
        side_in, side_out, side_send, side_recv = refs[0], refs[1 + 1 + n_extra + n_local + n_ag], refs[-2], refs[-1]
        refs = refs[1 : 2 + n_extra + n_local + n_ag] + refs[3 + n_extra + n_local + n_ag : -2]
    parts = refs[0]
    extras = refs[1 : 1 + n_extra]
    locals_ = refs[1 + n_extra : 1 + n_extra + n_local]
    gathers = refs[1 + n_extra + n_local : 1 + n_extra + n_local + n_ag]
    pre, recv, agbuf, send_sem, recv_sem, local_sem = refs[1 + n_extra + n_local + n_ag :]
    me = place()
    c, y = me["c"], me["y"]
    twin = {**me, "c": 1 - c}
    near = [(moved(me, {"y": i}, 1), moved(me, {"y": i}, -1)) for i in range(1, 4)]
    use_twin = both or spread
    places = [source for _, source in near] + ([twin] if use_twin else [])
    if side is not None:
        places += side.places(me)
    barrier = greet_all(places)
    pl.semaphore_wait(barrier, len(places))
    if both:
        swap = remote(parts.at[1 - c], pre, send_sem.at[0], recv_sem.at[0], twin)
        swap.start()
        if side is not None:
            side.start(me, side_in, side_out, side_send, side_recv)
        swap.wait()
        for i in range(4):
            pre[i] = (pre[i].astype(F32) + parts[c, i].astype(F32)).astype(BF)
        mine = pre
    else:
        mine = parts
    waits = []
    for i, (target, source) in enumerate(near):
        sems = (send_sem.at[1 + i], recv_sem.at[1 + i])
        remote(mine.at[target["y"]], recv.at[i], *sems, target).start()
        waits.append(remote(mine.at[target["y"]], recv.at[i], *sems, target))
    if side is not None and not both:
        side.start(me, side_in, side_out, side_send, side_recv)
    total = mine[y].astype(F32)
    for i in range(3):
        waits[i].wait()
        total = total + recv[i].astype(F32)
    local_vals, ag_vals = fn(total, *[e[...] for e in extras])
    for i, value in enumerate(ag_vals):
        agbuf[i] = value.astype(BF)
    waits, own = [], []
    for j in range(n_ag):
        out = gathers[j].at[c] if spread else gathers[j]
        for i, (target, source) in enumerate(near):
            sems = (send_sem.at[4 + 3 * j + i], recv_sem.at[4 + 3 * j + i])
            remote(agbuf.at[j], out.at[y], *sems, target).start()
            waits.append(remote(agbuf.at[j], out.at[source["y"]], *sems, target))
        own.append(pltpu.make_async_copy(agbuf.at[j], out.at[y], local_sem.at[j]))
        own[-1].start()
    for ref, value in zip(locals_, local_vals):
        ref[...] = value
    if side is not None:
        side.middle()
    for copy in own + waits:
        copy.wait()
    if spread:
        for j in range(n_ag):
            g = gathers[j]
            sems = (send_sem.at[4 + 3 * n_ag + j], recv_sem.at[4 + 3 * n_ag + j])
            remote(g.at[c], g.at[c], *sems, twin).start()
            remote(g.at[c], g.at[1 - c], *sems, twin).wait()
    if side is not None:
        side.finish()


def sum_then_gather(fn, parts, extras, local_shapes, n_ag, spread, cid, side=None, side_in=None):
    both = parts.ndim == 4
    rows = parts.shape[-2:]
    vmem = pl.BlockSpec(memory_space=pltpu.VMEM)
    gathered = ((2, 4) if spread else (4,)) + rows
    n_sem = 4 + 4 * n_ag
    hbm = pl.BlockSpec(memory_space=pl.ANY)
    more = side is not None
    return pl.pallas_call(
        functools.partial(sum_body, fn, both, spread, side, len(extras), len(local_shapes), n_ag),
        out_shape=[jax.ShapeDtypeStruct(s, F32) for s in local_shapes]
        + [jax.ShapeDtypeStruct(gathered, BF)] * n_ag
        + ([side.shape(side_in)] if more else []),
        in_specs=[hbm] * more + [vmem] * (1 + len(extras)),
        out_specs=[vmem] * (len(local_shapes) + n_ag) + [hbm] * more,
        scratch_shapes=[
            pltpu.VMEM((4,) + rows, BF),
            pltpu.VMEM((3,) + rows, BF),
            pltpu.VMEM((n_ag,) + rows, BF),
            pltpu.SemaphoreType.DMA((n_sem,)),
            pltpu.SemaphoreType.DMA((n_sem,)),
            pltpu.SemaphoreType.DMA((n_ag,)),
        ]
        + ([pltpu.SemaphoreType.DMA((side.sems,))] * 2 if more else []),
        compiler_params=pltpu.CompilerParams(
            collective_id=cid, has_side_effects=True, vmem_limit_bytes=32 * 1024 * 1024
        ),
    )(*([side_in] if more else []), parts, *extras)


def inv_rms(values):
    return lax.rsqrt(jnp.mean(values * values, axis=-1, keepdims=True) + EPSILON)


def rms_back(values, gain, s, grad):
    scaled = gain * grad
    dv = s * scaled - values * (s * s * s * jnp.mean(scaled * values, axis=-1, keepdims=True))
    return dv, jnp.sum(grad * values * s, axis=0, keepdims=True)


def rot(values, cosine, sine):
    front, back = values[:, :128], values[:, 128:]
    return jnp.concatenate([front * cosine - back * sine, back * cosine + front * sine], axis=-1)


def unrot(values, cosine, sine):
    return rot(values, cosine, -sine)


def mid_fn(u, hidden, g1, g2):
    hmid = hidden + u * inv_rms(u) * g1
    return [u, hmid], [hmid * inv_rms(hmid) * g2]


def ffn_out_fn(f, hmid, out_grad, g3):
    s = inv_rms(f)
    block = hmid + f * s * g3
    df, dg3 = rms_back(f, g3, s, out_grad)
    return [block, dg3], [df]


def ffn_in_fn(dbin, hmid, u, out_grad, g1, g2):
    dm, dg2 = rms_back(hmid, g2, inv_rms(hmid), dbin)
    dhmid = out_grad + dm
    du, dg1 = rms_back(u, g1, inv_rms(u), dhmid)
    return [dhmid, dg1, dg2], [du]


def last_fn(da, hidden, dhmid, block, g0):
    dh, dg0 = rms_back(hidden, g0, inv_rms(hidden), da)
    return [dg0], [dhmid + dh, block]


def dot(a, b, dims):
    return lax.dot_general(a, b, (dims, ((), ())), preferred_element_type=F32)


NN = ((1,), (0,))
NT = ((1,), (1,))
TN = ((0,), (0,))


def rope_tables():
    freqs = 10000.0 ** (-np.arange(128, dtype=np.float64) * 2.0 / 256)
    base = (np.arange(32, dtype=np.float64) - 2)[:, None] * 256 * freqs[None]
    step = np.arange(768, dtype=np.float64)[:, None] * freqs[None]
    return [t.astype(np.float32) for t in (np.cos(base), np.sin(base), np.cos(step), np.sin(step))]


def to_columns(ffn, attn):
    big = jnp.pad(ffn, ((0, 0), (0, 0), (0, FFP - FFT))).reshape(3, ROWS, 2, 4, BLK)
    big = big.transpose(0, 3, 2, 1, 4).reshape(24, ROWS, BLK)
    small = []
    for piece in attn:
        half = piece.shape[1] // 2
        piece = piece.reshape(ROWS, 2, half).transpose(1, 0, 2)
        small.append(jnp.pad(piece, ((0, 0), (0, 0), (0, BLK - half))))
    return jnp.concatenate([big] + small, axis=0)


def from_columns(blocks):
    big = blocks[:24].reshape(3, 4, 2, ROWS, BLK).transpose(0, 3, 2, 1, 4).reshape(3, ROWS, FFP)[:, :, :FFT]
    small = []
    for i, half in enumerate((128, 128, 32, 32)):
        piece = blocks[24 + 2 * i : 26 + 2 * i, :, :half]
        small.append(piece.transpose(1, 0, 2).reshape(ROWS, 2 * half))
    return big, small


def orthogonal(gram, columns):
    diag = jnp.sum(jnp.where(jnp.eye(D, dtype=bool), gram.astype(F32), 0.0))
    inv = 1.0 / (jnp.sqrt(diag) + 1e-07)
    a = (gram.astype(F32) * inv * inv).astype(BF)
    x = columns * inv
    for i in range(3):
        r = (COEF_TWO * a.astype(F32) + COEF_THREE * dot(a, a, NN)).astype(BF)
        x = COEF_ONE * x + dot(x.astype(BF), r, NN)
        if i < 2:
            t = (COEF_ONE * a.astype(F32) + dot(a, r, NN)).astype(BF)
            a = (COEF_ONE * t.astype(F32) + dot(t, r, NN)).astype(BF)
    return x


def local(
    hidden_in,
    out_grad,
    segment_ids,
    w_query,
    w_keyval,
    w_output,
    w_gateup,
    w_down,
    norm_gains,
    qk_gains,
    mom_query,
    mom_keyval,
    mom_output,
    mom_gateup,
    mom_down,
    gain_moms,
    qk_moms,
):
    dp = lax.axis_index("dp")
    y = lax.axis_index("tensor")
    z, x, c = dp // 8, (dp // 2) % 4, dp % 2

    ffn_w = jnp.concatenate([w_gateup, w_down.T[None]], axis=0).astype(BF)
    ffn_w = jnp.pad(ffn_w, ((0, 0), (0, 0), (0, FFP - FFT))).reshape(3, ROWS, 2, HALF).transpose(2, 0, 1, 3)
    moms = to_columns(
        jnp.concatenate([mom_gateup, mom_down.T[None]], axis=0).astype(BF),
        [m.astype(BF) for m in (mom_query, mom_output.T, mom_keyval[0], mom_keyval[1])],
    )

    segs = jnp.pad(segment_ids.astype(F32).reshape(4, 64), ((0, ROWS - 4), (0, 0)))
    attn_w = jnp.stack(
        [
            jnp.concatenate([w_query, w_keyval[0], w_keyval[1]], axis=1),
            jnp.concatenate(
                [
                    w_output.T,
                    norm_gains.T,
                    jnp.broadcast_to(qk_gains.reshape(1, 4), (ROWS, 4)),
                    segs,
                    jnp.zeros((ROWS, 56), F32),
                ],
                axis=1,
            ),
        ]
    ).astype(BF)
    attn_got, ffn_near = gather_plane(attn_w, ffn_w, 1)
    attn_all = attn_got.transpose(3, 1, 2, 0, 4, 5).reshape(2, 32, ROWS, 384)
    w_qkv = attn_all[0].reshape(D, 384)
    wq, wkv = w_qkv[:, :256], w_qkv[:, 256:]
    woT = attn_all[1, :, :, :256].reshape(D, 256)
    gains = attn_all[1, :, :, 256:260].reshape(D, 4).T.astype(F32)
    g0, g1, g2, g3 = (gains[i : i + 1] for i in range(4))
    qk_mine = attn_all[1, :, 0, 260:264].reshape(32, 2, 2).transpose(1, 0, 2).reshape(2, 64)
    qk_mine = jnp.pad(qk_mine, ((0, 14), (0, 64)))
    segs_all = attn_all[1, :, :4, 264:328].reshape(32, TOK).astype(jnp.int32)

    cos_b, sin_b, cos_s, sin_s = (jnp.asarray(t) for t in rope_tables())
    cb = lax.dynamic_slice_in_dim(cos_b, dp, 1, 0)
    sb = lax.dynamic_slice_in_dim(sin_b, dp, 1, 0)
    cosine = cb * cos_s - sb * sin_s
    sine = sb * cos_s + cb * sin_s
    cos_q, sin_q = cosine[512:], sine[512:]

    normed = (hidden_in * inv_rms(hidden_in) * g0).astype(BF)
    proj = dot(normed, w_qkv, NN)
    q_raw = proj[:, :256]
    kv_all, qk_all = halo([(proj[:, 256:].astype(BF), "all"), (qk_mine, "near")], 1, 2)
    qk_full = qk_all[:, :2, :64].reshape(4, 2, 32, 2).transpose(1, 2, 0, 3).reshape(2, HD).astype(F32)
    gq, gk = qk_full[0:1], qk_full[1:2]
    kv_all = kv_all[::-1].reshape(3, 4, TOK, 2, 64).transpose(3, 0, 2, 1, 4).reshape(2, 3 * TOK, HD)
    k_raw = kv_all[0].astype(F32)
    vb = kv_all[1]
    q_s = inv_rms(q_raw)
    qr = rot(q_raw * q_s * gq, cos_q, sin_q).astype(BF)
    kr = rot(k_raw * inv_rms(k_raw) * gk, cosine, sine).astype(BF)
    first = jnp.maximum(dp - 2, 0)
    seg_rows = lax.dynamic_slice_in_dim(segs_all, first, 3, 0)
    seg_keys = jnp.where(
        dp >= 2, seg_rows, jnp.where(dp == 1, jnp.roll(seg_rows, 1, axis=0), jnp.roll(seg_rows, 2, axis=0))
    ).reshape(3 * TOK)
    key_no = jnp.arange(3 * TOK, dtype=jnp.int32)
    gap = (jnp.arange(TOK, dtype=jnp.int32) + 2 * TOK)[:, None] - key_no[None, :]
    allowed = (
        (segment_ids[:, None] == seg_keys[None, :])
        & (gap >= 0)
        & (gap < WINDOW)
        & (key_no + (dp - 2) * TOK >= 0)[None, :]
    )
    scale = HD ** (-0.5)
    scores = jnp.where(allowed, dot(qr, kr, NT) * scale, -1e30)
    top = jnp.max(scores, axis=-1, keepdims=True)
    exps = jnp.exp(scores - top)
    probs = exps / jnp.sum(exps, axis=-1, keepdims=True)
    pb = probs.astype(BF)
    ob = dot(pb, vb, NN).astype(BF)
    u_part = dot(ob, woT, NT).astype(BF).reshape(4, QTOK, D)
    hidden_q = lax.dynamic_slice_in_dim(hidden_in, y * QTOK, QTOK, 0)
    grad_q = lax.dynamic_slice_in_dim(out_grad, y * QTOK, QTOK, 0)
    u, hmid, bin_all, ffn_all = sum_then_gather(
        mid_fn, u_part, [hidden_q, g1, g2], [(QTOK, D)] * 2, 1, True, 3, SideGather(), ffn_near
    )

    ffn_full = ffn_all.reshape(32, 3, ROWS, HALF).transpose(1, 0, 2, 3).reshape(3, D, HALF)
    wg, wu, wdT = ffn_full[0], ffn_full[1], ffn_full[2]
    bin_low = bin_all.reshape(512, D)
    gate = dot(bin_low, wg, NN)
    up = dot(bin_low, wu, NN)
    inner = math.sqrt(2.0 / math.pi)
    th = jnp.tanh(inner * (gate + 0.044715 * gate * gate * gate))
    gelu = 0.5 * gate * (1.0 + th)
    gelu_d = 0.5 * (1.0 + th) + 0.5 * gate * (1.0 - th * th) * inner * (1.0 + 3 * 0.044715 * gate * gate)
    mixed = (gelu * up).astype(BF)
    f_part = dot(mixed, wdT, NT).astype(BF).reshape(2, 4, QTOK, D)
    block, dg3, df_all, moms_all = sum_then_gather(
        ffn_out_fn, f_part, [hmid, grad_q, g3], [(QTOK, D), (1, D)], 1, True, 5, SideSwap(), moms
    )
    dfb = df_all.reshape(512, D)
    dz = dot(dfb, wdT, NN)
    dgate = (dz * up * gelu_d).astype(BF)
    dup = (dz * gelu).astype(BF)
    dbin_part = (dot(dgate, wg, NT) + dot(dup, wu, NT)).astype(BF).reshape(2, 4, QTOK, D)
    dhmid, dg1, dg2, du_all = sum_then_gather(
        ffn_in_fn,
        dbin_part,
        [hmid, u, grad_q, g1, g2],
        [(QTOK, D), (1, D), (1, D)],
        1,
        True,
        6,
    )

    dub_all = du_all.reshape(512, D)
    dub = lax.dynamic_slice_in_dim(dub_all, c * TOK, TOK, 0)
    dob = dot(dub, woT, NN).astype(BF)
    dP = dot(dob, vb, NT)
    ds = (probs * (dP - jnp.sum(probs * dP, axis=-1, keepdims=True))).astype(BF)
    dqr = dot(ds, kr, NN) * scale
    dkr = dot(ds, qr, TN) * scale
    dv = dot(pb, dob, TN)
    dkv_part = jnp.concatenate([dkr, dv], axis=1).astype(BF).reshape(3, 4, QTOK, 512)[::-1]
    (dkv_got,) = halo([(dkv_part, "split")], -1, 7)
    dkv_sum = jnp.sum(dkv_got.reshape(12, QTOK, 512).astype(F32), axis=0)
    k_own = lax.dynamic_slice_in_dim(k_raw, 2 * TOK + y * QTOK, QTOK, 0)
    cos_k = lax.dynamic_slice_in_dim(cos_q, y * QTOK, QTOK, 0)
    sin_k = lax.dynamic_slice_in_dim(sin_q, y * QTOK, QTOK, 0)
    dk, dgk = rms_back(k_own, gk, inv_rms(k_own), unrot(dkv_sum[:, :256], cos_k, sin_k))
    dq, dgq = rms_back(q_raw, gq, q_s, unrot(dqr, cos_q, sin_q))
    dkvb = jnp.concatenate([dk, dkv_sum[:, 256:]], axis=1).astype(BF)
    dqb = dq.astype(BF)
    pair = jnp.concatenate([normed, ob, dqb], axis=1)
    dkv_all, pair = exchange([(dkvb, "ag"), (pair, "ag", ("c",))], ("c", "y"), 8)
    pair = pair.reshape(512, D + 512)
    dkv_all = dkv_all.reshape(512, 2, 4, 64)
    dkv_cols = lax.dynamic_slice_in_dim(dkv_all, y, 1, 2).reshape(512, 128)
    da_part = (
        dot(
            jnp.concatenate([dqb, lax.dynamic_slice_in_dim(dkv_cols, c * TOK, TOK, 0)], axis=1),
            w_qkv,
            NT,
        )
        .astype(BF)
        .reshape(4, QTOK, D)
    )
    dg0, last_in, last_out = sum_then_gather(
        last_fn, da_part, [hidden_q, dhmid, block, g0], [(1, D)], 2, False, 10
    )
    input_grad = last_in.reshape(TOK, D).astype(F32)
    block_out = last_out.reshape(TOK, D).astype(F32)

    gain_rows = jnp.concatenate(
        [dg0, dg1, dg2, dg3, jnp.concatenate([dgq, dgk, jnp.zeros((1, D - 2 * HD), F32)], axis=1)], axis=0
    ).astype(BF)

    a_all, ob_all, dq_all = pair[:, :D], pair[:, D : D + 256], pair[:, D + 256 :]
    ob_cols = lax.dynamic_slice_in_dim(ob_all, c * 128, 128, 1)
    dq_cols = lax.dynamic_slice_in_dim(dq_all, c * 128, 128, 1)
    dk_cols = lax.dynamic_slice_in_dim(dkv_cols, c * 32, 32, 1)
    dv_cols = lax.dynamic_slice_in_dim(dkv_cols, 64 + c * 32, 32, 1)
    d_gate = dot(dgate, bin_low, TN).astype(BF)
    d_up = dot(dup, bin_low, TN).astype(BF)
    d_down = dot(mixed, dfb, TN).astype(BF)
    d_q = dot(dq_cols, a_all, TN).astype(BF)
    d_kv = dot(jnp.concatenate([dk_cols, dv_cols], axis=1), a_all, TN).astype(BF)
    d_o = dot(ob_cols, dub_all, TN).astype(BF)
    wgrads = jnp.concatenate(
        [
            d_gate.reshape(4, BLK, D),
            d_up.reshape(4, BLK, D),
            d_down.reshape(4, BLK, D),
            jnp.pad(d_q, ((0, BLK - 128), (0, 0)))[None],
            jnp.pad(d_o, ((0, BLK - 128), (0, 0)))[None],
            jnp.pad(d_kv[:32], ((0, BLK - 32), (0, 0)))[None],
            jnp.concatenate([d_kv[32:], gain_rows, jnp.zeros((BLK - 37, D), BF)], axis=0)[None],
        ],
        axis=0,
    )
    wgrad = reduce_plane(wgrads.reshape(4, 4, BLK, D), 11)

    mom = 0.95 * moms_all.reshape(D, BLK).T.astype(F32) + wgrad
    kept = jnp.where((z == 3) & (x == 3), 32, BLK)
    mom = jnp.where(jnp.arange(BLK)[:, None] < kept, mom, 0.0)
    mom_low = mom.astype(BF)
    gram_part = dot(mom_low, mom_low, TN).astype(BF).reshape(2, 16, ROWS, D)
    gram, gains_got = gram_sum(gram_part, wgrad[32:48].astype(BF), 13)
    ortho = orthogonal(gram.reshape(D, D), mom)
    gain_sum = jnp.sum(gains_got[:, :5].astype(F32), axis=0)
    gain_cols = jnp.concatenate(
        [
            gain_sum[:4].T.reshape(32, ROWS, 4),
            jnp.pad(
                gain_sum[4, : 2 * HD].reshape(2, 32, 4, 2)[:, :, y].transpose(1, 0, 2).reshape(32, 1, 4),
                ((0, 0), (0, ROWS - 1), (0, 0)),
            ),
        ],
        axis=2,
    )
    back = jnp.concatenate([ortho.astype(BF), wgrad.astype(BF)], axis=0).T.reshape(32, ROWS, 2 * BLK)
    back = jnp.concatenate([back, gain_cols.astype(BF), jnp.zeros((32, ROWS, 56), BF)], axis=2)
    (back_got,) = exchange([(back, "a2a")], ("z", "x", "c"), 14)
    o_big, o_small = from_columns(back_got[:, :, :BLK].astype(F32))
    w_big, w_small = from_columns(back_got[:, :, BLK : 2 * BLK].astype(F32))
    gains_red = back_got[30, :, 448:452].T.astype(F32)
    qk_red = back_got[30, 0, 452:456].reshape(2, 2).astype(F32)
    gain_rate = 2.0 / math.sqrt(8192)
    next_gain_moms = 0.9 * gain_moms + 0.1 * gains_red
    new_norm_gains = norm_gains - gain_rate * next_gain_moms
    next_qk_moms = 0.9 * qk_moms + 0.1 * qk_red
    new_qk_gains = qk_gains - gain_rate * next_qk_moms

    def step(columns):
        return 0.15 * 0.2 * math.sqrt(max(D, columns))

    new_query = w_query - step(1024) * o_small[0]
    new_output = w_output - step(1024) * o_small[1].T
    new_keyval = w_keyval - step(256) * jnp.stack(o_small[2:])
    new_gateup = w_gateup - step(6912) * o_big[:2]
    new_down = w_down - step(6912) * o_big[2].T
    next_query = 0.95 * mom_query + w_small[0]
    next_output = 0.95 * mom_output + w_small[1].T
    next_keyval = 0.95 * mom_keyval + jnp.stack(w_small[2:])
    next_gateup = 0.95 * mom_gateup + w_big[:2]
    next_down = 0.95 * mom_down + w_big[2].T
    return (
        block_out,
        input_grad,
        new_query,
        new_keyval,
        new_output,
        new_gateup,
        new_down,
        next_query,
        next_keyval,
        next_output,
        next_gateup,
        next_down,
        new_norm_gains,
        next_gain_moms,
        new_qk_gains,
        next_qk_moms,
    )


def solution(mesh):
    return jax.shard_map(
        local,
        mesh=mesh,
        in_specs=(
            P("dp", None),
            P("dp", None),
            P("dp"),
            P("dp", "tensor"),
            P(None, "dp", "tensor"),
            P("tensor", "dp"),
            P(None, "dp", "tensor"),
            P("tensor", "dp"),
            P(None, "dp"),
            P(None, ("dp", "tensor")),
            P("dp", "tensor"),
            P(None, "dp", "tensor"),
            P("tensor", "dp"),
            P(None, "dp", "tensor"),
            P("tensor", "dp"),
            P(None, "dp"),
            P(None, ("dp", "tensor")),
        ),
        out_specs=(
            P("dp", None),
            P("dp", None),
            P("dp", "tensor"),
            P(None, "dp", "tensor"),
            P("tensor", "dp"),
            P(None, "dp", "tensor"),
            P("tensor", "dp"),
            P("dp", "tensor"),
            P(None, "dp", "tensor"),
            P("tensor", "dp"),
            P(None, "dp", "tensor"),
            P("tensor", "dp"),
            P(None, "dp"),
            P(None, "dp"),
            P(None, ("dp", "tensor")),
            P(None, ("dp", "tensor")),
        ),
        check_vma=False,
    )
```

```python
import functools
import math

import jax
import jax.numpy as jnp
import numpy as np
from jax import lax
from jax.experimental import pallas as pl
from jax.experimental.pallas import tpu as pltpu
from jax.sharding import PartitionSpec as P

WINDOW = 512
EPSILON = 1e-06
COEF_ONE = 3.4445
COEF_TWO = -4.775
COEF_THREE = 2.0315

D = 1152
HD = 256
TOK = 256
QTOK = 64
ROWS = 36
FFT = 1728
FFP = 1792
HALF = 896
BLK = 224
PART = 192
BF = jnp.bfloat16
F32 = jnp.float32
MESH = pl.DeviceIdType.MESH

SIZES = {"z": 4, "x": 4, "c": 2, "y": 4}


def place():
    dp = lax.axis_index("dp")
    return {"z": dp // 8, "x": (dp // 2) % 4, "c": dp % 2, "y": lax.axis_index("tensor")}


def rank(at, axes):
    r = 0
    for a in axes:
        r = r * SIZES[a] + at[a]
    return r


def count(axes):
    return math.prod(SIZES[a] for a in axes)


def decode(p, axes):
    out = {}
    for a in reversed(axes):
        out[a] = p % SIZES[a]
        p = p // SIZES[a]
    return out


def moved(at, off, sign):
    return {a: (at[a] + (off[a] if sign > 0 else SIZES[a] - off[a])) % SIZES[a] if a in off else at[a] for a in at}


def device(at):
    return {"dp": at["z"] * 8 + at["x"] * 2 + at["c"], "tensor": at["y"]}


def slot(ref, mode, axes, target):
    if mode == "ag":
        return ref
    if mode == "a2a":
        return ref.at[rank(target, axes)]
    return ref.at[rank(target, mode[1])]


def exchange_body(axes, modes, subs, *refs):
    k = len(modes)
    n = count(axes)
    ins, outs = refs[:k], refs[k : 2 * k]
    send_sem, recv_sem, local_sem = refs[2 * k :]
    me = place()
    barrier = pltpu.get_barrier_semaphore()

    def greet(p, carry):
        pl.semaphore_signal(barrier, inc=1, device_id=device(moved(me, decode(p, axes), -1)), device_id_type=MESH)
        return carry

    def copies(p, arriving, items):
        off = decode(p, axes)
        target = moved(me, off, 1)
        place_of = moved(me, off, -1) if arriving else me
        return [
            pltpu.make_async_remote_copy(
                src_ref=slot(ins[i], modes[i], axes, target),
                dst_ref=outs[i].at[rank(place_of, subs[i])],
                send_sem=send_sem.at[i, p],
                recv_sem=recv_sem.at[i, p],
                device_id=device(target),
                device_id_type=MESH,
            )
            for i in items
        ]

    own = [
        pltpu.make_async_copy(slot(ins[i], modes[i], axes, me), outs[i].at[rank(me, subs[i])], local_sem.at[i])
        for i in range(k)
    ]
    lax.fori_loop(1, n, greet, 0)
    for copy in own:
        copy.start()
    pl.semaphore_wait(barrier, n - 1)
    if all(s == axes for s in subs):

        def launch(p, carry):
            for copy in copies(p, False, range(k)):
                copy.start()
            return carry

        def finish(p, carry):
            for copy in copies(p, True, range(k)):
                copy.wait()
            return carry

        lax.fori_loop(1, n, launch, 0)
        for copy in own:
            copy.wait()
        lax.fori_loop(1, n, finish, 0)
        return
    items = []
    for p in range(1, n):
        off = decode(p, axes)
        items.append((p, [i for i in range(k) if all(off[ax] == 0 for ax in axes if ax not in subs[i])]))
    for p, mine in items:
        for copy in copies(p, False, mine):
            copy.start()
    for copy in own:
        copy.wait()
    for p, mine in items:
        for copy in copies(p, True, mine):
            copy.wait()


def exchange(items, axes, cid):
    arrays = [i[0] for i in items]
    modes = [i[1] for i in items]
    subs = [i[2] if len(i) > 2 else axes for i in items]
    shapes = [
        (count(sub),) + (a.shape if m == "ag" else a.shape[1:]) for a, m, sub in zip(arrays, modes, subs)
    ]
    k, n = len(items), count(axes)
    vmem = pl.BlockSpec(memory_space=pltpu.VMEM)
    return pl.pallas_call(
        functools.partial(exchange_body, axes, modes, subs),
        out_shape=[jax.ShapeDtypeStruct(s, a.dtype) for s, a in zip(shapes, arrays)],
        in_specs=[vmem] * k,
        out_specs=[vmem] * k,
        scratch_shapes=[
            pltpu.SemaphoreType.DMA((k, n)),
            pltpu.SemaphoreType.DMA((k, n)),
            pltpu.SemaphoreType.DMA((k,)),
        ],
        compiler_params=pltpu.CompilerParams(
            collective_id=cid, has_side_effects=True, vmem_limit_bytes=32 * 1024 * 1024
        ),
    )(*arrays)


def virtual(me, p, q):
    c = me["c"]
    first = {"a": jnp.where(c == 0, me[p], me[q]), "b": jnp.where(c == 0, me[q], me[p])}

    def to(av, bv):
        return {**me, p: jnp.where(c == 0, av, bv), q: jnp.where(c == 0, bv, av)}

    return first["a"], first["b"], to


def remote(src, dst, send_sem, recv_sem, at):
    return pltpu.make_async_remote_copy(
        src_ref=src, dst_ref=dst, send_sem=send_sem, recv_sem=recv_sem, device_id=device(at), device_id_type=MESH
    )


def greet_all(places):
    barrier = pltpu.get_barrier_semaphore()
    for at in places:
        pl.semaphore_signal(barrier, inc=1, device_id=device(at), device_id_type=MESH)
    return barrier


def gather_body(block, ffn, out, near, send_sem, recv_sem, local_sem):
    me = place()
    a, b, to = virtual(me, "z", "x")
    twin = {**me, "c": 1 - me["c"]}
    a_next, a_last, a_far = (a + 1) % 4, (a + 3) % 4, (a + 2) % 4
    b_next, b_last = (b + 1) % 4, (b + 3) % 4
    barrier = greet_all([to(a_next, b), to(a_last, b), to(a, b_next), to(a, b_last)] + [twin])

    def spot(av, bv):
        at = to(av, bv)
        return out.at[me["c"], at["z"], at["x"]]

    here = spot(a, b)
    mine = near.at[a, me["c"]]
    theirs = near.at[a, 1 - me["c"]]
    own = pltpu.make_async_copy(block, here, local_sem.at[0])
    own.start()
    keep = pltpu.make_async_copy(ffn.at[me["c"]], mine, local_sem.at[1])
    keep.start()
    pl.semaphore_wait(barrier, 5)

    def sent(src, dst_here, sem, at):
        remote(src, src, send_sem.at[sem], recv_sem.at[sem], at).start()
        return remote(src, dst_here, send_sem.at[sem], recv_sem.at[sem], at)

    own.wait()
    up, down = to(a_next, b), to(a_last, b)
    first = [sent(here, spot(a_last, b), 1, up), sent(here, spot(a_next, b), 2, down)]
    there = near.at[b, me["c"]]
    remote(ffn.at[1 - me["c"]], there, send_sem.at[0], recv_sem.at[0], twin).start()
    keep.wait()
    remote(ffn.at[1 - me["c"]], theirs, send_sem.at[0], recv_sem.at[0], twin).wait()
    ffn_first = [sent(near.at[a], near.at[a_last], 17, up), sent(near.at[a], near.at[a_next], 18, down)]
    for w in first:
        w.wait()
    left, right, far = spot(a_last, b), spot(a_next, b), spot(a_far, b)
    for w in [sent(left.at[0], far.at[0], 3, up), sent(right.at[1], far.at[1], 4, down)]:
        w.wait()
    up2, down2 = to(a, b_next), to(a, b_last)
    waits = [
        (sent(spot(i, b), spot(i, b_last), 5 + 2 * i, up2), sent(spot(i, b), spot(i, b_next), 6 + 2 * i, down2))
        for i in range(4)
    ]
    for w in ffn_first:
        w.wait()
    late = [
        sent(near.at[a_last, 0], near.at[a_far, 0], 19, up),
        sent(near.at[a_next, 1], near.at[a_far, 1], 20, down),
    ]
    for i in range(4):
        w_last, w_next = waits[i]
        far = spot(i, (b + 2) % 4)
        if i < 2:
            w_last.wait()
            late += [sent(spot(i, b_last), far, 13 + i, up2), w_next]
        else:
            w_next.wait()
            late += [sent(spot(i, b_next), far, 13 + i, down2), w_last]
    for w in late:
        w.wait()
    remote(out.at[me["c"]], out.at[me["c"]], send_sem.at[21], recv_sem.at[21], twin).start()
    remote(out.at[me["c"]], out.at[1 - me["c"]], send_sem.at[21], recv_sem.at[21], twin).wait()


def gather_plane(block, ffn, cid):
    hbm = pl.BlockSpec(memory_space=pl.ANY)
    return pl.pallas_call(
        gather_body,
        out_shape=[
            jax.ShapeDtypeStruct((2, 4, 4) + block.shape, block.dtype),
            jax.ShapeDtypeStruct((4, 2) + ffn.shape[1:], ffn.dtype),
        ],
        in_specs=[hbm, hbm],
        out_specs=[hbm, hbm],
        scratch_shapes=[
            pltpu.SemaphoreType.DMA((22,)),
            pltpu.SemaphoreType.DMA((22,)),
            pltpu.SemaphoreType.DMA((2,)),
        ],
        compiler_params=pltpu.CompilerParams(collective_id=cid, has_side_effects=True),
    )(block, ffn)


class SideGather:
    sems = 16

    def shape(self, near):
        return jax.ShapeDtypeStruct((4, 4) + near.shape[1:], near.dtype)

    def places(self, me):
        a, b, to = virtual(me, "z", "x")
        return [to(a, (b + 1) % 4), to(a, (b + 3) % 4)]

    def start(self, me, near, out, send_sem, recv_sem):
        a, b, to = virtual(me, "z", "x")
        b_next, b_last = (b + 1) % 4, (b + 3) % 4
        up, down = to(a, b_next), to(a, b_last)

        def spot(av, bv):
            at = to(av, bv)
            return out.at[at["z"], at["x"]]

        def sent(src, dst, dst_here, sem, at):
            remote(src, dst, send_sem.at[sem], recv_sem.at[sem], at).start()
            return remote(src, dst_here, send_sem.at[sem], recv_sem.at[sem], at)

        self.waits = []
        for i in range(4):
            self.waits.append(
                (
                    sent(near.at[i], spot(i, b), spot(i, b_last), 2 * i, up),
                    sent(near.at[i], spot(i, b), spot(i, b_next), 2 * i + 1, down),
                )
            )
        self.late = []
        for i in range(4):
            copy = pltpu.make_async_copy(near.at[i], spot(i, b), recv_sem.at[12 + i])
            copy.start()
            self.late.append(copy)

        def middle():
            for i in range(4):
                w_last, w_next = self.waits[i]
                far = spot(i, (b + 2) % 4)
                if i < 2:
                    w_last.wait()
                    src = spot(i, b_last)
                    self.late += [sent(src, src, far, 8 + i, up), w_next]
                else:
                    w_next.wait()
                    src = spot(i, b_next)
                    self.late += [sent(src, src, far, 8 + i, down), w_last]

        self.middle = middle

    def finish(self):
        for w in self.late:
            w.wait()


class SideSwap:
    sems = 33
    axes = ("z", "x", "c")

    def shape(self, parts):
        return jax.ShapeDtypeStruct(parts.shape, parts.dtype)

    def places(self, me):
        return [moved(me, decode(p, self.axes), -1) for p in range(1, 32)]

    def start(self, me, parts, out, send_sem, recv_sem):
        def copies(p, arriving):
            off = decode(p, self.axes)
            target = moved(me, off, 1)
            spot = moved(me, off, -1) if arriving else me
            return remote(
                parts.at[rank(target, self.axes)],
                out.at[rank(spot, self.axes)],
                send_sem.at[p],
                recv_sem.at[p],
                target,
            )

        def launch(p, carry):
            copies(p, False).start()
            return carry

        def finish(p, carry):
            copies(p, True).wait()
            return carry

        lax.fori_loop(1, 32, launch, 0)
        mine = rank(me, self.axes)
        copy = pltpu.make_async_copy(parts.at[mine], out.at[mine], recv_sem.at[32])
        copy.start()
        copy.wait()
        self.finish = lambda: lax.fori_loop(1, 32, finish, 0)
        self.middle = lambda: None


def reduce_body(by0, by1, by2, by3, total, p, r1, r2, q, r3, r4, send_sem, recv_sem, local_sem):
    me = place()
    a, b, to = virtual(me, "z", "x")
    a_next, a_last, a_far = (a + 1) % 4, (a + 3) % 4, (a + 2) % 4
    b_next, b_last, b_far = (b + 1) % 4, (b + 3) % 4, (b + 2) % 4
    up, down = to(a_next, b), to(a_last, b)
    up2, down2 = to(a, b_next), to(a, b_last)
    barrier = greet_all([up, down, up2, down2])

    def at(ref, av, bv):
        w = to(av, bv)
        return ref.at[w["z"], w["x"]]

    loads = [pltpu.make_async_copy(by, p.at[i], local_sem.at[i]) for i, by in enumerate((by0, by1, by2, by3))]
    for load in loads:
        load.start()
    pl.semaphore_wait(barrier, 4)
    for load in loads:
        load.wait()
    first = []
    for i in range(4):
        first.append(remote(at(p, a_far, i), r1.at[i], send_sem.at[i], recv_sem.at[i], up if i < 2 else down))
        first[-1].start()
    second = []

    def onward(i, way, src):
        sem = 4 + 2 * i + way
        copy = remote(src, r2.at[way, i], send_sem.at[sem], recv_sem.at[sem], down if way else up)
        copy.start()
        second.append(copy)

    for i in range(4):
        onward(i, 1 if i < 2 else 0, at(p, a_last if i < 2 else a_next, i))
    for i in range(4):
        first[i].wait()
        dest = at(p, a_next if i < 2 else a_last, i)
        dest[...] = (dest[...].astype(F32) + r1[i].astype(F32)).astype(BF)
        onward(i, 0 if i < 2 else 1, dest)
    for copy in second:
        copy.wait()
    for i in range(4):
        q[i] = (at(p, a, i)[...].astype(F32) + r2[0, i].astype(F32) + r2[1, i].astype(F32)).astype(BF)
    lo, hi = pl.ds(0, BLK // 2), pl.ds(BLK // 2, BLK // 2)
    one = remote(q.at[b_far, lo], r3.at[0], send_sem.at[12], recv_sem.at[12], up2)
    two = remote(q.at[b_far, hi], r3.at[1], send_sem.at[13], recv_sem.at[13], down2)
    one.start()
    two.start()
    three = remote(q.at[b_next, hi], r4.at[0, hi], send_sem.at[14], recv_sem.at[14], up2)
    four = remote(q.at[b_last, lo], r4.at[1, lo], send_sem.at[15], recv_sem.at[15], down2)
    three.start()
    four.start()
    one.wait()
    dest = q.at[b_next, lo]
    dest[...] = (dest[...].astype(F32) + r3[0].astype(F32)).astype(BF)
    five = remote(q.at[b_next, lo], r4.at[0, lo], send_sem.at[16], recv_sem.at[16], up2)
    five.start()
    two.wait()
    dest = q.at[b_last, hi]
    dest[...] = (dest[...].astype(F32) + r3[1].astype(F32)).astype(BF)
    six = remote(q.at[b_last, hi], r4.at[1, hi], send_sem.at[17], recv_sem.at[17], down2)
    six.start()
    for copy in (three, four, five, six):
        copy.wait()
    total[...] = q[b].astype(F32) + r4[0].astype(F32) + r4[1].astype(F32)


def reduce_plane(parts, cid):
    block = parts[0].shape[1:]
    return pl.pallas_call(
        reduce_body,
        out_shape=jax.ShapeDtypeStruct(block, F32),
        in_specs=[pl.BlockSpec(memory_space=pl.ANY)] * 4,
        out_specs=pl.BlockSpec(memory_space=pltpu.VMEM),
        scratch_shapes=[
            pltpu.VMEM((4, 4) + block, BF),
            pltpu.VMEM((4,) + block, BF),
            pltpu.VMEM((2, 4) + block, BF),
            pltpu.VMEM((4,) + block, BF),
            pltpu.VMEM((2, BLK // 2, D), BF),
            pltpu.VMEM((2,) + block, BF),
            pltpu.SemaphoreType.DMA((18,)),
            pltpu.SemaphoreType.DMA((18,)),
            pltpu.SemaphoreType.DMA((4,)),
        ],
        compiler_params=pltpu.CompilerParams(
            collective_id=cid, has_side_effects=True, vmem_limit_bytes=48 * 1024 * 1024
        ),
    )(*parts)


def gram_body(kept, moms, grad, extra, gram, extras, mom, flat, parts, p, got, mine, bx, send_sem, recv_sem, local_sem):
    me = place()
    c, z = me["c"], me["z"]
    axes = ("x", "y")
    twin = {**me, "c": 1 - c}
    barrier = pltpu.get_barrier_semaphore()
    for i in range(1, 16):
        pl.semaphore_signal(barrier, inc=1, device_id=device(moved(me, decode(i, axes), -1)), device_id_type=MESH)
    for i in range(4):
        pl.semaphore_signal(barrier, inc=1, device_id=device({**twin, "y": (me["y"] + i) % 4}), device_id_type=MESH)
    new = 0.95 * moms[...].astype(F32) + grad[...]
    new = jnp.where(lax.broadcasted_iota(jnp.int32, (BLK, 1), 0) < kept[...], new, 0.0)
    mom[...] = new
    flat[...] = new.astype(BF)
    start = 0
    for j in range(D // 128):
        tall = 128 * (j + 1)
        value = dot(flat[:, pl.ds(0, tall)], flat[:, pl.ds(128 * j, 128)], TN).astype(BF)
        while tall:
            part, row = divmod(start, PART)
            size = min(tall, PART - row)
            done = 128 * (j + 1) - tall
            parts[part // 16, part % 16, pl.ds(row, size), :] = value[done : done + size]
            start, tall = start + size, tall - size
    for part in range(start // PART, 32):
        row = start % PART if part == start // PART else 0
        parts[part // 16, part % 16, pl.ds(row, PART - row), :] = jnp.zeros((PART - row, 128), BF)
    load = pltpu.make_async_copy(parts.at[c], p, local_sem.at[0])
    load.start()
    keep = pltpu.make_async_copy(extra, extras.at[rank(me, ("c", "y"))], local_sem.at[1])
    keep.start()
    pl.semaphore_wait(barrier, 19)
    swap = remote(parts.at[1 - c], got, send_sem.at[0, 0], recv_sem.at[0, 0], twin)
    swap.start()
    extra_waits = []
    for i in range(1, 8):
        off = decode(i, ("c", "y"))
        target, source = moved(me, off, 1), moved(me, off, -1)
        sems = (send_sem.at[3, i], recv_sem.at[3, i])
        remote(extra, extras.at[rank(me, ("c", "y"))], *sems, target).start()
        extra_waits.append(remote(extra, extras.at[rank(source, ("c", "y"))], *sems, target))
    load.wait()
    swap.wait()
    for i in range(16):
        p[i] = (p[i].astype(F32) + got[i].astype(F32)).astype(BF)
    waits = []
    for i in range(1, 16):
        off = decode(i, axes)
        target, source = moved(me, off, 1), moved(me, off, -1)
        sems = (send_sem.at[1, i], recv_sem.at[1, i])
        remote(p.at[rank(target, axes)], mine.at[rank(me, axes)], *sems, target).start()
        waits.append(remote(p.at[rank(target, axes)], mine.at[rank(source, axes)], *sems, target))
    own = pltpu.make_async_copy(p.at[rank(me, axes)], mine.at[rank(me, axes)], local_sem.at[0])
    own.start()
    own.wait()
    for w in waits:
        w.wait()
    sums = []
    for i in range(4):
        part = mine[4 * i].astype(F32)
        for j in range(1, 4):
            part = part + mine[4 * i + j].astype(F32)
        sums.append(part)
    whole = sums[0] + sums[1] + sums[2] + sums[3]
    for i in range(4):
        bx[i] = jnp.where(z < 3, whole, sums[i]).astype(BF)
    waits = []
    spot = gram.at[c]
    for i in range(1, 16):
        off = decode(i, axes)
        target, source = moved(me, off, 1), moved(me, off, -1)
        sems = (send_sem.at[2, i], recv_sem.at[2, i])
        remote(bx.at[target["x"]], spot.at[rank(me, axes)], *sems, target).start()
        waits.append(remote(bx.at[target["x"]], spot.at[rank(source, axes)], *sems, target))
    own = pltpu.make_async_copy(bx.at[me["x"]], spot.at[rank(me, axes)], local_sem.at[0])
    own.start()
    own.wait()
    for w in waits:
        w.wait()
    remote(gram.at[c], gram.at[c], send_sem.at[2, 0], recv_sem.at[2, 0], twin).start()
    remote(gram.at[c], gram.at[1 - c], send_sem.at[2, 0], recv_sem.at[2, 0], twin).wait()
    keep.wait()
    for w in extra_waits:
        w.wait()


def gram_sum(kept, moms, grad, extra, cid):
    vmem = pl.BlockSpec(memory_space=pltpu.VMEM)
    half = (16, PART, 128)
    return pl.pallas_call(
        gram_body,
        out_shape=[
            jax.ShapeDtypeStruct((2,) + half, BF),
            jax.ShapeDtypeStruct((8,) + extra.shape, extra.dtype),
            jax.ShapeDtypeStruct(grad.shape, F32),
        ],
        in_specs=[vmem] * 4,
        out_specs=[vmem] * 3,
        scratch_shapes=[
            pltpu.VMEM(moms.shape, BF),
            pltpu.VMEM((2,) + half, BF),
            pltpu.VMEM(half, BF),
            pltpu.VMEM(half, BF),
            pltpu.VMEM(half, BF),
            pltpu.VMEM((4,) + half[1:], BF),
            pltpu.SemaphoreType.DMA((4, 16)),
            pltpu.SemaphoreType.DMA((4, 16)),
            pltpu.SemaphoreType.DMA((2,)),
        ],
        compiler_params=pltpu.CompilerParams(
            collective_id=cid, has_side_effects=True, vmem_limit_bytes=48 * 1024 * 1024
        ),
    )(kept, moms, grad, extra)


def halo_body(sign, kinds, *refs):
    k = len(kinds)
    ins, outs = refs[:k], refs[k : 2 * k]
    send_sem, recv_sem, local_sem = refs[2 * k :]
    dp = lax.axis_index("dp")
    y = lax.axis_index("tensor")
    barrier = pltpu.get_barrier_semaphore()
    offs = [(d, t) for d in range(3) for t in range(4)]

    def dev(d, t, way):
        shift = d if way > 0 else 32 - d
        return {"dp": (dp + shift) % 32, "tensor": (y + (t if way > 0 else 4 - t)) % 4}

    for d, t in offs[1:]:
        back = dev(d, t, -1) if sign > 0 else {"dp": (dp + d) % 32, "tensor": (y + 4 - t) % 4}
        pl.semaphore_signal(barrier, inc=1, device_id=back, device_id_type=MESH)
    own = []
    copies = []
    for i, kind in enumerate(kinds):
        for p, (d, t) in enumerate(offs):
            if kind == "near" and d > 0:
                continue
            ty = (y + t) % 4
            sy = (y + 4 - t) % 4
            src = ins[i].at[pl.ds(pl.multiple_of((2 - d) * TOK + ty * QTOK, QTOK), QTOK)] if kind == "split" else ins[i]
            tdp = (dp + d) % 32 if sign > 0 else (dp + 32 - d) % 32
            if kind == "near":
                to, frm = outs[i].at[y], outs[i].at[sy]
            elif kind == "all":
                rows = pl.ds((2 - d) * TOK, TOK)
                to, frm = (outs[i].at[rows, pl.ds(pl.multiple_of(at * 128, 128), 128)] for at in (y, sy))
            else:
                to, frm = outs[i].at[d, y], outs[i].at[d, sy]
            if p == 0:
                own.append(pltpu.make_async_copy(src, to, local_sem.at[i]))
                continue
            args = dict(send_sem=send_sem.at[i, p], recv_sem=recv_sem.at[i, p], device_id={"dp": tdp, "tensor": ty}, device_id_type=MESH)
            copies.append(
                (
                    pltpu.make_async_remote_copy(src_ref=src, dst_ref=to, **args),
                    pltpu.make_async_remote_copy(src_ref=src, dst_ref=frm, **args),
                )
            )
    for copy in own:
        copy.start()
    pl.semaphore_wait(barrier, len(offs) - 1)
    for out_copy, _ in copies:
        out_copy.start()
    for copy in own:
        copy.wait()
    for _, in_copy in copies:
        in_copy.wait()


def halo(items, sign, cid):
    arrays = [a for a, _ in items]
    kinds = [m for _, m in items]
    shapes = []
    for a, m in items:
        shapes.append({"near": (4,) + a.shape, "all": (3 * TOK, 512), "split": (3, 4, QTOK, 512)}[m])
    k = len(items)
    return pl.pallas_call(
        functools.partial(halo_body, sign, kinds),
        out_shape=[jax.ShapeDtypeStruct(s, a.dtype) for s, a in zip(shapes, arrays)],
        in_specs=[pl.BlockSpec(memory_space=pl.ANY)] * k,
        out_specs=[pl.BlockSpec(memory_space=pl.ANY)] * k,
        scratch_shapes=[
            pltpu.SemaphoreType.DMA((k, 12)),
            pltpu.SemaphoreType.DMA((k, 12)),
            pltpu.SemaphoreType.DMA((k,)),
        ],
        compiler_params=pltpu.CompilerParams(collective_id=cid, has_side_effects=True),
    )(*arrays)


def sum_body(fn, both, spread, side, n_extra, n_local, n_ag, *refs):
    if side is not None:
        side_in, side_out, side_send, side_recv = refs[0], refs[1 + 1 + n_extra + n_local + n_ag], refs[-2], refs[-1]
        refs = refs[1 : 2 + n_extra + n_local + n_ag] + refs[3 + n_extra + n_local + n_ag : -2]
    parts = refs[0]
    extras = refs[1 : 1 + n_extra]
    locals_ = refs[1 + n_extra : 1 + n_extra + n_local]
    gathers = refs[1 + n_extra + n_local : 1 + n_extra + n_local + n_ag]
    pre, recv, agbuf, send_sem, recv_sem, local_sem = refs[1 + n_extra + n_local + n_ag :]
    me = place()
    c, y = me["c"], me["y"]
    twin = {**me, "c": 1 - c}
    near = [(moved(me, {"y": i}, 1), moved(me, {"y": i}, -1)) for i in range(1, 4)]
    use_twin = both or spread
    places = [source for _, source in near] + ([twin] if use_twin else [])
    if side is not None:
        places += side.places(me)
    barrier = greet_all(places)
    pl.semaphore_wait(barrier, len(places))
    if both:
        swap = remote(parts.at[1 - c], pre, send_sem.at[0], recv_sem.at[0], twin)
        swap.start()
        if side is not None:
            side.start(me, side_in, side_out, side_send, side_recv)
        swap.wait()
        for i in range(4):
            pre[i] = (pre[i].astype(F32) + parts[c, i].astype(F32)).astype(BF)
        mine = pre
    else:
        mine = parts
    waits = []
    for i, (target, source) in enumerate(near):
        sems = (send_sem.at[1 + i], recv_sem.at[1 + i])
        remote(mine.at[target["y"]], recv.at[i], *sems, target).start()
        waits.append(remote(mine.at[target["y"]], recv.at[i], *sems, target))
    if side is not None and not both:
        side.start(me, side_in, side_out, side_send, side_recv)
    total = mine[y].astype(F32)
    for i in range(3):
        waits[i].wait()
        total = total + recv[i].astype(F32)
    local_vals, ag_vals = fn(total, *[e[...] for e in extras])
    for i, value in enumerate(ag_vals):
        agbuf[i] = value.astype(BF)
    waits, own = [], []
    for j in range(n_ag):
        out = gathers[j].at[c] if spread else gathers[j]
        for i, (target, source) in enumerate(near):
            sems = (send_sem.at[4 + 3 * j + i], recv_sem.at[4 + 3 * j + i])
            remote(agbuf.at[j], out.at[y], *sems, target).start()
            waits.append(remote(agbuf.at[j], out.at[source["y"]], *sems, target))
        own.append(pltpu.make_async_copy(agbuf.at[j], out.at[y], local_sem.at[j]))
        own[-1].start()
    for ref, value in zip(locals_, local_vals):
        ref[...] = value
    if side is not None:
        side.middle()
    for copy in own + waits:
        copy.wait()
    if spread:
        for j in range(n_ag):
            g = gathers[j]
            sems = (send_sem.at[4 + 3 * n_ag + j], recv_sem.at[4 + 3 * n_ag + j])
            remote(g.at[c], g.at[c], *sems, twin).start()
            remote(g.at[c], g.at[1 - c], *sems, twin).wait()
    if side is not None:
        side.finish()


def sum_then_gather(fn, parts, extras, local_shapes, n_ag, spread, cid, side=None, side_in=None):
    both = parts.ndim == 4
    rows = parts.shape[-2:]
    vmem = pl.BlockSpec(memory_space=pltpu.VMEM)
    gathered = ((2, 4) if spread else (4,)) + rows
    n_sem = 4 + 4 * n_ag
    hbm = pl.BlockSpec(memory_space=pl.ANY)
    more = side is not None
    return pl.pallas_call(
        functools.partial(sum_body, fn, both, spread, side, len(extras), len(local_shapes), n_ag),
        out_shape=[jax.ShapeDtypeStruct(s, F32) for s in local_shapes]
        + [jax.ShapeDtypeStruct(gathered, BF)] * n_ag
        + ([side.shape(side_in)] if more else []),
        in_specs=[hbm] * more + [vmem] * (1 + len(extras)),
        out_specs=[vmem] * (len(local_shapes) + n_ag) + [hbm] * more,
        scratch_shapes=[
            pltpu.VMEM((4,) + rows, BF),
            pltpu.VMEM((3,) + rows, BF),
            pltpu.VMEM((n_ag,) + rows, BF),
            pltpu.SemaphoreType.DMA((n_sem,)),
            pltpu.SemaphoreType.DMA((n_sem,)),
            pltpu.SemaphoreType.DMA((n_ag,)),
        ]
        + ([pltpu.SemaphoreType.DMA((side.sems,))] * 2 if more else []),
        compiler_params=pltpu.CompilerParams(
            collective_id=cid, has_side_effects=True, vmem_limit_bytes=32 * 1024 * 1024
        ),
    )(*([side_in] if more else []), parts, *extras)


def inv_rms(values):
    return lax.rsqrt(jnp.mean(values * values, axis=-1, keepdims=True) + EPSILON)


def rms_back(values, gain, s, grad):
    scaled = gain * grad
    dv = s * scaled - values * (s * s * s * jnp.mean(scaled * values, axis=-1, keepdims=True))
    return dv, jnp.sum(grad * values * s, axis=0, keepdims=True)


def rot(values, cosine, sine):
    front, back = values[:, :128], values[:, 128:]
    return jnp.concatenate([front * cosine - back * sine, back * cosine + front * sine], axis=-1)


def unrot(values, cosine, sine):
    return rot(values, cosine, -sine)


def mid_fn(u, hidden, g1, g2):
    hmid = hidden + u * inv_rms(u) * g1
    return [u, hmid], [hmid * inv_rms(hmid) * g2]


def ffn_out_fn(f, hmid, out_grad, g3):
    s = inv_rms(f)
    block = hmid + f * s * g3
    df, dg3 = rms_back(f, g3, s, out_grad)
    return [block, dg3], [df]


def ffn_in_fn(dbin, hmid, u, out_grad, g1, g2):
    dm, dg2 = rms_back(hmid, g2, inv_rms(hmid), dbin)
    dhmid = out_grad + dm
    du, dg1 = rms_back(u, g1, inv_rms(u), dhmid)
    return [dhmid, dg1, dg2], [du]


def last_fn(da, hidden, dhmid, block, g0):
    dh, dg0 = rms_back(hidden, g0, inv_rms(hidden), da)
    return [dg0], [dhmid + dh, block]


def dot(a, b, dims):
    return lax.dot_general(a, b, (dims, ((), ())), preferred_element_type=F32)


NN = ((1,), (0,))
NT = ((1,), (1,))
TN = ((0,), (0,))


def ffn_body(blocks, tokens, dense, gate, up, mixed, f):
    for k in range(32):
        for m in range(3):
            dense[m, pl.ds(ROWS * k, ROWS), :] = blocks[k, pl.ds(ROWS * m, ROWS), :]
    inner = math.sqrt(2.0 / math.pi)

    def body(i, carry):
        rows = pl.ds(pl.multiple_of(i * TOK, TOK), TOK)
        low = tokens[rows, :]
        g = dot(low, dense[0], NN)
        gate[rows, :] = g
        u = dot(low, dense[1], NN)
        up[rows, :] = u
        th = jnp.tanh(inner * (g + 0.044715 * g * g * g))
        z = (0.5 * g * (1.0 + th) * u).astype(BF)
        mixed[rows, :] = z
        f[rows, :] = dot(z, dense[2], NT).astype(BF)
        return carry

    lax.fori_loop(0, 2, body, 0)


def ffn_forward(blocks, tokens):
    vmem = pl.BlockSpec(memory_space=pltpu.VMEM)
    return pl.pallas_call(
        ffn_body,
        out_shape=[
            jax.ShapeDtypeStruct((3, D, HALF), BF),
            jax.ShapeDtypeStruct((512, HALF), F32),
            jax.ShapeDtypeStruct((512, HALF), F32),
            jax.ShapeDtypeStruct((512, HALF), BF),
            jax.ShapeDtypeStruct((512, D), BF),
        ],
        in_specs=[vmem] * 2,
        out_specs=[vmem] * 5,
        compiler_params=pltpu.CompilerParams(vmem_limit_bytes=48 * 1024 * 1024),
    )(blocks, tokens)


def attention_body(kv, sort, q_raw, gq, gk, cosine, sine, seg_q, seg_k, woT, qr, kr, vb, k_own, probs, ob, u):
    sorted_kv = dot(kv[...], sort[...], NN)
    k_raw = sorted_kv[:, :HD]
    v = sorted_kv[:, HD:].astype(BF)
    vb[...] = v
    k_own[...] = k_raw[2 * TOK :]
    k = rot(k_raw * inv_rms(k_raw) * gk[...], cosine[...], sine[...]).astype(BF)
    kr[...] = k
    raw = q_raw[...]
    q = rot(raw * inv_rms(raw) * gq[...], cosine[pl.ds(2 * TOK, TOK), :], sine[pl.ds(2 * TOK, TOK), :]).astype(BF)
    qr[...] = q
    shape = (TOK, 3 * TOK)
    gap = lax.broadcasted_iota(jnp.int32, shape, 0) + 2 * TOK - lax.broadcasted_iota(jnp.int32, shape, 1)
    allowed = (seg_q[...] == seg_k[...]) & (gap >= 0) & (gap < WINDOW)
    scores = jnp.where(allowed, dot(q, k, NT) * (HD**-0.5), -1e30)
    exps = jnp.exp(scores - jnp.max(scores, axis=-1, keepdims=True))
    p = exps / jnp.sum(exps, axis=-1, keepdims=True)
    probs[...] = p
    o = dot(p.astype(BF), v, NN).astype(BF)
    ob[...] = o
    u[...] = dot(o, woT[...], NT).astype(BF)


def attention(*args):
    vmem = pl.BlockSpec(memory_space=pltpu.VMEM)
    wide = 3 * TOK
    shapes = [
        ((TOK, HD), BF),
        ((wide, HD), BF),
        ((wide, HD), BF),
        ((TOK, HD), F32),
        ((TOK, wide), F32),
        ((TOK, HD), BF),
        ((TOK, D), BF),
    ]
    return pl.pallas_call(
        attention_body,
        out_shape=[jax.ShapeDtypeStruct(s, t) for s, t in shapes],
        in_specs=[vmem] * len(args),
        out_specs=[vmem] * len(shapes),
        compiler_params=pltpu.CompilerParams(vmem_limit_bytes=32 * 1024 * 1024),
    )(*args)


def attention_back_body(*refs):
    du_all, woT, vb, probs, kr, qr, q_raw, gq, gk, cosine, sine, k_own, normed, ob = refs[:14]
    dkv_all, a_all, ob_all, dq_all, dgq, dgk = refs[14:20]
    part, got, dkvb, send_sem, recv_sem, local_sem = refs[20:]
    me = place()
    c, y, dp = me["c"], me["y"], lax.axis_index("dp")
    twin = {**me, "c": 1 - c}

    def along(d, t):
        at = (dp + d + 32) % 32
        return {"z": at // 8, "x": (at // 2) % 4, "c": at % 2, "y": (y + t + 4) % 4}

    offs = [(d, t) for d in range(3) for t in range(4)][1:]
    group = [decode(p, ("c", "y")) for p in range(1, 8)]
    places = [along(d, -t) for d, t in offs] + [moved(me, off, -1) for off in group]
    barrier = greet_all(places)
    pl.semaphore_wait(barrier, len(places))
    waits = []

    def to_twin(src, out, sem):
        remote(src, out.at[c], send_sem.at[sem], recv_sem.at[sem], twin).start()
        waits.append(remote(src, out.at[1 - c], send_sem.at[sem], recv_sem.at[sem], twin))
        own = pltpu.make_async_copy(src, out.at[c], local_sem.at[sem])
        own.start()
        waits.append(own)

    to_twin(normed, a_all, 0)
    to_twin(ob, ob_all, 1)
    scale = HD**-0.5
    dub = du_all[pl.ds(pl.multiple_of(c * TOK, TOK), TOK), :]
    dob = dot(dub, woT[...], NN).astype(BF)
    p = probs[...]
    dp_ = dot(dob, vb[...], NT)
    ds = (p * (dp_ - jnp.sum(p * dp_, axis=-1, keepdims=True))).astype(BF)
    part[:, pl.ds(0, HD)] = (dot(ds, qr[...], TN) * scale).astype(BF)
    part[:, pl.ds(HD, HD)] = dot(p.astype(BF), dob, TN).astype(BF)
    own = pltpu.make_async_copy(part.at[pl.ds(pl.multiple_of(2 * TOK + y * QTOK, QTOK), QTOK)], got.at[0, y], local_sem.at[2])
    own.start()
    halo_waits = []
    for i, (d, t) in enumerate(offs):
        target = along(-d, t)
        src = part.at[pl.ds(pl.multiple_of((2 - d) * TOK + target["y"] * QTOK, QTOK), QTOK)]
        sems = (send_sem.at[3 + i], recv_sem.at[3 + i])
        remote(src, got.at[d, y], *sems, target).start()
        halo_waits.append(remote(src, got.at[d, (y + 4 - t) % 4], *sems, target))
    raw = q_raw[...]
    dqr = dot(ds, kr[...], NN) * scale
    here = pl.ds(2 * TOK, TOK)
    dq, dg = rms_back(raw, gq[...], inv_rms(raw), unrot(dqr, cosine[here, :], sine[here, :]))
    dgq[...] = dg
    dq_all[c] = dq.astype(BF)
    remote(dq_all.at[c], dq_all.at[c], send_sem.at[2], recv_sem.at[2], twin).start()
    waits.append(remote(dq_all.at[c], dq_all.at[1 - c], send_sem.at[2], recv_sem.at[2], twin))
    own.wait()
    for w in halo_waits:
        w.wait()
    total = got[0, 0].astype(F32)
    for i in range(1, 12):
        total = total + got[i // 4, i % 4].astype(F32)
    k = k_own[pl.ds(pl.multiple_of(y * QTOK, QTOK), QTOK), :]
    rows = pl.ds(pl.multiple_of(2 * TOK + y * QTOK, QTOK), QTOK)
    dk, dg = rms_back(k, gk[...], inv_rms(k), unrot(total[:, :HD], cosine[rows, :], sine[rows, :]))
    dgk[...] = dg
    dkvb[:, pl.ds(0, HD)] = dk.astype(BF)
    dkvb[:, pl.ds(HD, HD)] = total[:, HD:].astype(BF)
    own = pltpu.make_async_copy(dkvb, dkv_all.at[c, y], local_sem.at[3])
    own.start()
    waits.append(own)
    for i, off in enumerate(group):
        target, source = moved(me, off, 1), moved(me, off, -1)
        sems = (send_sem.at[14 + i], recv_sem.at[14 + i])
        remote(dkvb, dkv_all.at[c, y], *sems, target).start()
        waits.append(remote(dkvb, dkv_all.at[source["c"], source["y"]], *sems, target))
    for w in waits:
        w.wait()


def attention_back(cid, *args):
    vmem = pl.BlockSpec(memory_space=pltpu.VMEM)
    shapes = [
        ((2, 4, QTOK, 512), BF),
        ((2, TOK, D), BF),
        ((2, TOK, HD), BF),
        ((2, TOK, HD), BF),
        ((1, HD), F32),
        ((1, HD), F32),
    ]
    return pl.pallas_call(
        attention_back_body,
        out_shape=[jax.ShapeDtypeStruct(s, t) for s, t in shapes],
        in_specs=[vmem] * len(args),
        out_specs=[vmem] * len(shapes),
        scratch_shapes=[
            pltpu.VMEM((3 * TOK, 512), BF),
            pltpu.VMEM((3, 4, QTOK, 512), BF),
            pltpu.VMEM((QTOK, 512), BF),
            pltpu.SemaphoreType.DMA((21,)),
            pltpu.SemaphoreType.DMA((21,)),
            pltpu.SemaphoreType.DMA((4,)),
        ],
        compiler_params=pltpu.CompilerParams(
            collective_id=cid, has_side_effects=True, vmem_limit_bytes=40 * 1024 * 1024
        ),
    )(*args)


def rope_tables():
    freqs = 10000.0 ** (-np.arange(128, dtype=np.float64) * 2.0 / 256)
    base = (np.arange(32, dtype=np.float64) - 2)[:, None] * 256 * freqs[None]
    step = np.arange(768, dtype=np.float64)[:, None] * freqs[None]
    return [t.astype(np.float32) for t in (np.cos(base), np.sin(base), np.cos(step), np.sin(step))]


def to_columns(ffn, attn):
    big = jnp.pad(ffn, ((0, 0), (0, 0), (0, FFP - FFT))).reshape(3, ROWS, 2, 4, BLK)
    big = big.transpose(0, 3, 2, 1, 4).reshape(24, ROWS, BLK)
    small = []
    for piece in attn:
        half = piece.shape[1] // 2
        piece = piece.reshape(ROWS, 2, half).transpose(1, 0, 2)
        small.append(jnp.pad(piece, ((0, 0), (0, 0), (0, BLK - half))))
    return jnp.concatenate([big] + small, axis=0)


def from_columns(blocks):
    big = blocks[:24].reshape(3, 4, 2, ROWS, BLK).transpose(0, 3, 2, 1, 4).reshape(3, ROWS, FFP)[:, :, :FFT]
    small = []
    for i, half in enumerate((128, 128, 32, 32)):
        piece = blocks[24 + 2 * i : 26 + 2 * i, :, :half]
        small.append(piece.transpose(1, 0, 2).reshape(ROWS, 2 * half))
    return big, small


def block_row(i, j):
    return 128 * (j * (j + 1) // 2 + i)


def chain_body(side, side_in, gram, mom, x, side_out, a, r, t, side_send, side_recv):
    me = place()
    places = side.places(me)
    barrier = greet_all(places)
    pl.semaphore_wait(barrier, len(places))
    side.start(me, side_in, side_out, side_send, side_recv)
    eye = lax.broadcasted_iota(jnp.int32, (128, 128), 0) == lax.broadcasted_iota(jnp.int32, (128, 128), 1)
    total = jnp.zeros((128, 128), F32)
    for i in range(D // 128):
        total = total + jnp.where(eye, gram[pl.ds(block_row(i, i), 128), :].astype(F32), 0.0)
    diag = jnp.sum(jnp.sum(total, axis=1, keepdims=True), axis=0, keepdims=True)
    inv = 1.0 / (jnp.sqrt(diag) + 1e-07)
    step = 384

    def by_rows(fn):
        def body(i, carry):
            fn(pl.ds(pl.multiple_of(i * step, step), step))
            return carry

        lax.fori_loop(0, D // step, body, 0)

    def poly(rows):
        low = a[rows, :]
        r[rows, :] = (COEF_TWO * low.astype(F32) + COEF_THREE * dot(low, a[...], NN)).astype(BF)

    def once(rows):
        low = a[rows, :]
        t[rows, :] = (COEF_ONE * low.astype(F32) + dot(low, r[...], NN)).astype(BF)

    def twice(rows):
        low = t[rows, :]
        a[rows, :] = (COEF_ONE * low.astype(F32) + dot(low, r[...], NN)).astype(BF)

    for j in range(D // 128):
        for i in range(j + 1):
            block = gram[pl.ds(block_row(i, j), 128), :].astype(F32) * (inv * inv)
            a[pl.ds(128 * i, 128), pl.ds(128 * j, 128)] = block.astype(BF)
            if i < j:
                a[pl.ds(128 * j, 128), pl.ds(128 * i, 128)] = block.T.astype(BF)
    x[...] = mom[...] * inv
    for i in range(3):
        by_rows(poly)
        x[...] = COEF_ONE * x[...] + dot(x[...].astype(BF), r[...], NN)
        if i < 2:
            by_rows(once)
            by_rows(twice)
    side.finish()


def orthogonal(gram, columns, side_in, cid):
    side = SideSwap()
    vmem = pl.BlockSpec(memory_space=pltpu.VMEM)
    hbm = pl.BlockSpec(memory_space=pl.ANY)
    return pl.pallas_call(
        functools.partial(chain_body, side),
        out_shape=[jax.ShapeDtypeStruct(columns.shape, F32), side.shape(side_in)],
        in_specs=[hbm, vmem, vmem],
        out_specs=[vmem, hbm],
        scratch_shapes=[pltpu.VMEM((D, D), BF)] * 3 + [pltpu.SemaphoreType.DMA((side.sems,))] * 2,
        compiler_params=pltpu.CompilerParams(
            collective_id=cid, has_side_effects=True, vmem_limit_bytes=48 * 1024 * 1024
        ),
    )(side_in, gram, columns)


def local(
    hidden_in,
    out_grad,
    segment_ids,
    w_query,
    w_keyval,
    w_output,
    w_gateup,
    w_down,
    norm_gains,
    qk_gains,
    mom_query,
    mom_keyval,
    mom_output,
    mom_gateup,
    mom_down,
    gain_moms,
    qk_moms,
):
    dp = lax.axis_index("dp")
    y = lax.axis_index("tensor")
    z, x, c = dp // 8, (dp // 2) % 4, dp % 2

    ffn_w = jnp.concatenate([w_gateup, w_down.T[None]], axis=0).astype(BF)
    ffn_w = jnp.pad(ffn_w, ((0, 0), (0, 0), (0, FFP - FFT))).reshape(3, ROWS, 2, HALF).transpose(2, 0, 1, 3)
    ffn_w = jnp.pad(ffn_w.reshape(2, 3 * ROWS, HALF), ((0, 0), (0, 4), (0, 0)))
    moms = to_columns(
        jnp.concatenate([mom_gateup, mom_down.T[None]], axis=0).astype(BF),
        [m.astype(BF) for m in (mom_query, mom_output.T, mom_keyval[0], mom_keyval[1])],
    )

    segs = jnp.pad(segment_ids.astype(F32).reshape(4, 64), ((0, ROWS - 4), (0, 0)))
    attn_w = jnp.stack(
        [
            jnp.concatenate([w_query, w_keyval[0], w_keyval[1]], axis=1),
            jnp.concatenate(
                [
                    w_output.T,
                    norm_gains.T,
                    jnp.broadcast_to(qk_gains.reshape(1, 4), (ROWS, 4)),
                    segs,
                    jnp.zeros((ROWS, 56), F32),
                ],
                axis=1,
            ),
        ]
    ).astype(BF)
    attn_w = jnp.pad(attn_w, ((0, 0), (0, 12), (0, 0)))
    attn_got, ffn_near = gather_plane(attn_w, ffn_w, 1)
    attn_all = attn_got[..., :ROWS, :].transpose(3, 1, 2, 0, 4, 5).reshape(2, 32, ROWS, 384)
    w_qkv = attn_all[0].reshape(D, 384)
    wq, wkv = w_qkv[:, :256], w_qkv[:, 256:]
    woT = attn_all[1, :, :, :256].reshape(D, 256)
    gains = attn_all[1, :, :, 256:260].reshape(D, 4).T.astype(F32)
    g0, g1, g2, g3 = (gains[i : i + 1] for i in range(4))
    qk_mine = attn_all[1, :, 0, 260:264].reshape(32, 2, 2).transpose(1, 0, 2).reshape(2, 64)
    qk_mine = jnp.pad(qk_mine, ((0, 14), (0, 64)))
    segs_all = attn_all[1, :, :4, 264:328].reshape(32, TOK).astype(jnp.int32)

    cos_b, sin_b, cos_s, sin_s = (jnp.asarray(t) for t in rope_tables())
    cb = lax.dynamic_slice_in_dim(cos_b, dp, 1, 0)
    sb = lax.dynamic_slice_in_dim(sin_b, dp, 1, 0)
    cosine = cb * cos_s - sb * sin_s
    sine = sb * cos_s + cb * sin_s

    normed = (hidden_in * inv_rms(hidden_in) * g0).astype(BF)
    proj = dot(normed, w_qkv, NN)
    q_raw = proj[:, :256]
    kv_all, qk_all = halo([(proj[:, 256:].astype(BF), "all"), (qk_mine, "near")], 1, 2)
    qk_full = qk_all[:, :2, :64].reshape(4, 2, 32, 2).transpose(1, 2, 0, 3).reshape(2, HD).astype(F32)
    gq, gk = qk_full[0:1], qk_full[1:2]
    order = np.arange(512)
    sort = np.zeros((512, 512), np.float32)
    sort[(order % 256) // 64 * 128 + order // 256 * 64 + order % 64, order] = 1.0
    first = jnp.maximum(dp - 2, 0)
    seg_rows = lax.dynamic_slice_in_dim(segs_all, first, 3, 0)
    seg_keys = jnp.where(
        dp >= 2, seg_rows, jnp.where(dp == 1, jnp.roll(seg_rows, 1, axis=0), jnp.roll(seg_rows, 2, axis=0))
    ).reshape(3 * TOK)
    seg_keys = jnp.where(jnp.arange(3 * TOK) >= (2 - dp) * TOK, seg_keys, -1)
    qr, kr, vb, k_own, probs, ob, u_part = attention(
        kv_all, jnp.asarray(sort, BF), q_raw, gq, gk, cosine, sine, segment_ids[:, None], seg_keys[None, :], woT
    )
    u_part = u_part.reshape(4, QTOK, D)
    hidden_q = lax.dynamic_slice_in_dim(hidden_in, y * QTOK, QTOK, 0)
    grad_q = lax.dynamic_slice_in_dim(out_grad, y * QTOK, QTOK, 0)
    u, hmid, bin_all, ffn_all = sum_then_gather(
        mid_fn, u_part, [hidden_q, g1, g2], [(QTOK, D)] * 2, 1, True, 3, SideGather(), ffn_near
    )

    bin_low = bin_all.reshape(512, D)
    dense, gate, up, mixed, f_part = ffn_forward(ffn_all.reshape(32, 112, HALF), bin_low)
    wg, wu, wdT = dense[0], dense[1], dense[2]
    inner = math.sqrt(2.0 / math.pi)
    th = jnp.tanh(inner * (gate + 0.044715 * gate * gate * gate))
    gelu = 0.5 * gate * (1.0 + th)
    gelu_d = 0.5 * (1.0 + th) + 0.5 * gate * (1.0 - th * th) * inner * (1.0 + 3 * 0.044715 * gate * gate)
    f_part = f_part.reshape(2, 4, QTOK, D)
    block, dg3, df_all, moms_all = sum_then_gather(
        ffn_out_fn, f_part, [hmid, grad_q, g3], [(QTOK, D), (1, D)], 1, True, 5, SideSwap(), moms
    )
    moms_cols = moms_all.reshape(D, BLK).T
    dfb = df_all.reshape(512, D)
    dz = dot(dfb, wdT, NN)
    dgate = (dz * up * gelu_d).astype(BF)
    dup = (dz * gelu).astype(BF)
    dbin_part = (dot(dgate, wg, NT) + dot(dup, wu, NT)).astype(BF).reshape(2, 4, QTOK, D)
    dhmid, dg1, dg2, du_all = sum_then_gather(
        ffn_in_fn,
        dbin_part,
        [hmid, u, grad_q, g1, g2],
        [(QTOK, D), (1, D), (1, D)],
        1,
        True,
        6,
    )

    dub_all = du_all.reshape(512, D)
    dkv_all, a_all, ob_all, dq_all, dgq, dgk = attention_back(
        7, dub_all, woT, vb, probs, kr, qr, q_raw, gq, gk, cosine, sine, k_own, normed, ob
    )
    dqb = lax.dynamic_slice_in_dim(dq_all, c, 1, 0)[0]
    dkv_all = dkv_all.reshape(512, 512)
    a_all, ob_all, dq_all = a_all.reshape(512, D), ob_all.reshape(512, HD), dq_all.reshape(512, HD)
    src, col = jnp.arange(512)[:, None], jnp.arange(128)[None, :]
    pick_y = (src == col // 64 * 256 + y * 64 + col % 64).astype(BF)
    col = col[:, :64]
    pick_c = (src == col // 32 * 256 + y * 64 + c * 32 + col % 32).astype(BF)
    dkv_mine = lax.dynamic_slice_in_dim(dkv_all, c * TOK, TOK, 0)
    dkv_y = dot(dkv_mine, pick_y, NN).astype(BF)
    dkv_cols = dot(dkv_all, pick_c, NN).astype(BF)
    da_part = (
        dot(
            jnp.concatenate([dqb, dkv_y], axis=1),
            w_qkv,
            NT,
        )
        .astype(BF)
        .reshape(4, QTOK, D)
    )
    dg0, last_in, last_out = sum_then_gather(
        last_fn, da_part, [hidden_q, dhmid, block, g0], [(1, D)], 2, False, 10
    )
    input_grad = last_in.reshape(TOK, D).astype(F32)
    block_out = last_out.reshape(TOK, D).astype(F32)

    gain_rows = jnp.concatenate(
        [dg0, dg1, dg2, dg3, jnp.concatenate([dgq, dgk, jnp.zeros((1, D - 2 * HD), F32)], axis=1)], axis=0
    ).astype(BF)

    ob_cols = lax.dynamic_slice_in_dim(ob_all, c * 128, 128, 1)
    dq_cols = lax.dynamic_slice_in_dim(dq_all, c * 128, 128, 1)
    d_gate = dot(dgate, bin_low, TN).astype(BF)
    d_up = dot(dup, bin_low, TN).astype(BF)
    d_down = dot(mixed, dfb, TN).astype(BF)
    d_q = dot(dq_cols, a_all, TN).astype(BF)
    d_kv = dot(dkv_cols, a_all, TN).astype(BF)
    d_o = dot(ob_cols, dub_all, TN).astype(BF)
    small = jnp.stack(
        [
            jnp.pad(d_q, ((0, BLK - 128), (0, 0))),
            jnp.pad(d_o, ((0, BLK - 128), (0, 0))),
            jnp.pad(d_kv[:32], ((0, BLK - 32), (0, 0))),
            jnp.concatenate([d_kv[32:], gain_rows, jnp.zeros((BLK - 37, D), BF)], axis=0),
        ]
    )
    wgrad = reduce_plane([d_gate.reshape(4, BLK, D), d_up.reshape(4, BLK, D), d_down.reshape(4, BLK, D), small], 11)

    kept = jnp.where((z == 3) & (x == 3), 32, BLK).reshape(1, 1)
    gram, gains_got, mom = gram_sum(kept, moms_cols, wgrad, wgrad[32:48].astype(BF), 13)
    gain_sum = jnp.sum(gains_got[:, :5].astype(F32), axis=0)
    gain_cols = jnp.concatenate(
        [
            gain_sum[:4].T.reshape(32, ROWS, 4),
            jnp.pad(
                gain_sum[4, : 2 * HD].reshape(2, 32, 4, 2)[:, :, y].transpose(1, 0, 2).reshape(32, 1, 4),
                ((0, 0), (0, ROWS - 1), (0, 0)),
            ),
        ],
        axis=2,
    )
    w_back = jnp.concatenate(
        [wgrad.astype(BF).T.reshape(32, ROWS, BLK), gain_cols.astype(BF), jnp.zeros((32, ROWS, 24), BF)], axis=2
    )
    ortho, w_got = orthogonal(gram.reshape(32 * PART, 128), mom, w_back, 12)
    w_big, w_small = from_columns(w_got[:, :, :BLK].astype(F32))
    gains_red = w_got[30, :, 224:228].T.astype(F32)
    qk_red = w_got[30, 0, 228:232].reshape(2, 2).astype(F32)
    o_back = ortho.astype(BF).T.reshape(32, ROWS, BLK)
    (o_got,) = exchange([(o_back, "a2a")], ("z", "x", "c"), 14)
    o_big, o_small = from_columns(o_got.astype(F32))
    gain_rate = 2.0 / math.sqrt(8192)
    next_gain_moms = 0.9 * gain_moms + 0.1 * gains_red
    new_norm_gains = norm_gains - gain_rate * next_gain_moms
    next_qk_moms = 0.9 * qk_moms + 0.1 * qk_red
    new_qk_gains = qk_gains - gain_rate * next_qk_moms

    def step(columns):
        return 0.15 * 0.2 * math.sqrt(max(D, columns))

    new_query = w_query - step(1024) * o_small[0]
    new_output = w_output - step(1024) * o_small[1].T
    new_keyval = w_keyval - step(256) * jnp.stack(o_small[2:])
    new_gateup = w_gateup - step(6912) * o_big[:2]
    new_down = w_down - step(6912) * o_big[2].T
    next_query = 0.95 * mom_query + w_small[0]
    next_output = 0.95 * mom_output + w_small[1].T
    next_keyval = 0.95 * mom_keyval + jnp.stack(w_small[2:])
    next_gateup = 0.95 * mom_gateup + w_big[:2]
    next_down = 0.95 * mom_down + w_big[2].T
    return (
        block_out,
        input_grad,
        new_query,
        new_keyval,
        new_output,
        new_gateup,
        new_down,
        next_query,
        next_keyval,
        next_output,
        next_gateup,
        next_down,
        new_norm_gains,
        next_gain_moms,
        new_qk_gains,
        next_qk_moms,
    )


def solution(mesh):
    return jax.shard_map(
        local,
        mesh=mesh,
        in_specs=(
            P("dp", None),
            P("dp", None),
            P("dp"),
            P("dp", "tensor"),
            P(None, "dp", "tensor"),
            P("tensor", "dp"),
            P(None, "dp", "tensor"),
            P("tensor", "dp"),
            P(None, "dp"),
            P(None, ("dp", "tensor")),
            P("dp", "tensor"),
            P(None, "dp", "tensor"),
            P("tensor", "dp"),
            P(None, "dp", "tensor"),
            P("tensor", "dp"),
            P(None, "dp"),
            P(None, ("dp", "tensor")),
        ),
        out_specs=(
            P("dp", None),
            P("dp", None),
            P("dp", "tensor"),
            P(None, "dp", "tensor"),
            P("tensor", "dp"),
            P(None, "dp", "tensor"),
            P("tensor", "dp"),
            P("dp", "tensor"),
            P(None, "dp", "tensor"),
            P("tensor", "dp"),
            P(None, "dp", "tensor"),
            P("tensor", "dp"),
            P(None, "dp"),
            P(None, "dp"),
            P(None, ("dp", "tensor")),
            P(None, ("dp", "tensor")),
        ),
        check_vma=False,
    )
```

```python
import functools
import math

import jax
import jax.numpy as jnp
import numpy as np
from jax import lax
from jax.experimental import pallas as pl
from jax.experimental.pallas import tpu as pltpu
from jax.sharding import PartitionSpec as P

WINDOW = 512
EPSILON = 1e-06
COEF_ONE = 3.4445
COEF_TWO = -4.775
COEF_THREE = 2.0315

D = 1152
HD = 256
TOK = 256
QTOK = 64
ROWS = 36
FFT = 1728
FFP = 1792
HALF = 896
BLK = 224
PART = 192
BF = jnp.bfloat16
F32 = jnp.float32
MESH = pl.DeviceIdType.MESH

SIZES = {"z": 4, "x": 4, "c": 2, "y": 4}


def place():
    dp = lax.axis_index("dp")
    return {"z": dp // 8, "x": (dp // 2) % 4, "c": dp % 2, "y": lax.axis_index("tensor")}


def rank(at, axes):
    r = 0
    for a in axes:
        r = r * SIZES[a] + at[a]
    return r


def count(axes):
    return math.prod(SIZES[a] for a in axes)


def decode(p, axes):
    out = {}
    for a in reversed(axes):
        out[a] = p % SIZES[a]
        p = p // SIZES[a]
    return out


def moved(at, off, sign):
    return {a: (at[a] + (off[a] if sign > 0 else SIZES[a] - off[a])) % SIZES[a] if a in off else at[a] for a in at}


def device(at):
    return {"dp": at["z"] * 8 + at["x"] * 2 + at["c"], "tensor": at["y"]}


def slot(ref, mode, axes, target):
    if mode == "ag":
        return ref
    if mode == "a2a":
        return ref.at[rank(target, axes)]
    return ref.at[rank(target, mode[1])]


def exchange_body(axes, modes, subs, *refs):
    k = len(modes)
    n = count(axes)
    ins, outs = refs[:k], refs[k : 2 * k]
    send_sem, recv_sem, local_sem = refs[2 * k :]
    me = place()
    barrier = pltpu.get_barrier_semaphore()

    def greet(p, carry):
        pl.semaphore_signal(barrier, inc=1, device_id=device(moved(me, decode(p, axes), -1)), device_id_type=MESH)
        return carry

    def copies(p, arriving, items):
        off = decode(p, axes)
        target = moved(me, off, 1)
        place_of = moved(me, off, -1) if arriving else me
        return [
            pltpu.make_async_remote_copy(
                src_ref=slot(ins[i], modes[i], axes, target),
                dst_ref=outs[i].at[rank(place_of, subs[i])],
                send_sem=send_sem.at[i, p],
                recv_sem=recv_sem.at[i, p],
                device_id=device(target),
                device_id_type=MESH,
            )
            for i in items
        ]

    own = [
        pltpu.make_async_copy(slot(ins[i], modes[i], axes, me), outs[i].at[rank(me, subs[i])], local_sem.at[i])
        for i in range(k)
    ]
    lax.fori_loop(1, n, greet, 0)
    for copy in own:
        copy.start()
    pl.semaphore_wait(barrier, n - 1)
    if all(s == axes for s in subs):

        def launch(p, carry):
            for copy in copies(p, False, range(k)):
                copy.start()
            return carry

        def finish(p, carry):
            for copy in copies(p, True, range(k)):
                copy.wait()
            return carry

        lax.fori_loop(1, n, launch, 0)
        for copy in own:
            copy.wait()
        lax.fori_loop(1, n, finish, 0)
        return
    items = []
    for p in range(1, n):
        off = decode(p, axes)
        items.append((p, [i for i in range(k) if all(off[ax] == 0 for ax in axes if ax not in subs[i])]))
    for p, mine in items:
        for copy in copies(p, False, mine):
            copy.start()
    for copy in own:
        copy.wait()
    for p, mine in items:
        for copy in copies(p, True, mine):
            copy.wait()


def exchange(items, axes, cid):
    arrays = [i[0] for i in items]
    modes = [i[1] for i in items]
    subs = [i[2] if len(i) > 2 else axes for i in items]
    shapes = [
        (count(sub),) + (a.shape if m == "ag" else a.shape[1:]) for a, m, sub in zip(arrays, modes, subs)
    ]
    k, n = len(items), count(axes)
    vmem = pl.BlockSpec(memory_space=pltpu.VMEM)
    return pl.pallas_call(
        functools.partial(exchange_body, axes, modes, subs),
        out_shape=[jax.ShapeDtypeStruct(s, a.dtype) for s, a in zip(shapes, arrays)],
        in_specs=[vmem] * k,
        out_specs=[vmem] * k,
        scratch_shapes=[
            pltpu.SemaphoreType.DMA((k, n)),
            pltpu.SemaphoreType.DMA((k, n)),
            pltpu.SemaphoreType.DMA((k,)),
        ],
        compiler_params=pltpu.CompilerParams(
            collective_id=cid, has_side_effects=True, vmem_limit_bytes=32 * 1024 * 1024
        ),
    )(*arrays)


def virtual(me, p, q):
    c = me["c"]
    first = {"a": jnp.where(c == 0, me[p], me[q]), "b": jnp.where(c == 0, me[q], me[p])}

    def to(av, bv):
        return {**me, p: jnp.where(c == 0, av, bv), q: jnp.where(c == 0, bv, av)}

    return first["a"], first["b"], to


def remote(src, dst, send_sem, recv_sem, at):
    return pltpu.make_async_remote_copy(
        src_ref=src, dst_ref=dst, send_sem=send_sem, recv_sem=recv_sem, device_id=device(at), device_id_type=MESH
    )


def greet_all(places):
    barrier = pltpu.get_barrier_semaphore()
    for at in places:
        pl.semaphore_signal(barrier, inc=1, device_id=device(at), device_id_type=MESH)
    return barrier


def gather_body(block, out, send_sem, recv_sem, local_sem):
    me = place()
    a, b, to = virtual(me, "z", "x")
    twin = {**me, "c": 1 - me["c"]}
    a_next, a_last, a_far = (a + 1) % 4, (a + 3) % 4, (a + 2) % 4
    b_next, b_last = (b + 1) % 4, (b + 3) % 4
    barrier = greet_all([to(a_next, b), to(a_last, b), to(a, b_next), to(a, b_last)] + [twin])

    def spot(av, bv):
        at = to(av, bv)
        return out.at[me["c"], at["z"], at["x"]]

    here = spot(a, b)
    own = pltpu.make_async_copy(block, here, local_sem.at[0])
    own.start()
    pl.semaphore_wait(barrier, 5)

    def sent(src, dst_here, sem, at):
        remote(src, src, send_sem.at[sem], recv_sem.at[sem], at).start()
        return remote(src, dst_here, send_sem.at[sem], recv_sem.at[sem], at)

    own.wait()
    up, down = to(a_next, b), to(a_last, b)
    first = [sent(here, spot(a_last, b), 1, up), sent(here, spot(a_next, b), 2, down)]
    for w in first:
        w.wait()
    left, right, far = spot(a_last, b), spot(a_next, b), spot(a_far, b)
    for w in [sent(left.at[0], far.at[0], 3, up), sent(right.at[1], far.at[1], 4, down)]:
        w.wait()
    up2, down2 = to(a, b_next), to(a, b_last)
    waits = [
        (sent(spot(i, b), spot(i, b_last), 5 + 2 * i, up2), sent(spot(i, b), spot(i, b_next), 6 + 2 * i, down2))
        for i in range(4)
    ]
    late = []
    for i in range(4):
        w_last, w_next = waits[i]
        far = spot(i, (b + 2) % 4)
        if i < 2:
            w_last.wait()
            late += [sent(spot(i, b_last), far, 13 + i, up2), w_next]
        else:
            w_next.wait()
            late += [sent(spot(i, b_next), far, 13 + i, down2), w_last]
    for w in late:
        w.wait()
    remote(out.at[me["c"]], out.at[me["c"]], send_sem.at[0], recv_sem.at[0], twin).start()
    remote(out.at[me["c"]], out.at[1 - me["c"]], send_sem.at[0], recv_sem.at[0], twin).wait()


def gather_plane(block, cid):
    vmem = pl.BlockSpec(memory_space=pltpu.VMEM)
    return pl.pallas_call(
        gather_body,
        out_shape=jax.ShapeDtypeStruct((2, 4, 4) + block.shape, block.dtype),
        in_specs=[vmem],
        out_specs=vmem,
        scratch_shapes=[
            pltpu.SemaphoreType.DMA((17,)),
            pltpu.SemaphoreType.DMA((17,)),
            pltpu.SemaphoreType.DMA((1,)),
        ],
        compiler_params=pltpu.CompilerParams(
            collective_id=cid, has_side_effects=True, vmem_limit_bytes=32 * 1024 * 1024
        ),
    )(block)


class SideNear:
    sems = 7

    def shape(self, ffn):
        return jax.ShapeDtypeStruct((4, 2) + ffn.shape[1:], ffn.dtype)

    def places(self, me):
        a, b, to = virtual(me, "z", "x")
        return [to((a + 1) % 4, b), to((a + 3) % 4, b), {**me, "c": 1 - me["c"]}]

    def start(self, me, ffn, near, send_sem, recv_sem):
        a, b, to = virtual(me, "z", "x")
        c = me["c"]
        twin = {**me, "c": 1 - c}
        a_next, a_last, a_far = (a + 1) % 4, (a + 3) % 4, (a + 2) % 4
        up, down = to(a_next, b), to(a_last, b)

        def sent(src, dst_here, sem, at):
            remote(src, src, send_sem.at[sem], recv_sem.at[sem], at).start()
            return remote(src, dst_here, send_sem.at[sem], recv_sem.at[sem], at)

        keep = pltpu.make_async_copy(ffn.at[c], near.at[a, c], recv_sem.at[1])
        keep.start()
        remote(ffn.at[1 - c], near.at[b, c], send_sem.at[0], recv_sem.at[0], twin).start()
        keep.wait()
        remote(ffn.at[1 - c], near.at[a, 1 - c], send_sem.at[0], recv_sem.at[0], twin).wait()
        first = [sent(near.at[a], near.at[a_last], 2, up), sent(near.at[a], near.at[a_next], 3, down)]

        def middle():
            for w in first:
                w.wait()
            self.late = [
                sent(near.at[a_last, 0], near.at[a_far, 0], 4, up),
                sent(near.at[a_next, 1], near.at[a_far, 1], 5, down),
            ]

        self.middle = middle

    def finish(self):
        for w in self.late:
            w.wait()


class SideGather:
    sems = 16

    def shape(self, near):
        return jax.ShapeDtypeStruct((4, 4) + near.shape[1:], near.dtype)

    def places(self, me):
        a, b, to = virtual(me, "z", "x")
        return [to(a, (b + 1) % 4), to(a, (b + 3) % 4)]

    def start(self, me, near, out, send_sem, recv_sem):
        a, b, to = virtual(me, "z", "x")
        b_next, b_last = (b + 1) % 4, (b + 3) % 4
        up, down = to(a, b_next), to(a, b_last)

        def spot(av, bv):
            at = to(av, bv)
            return out.at[at["z"], at["x"]]

        def sent(src, dst, dst_here, sem, at):
            remote(src, dst, send_sem.at[sem], recv_sem.at[sem], at).start()
            return remote(src, dst_here, send_sem.at[sem], recv_sem.at[sem], at)

        self.waits = []
        for i in range(4):
            self.waits.append(
                (
                    sent(near.at[i], spot(i, b), spot(i, b_last), 2 * i, up),
                    sent(near.at[i], spot(i, b), spot(i, b_next), 2 * i + 1, down),
                )
            )
        self.late = []
        for i in range(4):
            copy = pltpu.make_async_copy(near.at[i], spot(i, b), recv_sem.at[12 + i])
            copy.start()
            self.late.append(copy)

        def middle():
            for i in range(4):
                w_last, w_next = self.waits[i]
                far = spot(i, (b + 2) % 4)
                if i < 2:
                    w_last.wait()
                    src = spot(i, b_last)
                    self.late += [sent(src, src, far, 8 + i, up), w_next]
                else:
                    w_next.wait()
                    src = spot(i, b_next)
                    self.late += [sent(src, src, far, 8 + i, down), w_last]

        self.middle = middle

    def finish(self):
        for w in self.late:
            w.wait()


class SideSwap:
    sems = 33
    axes = ("z", "x", "c")

    def shape(self, parts):
        return jax.ShapeDtypeStruct(parts.shape, parts.dtype)

    def places(self, me):
        return [moved(me, decode(p, self.axes), -1) for p in range(1, 32)]

    def start(self, me, parts, out, send_sem, recv_sem):
        def copies(p, arriving):
            off = decode(p, self.axes)
            target = moved(me, off, 1)
            spot = moved(me, off, -1) if arriving else me
            return remote(
                parts.at[rank(target, self.axes)],
                out.at[rank(spot, self.axes)],
                send_sem.at[p],
                recv_sem.at[p],
                target,
            )

        def launch(p, carry):
            copies(p, False).start()
            return carry

        def finish(p, carry):
            copies(p, True).wait()
            return carry

        lax.fori_loop(1, 32, launch, 0)
        mine = rank(me, self.axes)
        copy = pltpu.make_async_copy(parts.at[mine], out.at[mine], recv_sem.at[32])
        copy.start()
        copy.wait()
        self.finish = lambda: lax.fori_loop(1, 32, finish, 0)
        self.middle = lambda: None


def reduce_body(by0, by1, by2, by3, total, p, r1, r2, q, r3, r4, send_sem, recv_sem, local_sem):
    me = place()
    a, b, to = virtual(me, "z", "x")
    a_next, a_last, a_far = (a + 1) % 4, (a + 3) % 4, (a + 2) % 4
    b_next, b_last, b_far = (b + 1) % 4, (b + 3) % 4, (b + 2) % 4
    up, down = to(a_next, b), to(a_last, b)
    up2, down2 = to(a, b_next), to(a, b_last)
    barrier = greet_all([up, down, up2, down2])

    def at(ref, av, bv):
        w = to(av, bv)
        return ref.at[w["z"], w["x"]]

    loads = [pltpu.make_async_copy(by, p.at[i], local_sem.at[i]) for i, by in enumerate((by0, by1, by2, by3))]
    for load in loads:
        load.start()
    pl.semaphore_wait(barrier, 4)
    for load in loads:
        load.wait()
    first = []
    for i in range(4):
        first.append(remote(at(p, a_far, i), r1.at[i], send_sem.at[i], recv_sem.at[i], up if i < 2 else down))
        first[-1].start()
    second = []

    def onward(i, way, src):
        sem = 4 + 2 * i + way
        copy = remote(src, r2.at[way, i], send_sem.at[sem], recv_sem.at[sem], down if way else up)
        copy.start()
        second.append(copy)

    for i in range(4):
        onward(i, 1 if i < 2 else 0, at(p, a_last if i < 2 else a_next, i))
    for i in range(4):
        first[i].wait()
        dest = at(p, a_next if i < 2 else a_last, i)
        dest[...] = (dest[...].astype(F32) + r1[i].astype(F32)).astype(BF)
        onward(i, 0 if i < 2 else 1, dest)
    for copy in second:
        copy.wait()
    for i in range(4):
        q[i] = (at(p, a, i)[...].astype(F32) + r2[0, i].astype(F32) + r2[1, i].astype(F32)).astype(BF)
    lo, hi = pl.ds(0, BLK // 2), pl.ds(BLK // 2, BLK // 2)
    one = remote(q.at[b_far, lo], r3.at[0], send_sem.at[12], recv_sem.at[12], up2)
    two = remote(q.at[b_far, hi], r3.at[1], send_sem.at[13], recv_sem.at[13], down2)
    one.start()
    two.start()
    three = remote(q.at[b_next, hi], r4.at[0, hi], send_sem.at[14], recv_sem.at[14], up2)
    four = remote(q.at[b_last, lo], r4.at[1, lo], send_sem.at[15], recv_sem.at[15], down2)
    three.start()
    four.start()
    one.wait()
    dest = q.at[b_next, lo]
    dest[...] = (dest[...].astype(F32) + r3[0].astype(F32)).astype(BF)
    five = remote(q.at[b_next, lo], r4.at[0, lo], send_sem.at[16], recv_sem.at[16], up2)
    five.start()
    two.wait()
    dest = q.at[b_last, hi]
    dest[...] = (dest[...].astype(F32) + r3[1].astype(F32)).astype(BF)
    six = remote(q.at[b_last, hi], r4.at[1, hi], send_sem.at[17], recv_sem.at[17], down2)
    six.start()
    for copy in (three, four, five, six):
        copy.wait()
    total[...] = q[b].astype(F32) + r4[0].astype(F32) + r4[1].astype(F32)


def reduce_plane(parts, cid):
    block = parts[0].shape[1:]
    return pl.pallas_call(
        reduce_body,
        out_shape=jax.ShapeDtypeStruct(block, F32),
        in_specs=[pl.BlockSpec(memory_space=pl.ANY)] * 4,
        out_specs=pl.BlockSpec(memory_space=pltpu.VMEM),
        scratch_shapes=[
            pltpu.VMEM((4, 4) + block, BF),
            pltpu.VMEM((4,) + block, BF),
            pltpu.VMEM((2, 4) + block, BF),
            pltpu.VMEM((4,) + block, BF),
            pltpu.VMEM((2, BLK // 2, D), BF),
            pltpu.VMEM((2,) + block, BF),
            pltpu.SemaphoreType.DMA((18,)),
            pltpu.SemaphoreType.DMA((18,)),
            pltpu.SemaphoreType.DMA((4,)),
        ],
        compiler_params=pltpu.CompilerParams(
            collective_id=cid, has_side_effects=True, vmem_limit_bytes=48 * 1024 * 1024
        ),
    )(*parts)


def gram_body(kept, moms, grad, extra, gram, extras, mom, flat, parts, p, got, mine, bx, send_sem, recv_sem, local_sem):
    me = place()
    c, z = me["c"], me["z"]
    axes = ("x", "y")
    twin = {**me, "c": 1 - c}
    barrier = pltpu.get_barrier_semaphore()
    for i in range(1, 16):
        pl.semaphore_signal(barrier, inc=1, device_id=device(moved(me, decode(i, axes), -1)), device_id_type=MESH)
    for i in range(4):
        pl.semaphore_signal(barrier, inc=1, device_id=device({**twin, "y": (me["y"] + i) % 4}), device_id_type=MESH)
    new = 0.95 * moms[...].astype(F32) + grad[...]
    new = jnp.where(lax.broadcasted_iota(jnp.int32, (BLK, 1), 0) < kept[...], new, 0.0)
    mom[...] = new
    flat[...] = new.astype(BF)
    start = 0
    for j in range(D // 128):
        tall = 128 * (j + 1)
        value = dot(flat[:, pl.ds(0, tall)], flat[:, pl.ds(128 * j, 128)], TN).astype(BF)
        while tall:
            part, row = divmod(start, PART)
            size = min(tall, PART - row)
            done = 128 * (j + 1) - tall
            parts[part // 16, part % 16, pl.ds(row, size), :] = value[done : done + size]
            start, tall = start + size, tall - size
    for part in range(start // PART, 32):
        row = start % PART if part == start // PART else 0
        parts[part // 16, part % 16, pl.ds(row, PART - row), :] = jnp.zeros((PART - row, 128), BF)
    load = pltpu.make_async_copy(parts.at[c], p, local_sem.at[0])
    load.start()
    keep = pltpu.make_async_copy(extra, extras.at[rank(me, ("c", "y"))], local_sem.at[1])
    keep.start()
    pl.semaphore_wait(barrier, 19)
    swap = remote(parts.at[1 - c], got, send_sem.at[0, 0], recv_sem.at[0, 0], twin)
    swap.start()
    extra_waits = []
    for i in range(1, 8):
        off = decode(i, ("c", "y"))
        target, source = moved(me, off, 1), moved(me, off, -1)
        sems = (send_sem.at[3, i], recv_sem.at[3, i])
        remote(extra, extras.at[rank(me, ("c", "y"))], *sems, target).start()
        extra_waits.append(remote(extra, extras.at[rank(source, ("c", "y"))], *sems, target))
    load.wait()
    swap.wait()
    for i in range(16):
        p[i] = (p[i].astype(F32) + got[i].astype(F32)).astype(BF)
    waits = []
    for i in range(1, 16):
        off = decode(i, axes)
        target, source = moved(me, off, 1), moved(me, off, -1)
        sems = (send_sem.at[1, i], recv_sem.at[1, i])
        remote(p.at[rank(target, axes)], mine.at[rank(me, axes)], *sems, target).start()
        waits.append(remote(p.at[rank(target, axes)], mine.at[rank(source, axes)], *sems, target))
    own = pltpu.make_async_copy(p.at[rank(me, axes)], mine.at[rank(me, axes)], local_sem.at[0])
    own.start()
    own.wait()
    for w in waits:
        w.wait()
    sums = []
    for i in range(4):
        part = mine[4 * i].astype(F32)
        for j in range(1, 4):
            part = part + mine[4 * i + j].astype(F32)
        sums.append(part)
    whole = sums[0] + sums[1] + sums[2] + sums[3]
    for i in range(4):
        bx[i] = jnp.where(z < 3, whole, sums[i]).astype(BF)
    waits = []
    spot = gram.at[c]
    for i in range(1, 16):
        off = decode(i, axes)
        target, source = moved(me, off, 1), moved(me, off, -1)
        sems = (send_sem.at[2, i], recv_sem.at[2, i])
        remote(bx.at[target["x"]], spot.at[rank(me, axes)], *sems, target).start()
        waits.append(remote(bx.at[target["x"]], spot.at[rank(source, axes)], *sems, target))
    own = pltpu.make_async_copy(bx.at[me["x"]], spot.at[rank(me, axes)], local_sem.at[0])
    own.start()
    own.wait()
    for w in waits:
        w.wait()
    remote(gram.at[c], gram.at[c], send_sem.at[2, 0], recv_sem.at[2, 0], twin).start()
    remote(gram.at[c], gram.at[1 - c], send_sem.at[2, 0], recv_sem.at[2, 0], twin).wait()
    keep.wait()
    for w in extra_waits:
        w.wait()


def gram_sum(kept, moms, grad, extra, cid):
    vmem = pl.BlockSpec(memory_space=pltpu.VMEM)
    half = (16, PART, 128)
    return pl.pallas_call(
        gram_body,
        out_shape=[
            jax.ShapeDtypeStruct((2,) + half, BF),
            jax.ShapeDtypeStruct((8,) + extra.shape, extra.dtype),
            jax.ShapeDtypeStruct(grad.shape, F32),
        ],
        in_specs=[vmem] * 4,
        out_specs=[vmem] * 3,
        scratch_shapes=[
            pltpu.VMEM(moms.shape, BF),
            pltpu.VMEM((2,) + half, BF),
            pltpu.VMEM(half, BF),
            pltpu.VMEM(half, BF),
            pltpu.VMEM(half, BF),
            pltpu.VMEM((4,) + half[1:], BF),
            pltpu.SemaphoreType.DMA((4, 16)),
            pltpu.SemaphoreType.DMA((4, 16)),
            pltpu.SemaphoreType.DMA((2,)),
        ],
        compiler_params=pltpu.CompilerParams(
            collective_id=cid, has_side_effects=True, vmem_limit_bytes=48 * 1024 * 1024
        ),
    )(kept, moms, grad, extra)


def halo_body(sign, kinds, side, *refs):
    k = len(kinds)
    side_in, ins, outs, side_out = refs[0], refs[1 : 1 + k], refs[1 + k : 1 + 2 * k], refs[1 + 2 * k]
    send_sem, recv_sem, local_sem, side_send, side_recv = refs[2 + 2 * k :]
    me = place()
    dp = lax.axis_index("dp")
    y = lax.axis_index("tensor")
    barrier = pltpu.get_barrier_semaphore()
    offs = [(d, t) for d in range(3) for t in range(4)]

    def dev(d, t, way):
        shift = d if way > 0 else 32 - d
        return {"dp": (dp + shift) % 32, "tensor": (y + (t if way > 0 else 4 - t)) % 4}

    for d, t in offs[1:]:
        back = dev(d, t, -1) if sign > 0 else {"dp": (dp + d) % 32, "tensor": (y + 4 - t) % 4}
        pl.semaphore_signal(barrier, inc=1, device_id=back, device_id_type=MESH)
    more = side.places(me)
    greet_all(more)
    own = []
    copies = []
    for i, kind in enumerate(kinds):
        for p, (d, t) in enumerate(offs):
            if kind == "near" and d > 0:
                continue
            ty = (y + t) % 4
            sy = (y + 4 - t) % 4
            src = ins[i].at[pl.ds(pl.multiple_of((2 - d) * TOK + ty * QTOK, QTOK), QTOK)] if kind == "split" else ins[i]
            tdp = (dp + d) % 32 if sign > 0 else (dp + 32 - d) % 32
            if kind == "near":
                to, frm = outs[i].at[y], outs[i].at[sy]
            elif kind == "all":
                rows = pl.ds((2 - d) * TOK, TOK)
                to, frm = (outs[i].at[rows, pl.ds(pl.multiple_of(at * 128, 128), 128)] for at in (y, sy))
            else:
                to, frm = outs[i].at[d, y], outs[i].at[d, sy]
            if p == 0:
                own.append(pltpu.make_async_copy(src, to, local_sem.at[i]))
                continue
            args = dict(send_sem=send_sem.at[i, p], recv_sem=recv_sem.at[i, p], device_id={"dp": tdp, "tensor": ty}, device_id_type=MESH)
            copies.append(
                (
                    pltpu.make_async_remote_copy(src_ref=src, dst_ref=to, **args),
                    pltpu.make_async_remote_copy(src_ref=src, dst_ref=frm, **args),
                )
            )
    for copy in own:
        copy.start()
    pl.semaphore_wait(barrier, len(offs) - 1 + len(more))
    for out_copy, _ in copies:
        out_copy.start()
    side.start(me, side_in, side_out, side_send, side_recv)
    for copy in own:
        copy.wait()
    side.middle()
    for _, in_copy in copies:
        in_copy.wait()
    side.finish()


def halo(items, sign, cid, side, side_in):
    arrays = [a for a, _ in items]
    kinds = [m for _, m in items]
    shapes = []
    for a, m in items:
        shapes.append({"near": (4,) + a.shape, "all": (3 * TOK, 512), "split": (3, 4, QTOK, 512)}[m])
    k = len(items)
    return pl.pallas_call(
        functools.partial(halo_body, sign, kinds, side),
        out_shape=[jax.ShapeDtypeStruct(s, a.dtype) for s, a in zip(shapes, arrays)] + [side.shape(side_in)],
        in_specs=[pl.BlockSpec(memory_space=pl.ANY)] + [pl.BlockSpec(memory_space=pltpu.VMEM)] * k,
        out_specs=[pl.BlockSpec(memory_space=pltpu.VMEM)] * k + [pl.BlockSpec(memory_space=pl.ANY)],
        scratch_shapes=[
            pltpu.SemaphoreType.DMA((k, 12)),
            pltpu.SemaphoreType.DMA((k, 12)),
            pltpu.SemaphoreType.DMA((k,)),
            pltpu.SemaphoreType.DMA((side.sems,)),
            pltpu.SemaphoreType.DMA((side.sems,)),
        ],
        compiler_params=pltpu.CompilerParams(collective_id=cid, has_side_effects=True),
    )(side_in, *arrays)


def sum_body(fn, both, spread, side, n_extra, n_local, n_ag, *refs):
    if side is not None:
        side_in, side_out, side_send, side_recv = refs[0], refs[1 + 1 + n_extra + n_local + n_ag], refs[-2], refs[-1]
        refs = refs[1 : 2 + n_extra + n_local + n_ag] + refs[3 + n_extra + n_local + n_ag : -2]
    parts = refs[0]
    extras = refs[1 : 1 + n_extra]
    locals_ = refs[1 + n_extra : 1 + n_extra + n_local]
    gathers = refs[1 + n_extra + n_local : 1 + n_extra + n_local + n_ag]
    pre, recv, agbuf, send_sem, recv_sem, local_sem = refs[1 + n_extra + n_local + n_ag :]
    me = place()
    c, y = me["c"], me["y"]
    twin = {**me, "c": 1 - c}
    near = [(moved(me, {"y": i}, 1), moved(me, {"y": i}, -1)) for i in range(1, 4)]
    use_twin = both or spread
    places = [source for _, source in near] + ([twin] if use_twin else [])
    if side is not None:
        places += side.places(me)
    barrier = greet_all(places)
    pl.semaphore_wait(barrier, len(places))
    if both:
        swap = remote(parts.at[1 - c], pre, send_sem.at[0], recv_sem.at[0], twin)
        swap.start()
        if side is not None:
            side.start(me, side_in, side_out, side_send, side_recv)
        swap.wait()
        for i in range(4):
            pre[i] = (pre[i].astype(F32) + parts[c, i].astype(F32)).astype(BF)
        mine = pre
    else:
        mine = parts
    waits = []
    for i, (target, source) in enumerate(near):
        sems = (send_sem.at[1 + i], recv_sem.at[1 + i])
        remote(mine.at[target["y"]], recv.at[i], *sems, target).start()
        waits.append(remote(mine.at[target["y"]], recv.at[i], *sems, target))
    if side is not None and not both:
        side.start(me, side_in, side_out, side_send, side_recv)
    total = mine[y].astype(F32)
    for i in range(3):
        waits[i].wait()
        total = total + recv[i].astype(F32)
    local_vals, ag_vals = fn(total, *[e[...] for e in extras])
    for i, value in enumerate(ag_vals):
        agbuf[i] = value.astype(BF)
    waits, own = [], []
    for j in range(n_ag):
        out = gathers[j].at[c] if spread else gathers[j]
        for i, (target, source) in enumerate(near):
            sems = (send_sem.at[4 + 3 * j + i], recv_sem.at[4 + 3 * j + i])
            remote(agbuf.at[j], out.at[y], *sems, target).start()
            waits.append(remote(agbuf.at[j], out.at[source["y"]], *sems, target))
        own.append(pltpu.make_async_copy(agbuf.at[j], out.at[y], local_sem.at[j]))
        own[-1].start()
    for ref, value in zip(locals_, local_vals):
        ref[...] = value
    if side is not None:
        side.middle()
    for copy in own + waits:
        copy.wait()
    if spread:
        for j in range(n_ag):
            g = gathers[j]
            sems = (send_sem.at[4 + 3 * n_ag + j], recv_sem.at[4 + 3 * n_ag + j])
            remote(g.at[c], g.at[c], *sems, twin).start()
            remote(g.at[c], g.at[1 - c], *sems, twin).wait()
    if side is not None:
        side.finish()


def sum_then_gather(fn, parts, extras, local_shapes, n_ag, spread, cid, side=None, side_in=None):
    both = parts.ndim == 4
    rows = parts.shape[-2:]
    vmem = pl.BlockSpec(memory_space=pltpu.VMEM)
    gathered = ((2, 4) if spread else (4,)) + rows
    n_sem = 4 + 4 * n_ag
    hbm = pl.BlockSpec(memory_space=pl.ANY)
    more = side is not None
    return pl.pallas_call(
        functools.partial(sum_body, fn, both, spread, side, len(extras), len(local_shapes), n_ag),
        out_shape=[jax.ShapeDtypeStruct(s, F32) for s in local_shapes]
        + [jax.ShapeDtypeStruct(gathered, BF)] * n_ag
        + ([side.shape(side_in)] if more else []),
        in_specs=[hbm] * more + [vmem] * (1 + len(extras)),
        out_specs=[vmem] * (len(local_shapes) + n_ag) + [hbm] * more,
        scratch_shapes=[
            pltpu.VMEM((4,) + rows, BF),
            pltpu.VMEM((3,) + rows, BF),
            pltpu.VMEM((n_ag,) + rows, BF),
            pltpu.SemaphoreType.DMA((n_sem,)),
            pltpu.SemaphoreType.DMA((n_sem,)),
            pltpu.SemaphoreType.DMA((n_ag,)),
        ]
        + ([pltpu.SemaphoreType.DMA((side.sems,))] * 2 if more else []),
        compiler_params=pltpu.CompilerParams(
            collective_id=cid, has_side_effects=True, vmem_limit_bytes=32 * 1024 * 1024
        ),
    )(*([side_in] if more else []), parts, *extras)


def inv_rms(values):
    return lax.rsqrt(jnp.mean(values * values, axis=-1, keepdims=True) + EPSILON)


def rms_back(values, gain, s, grad):
    scaled = gain * grad
    dv = s * scaled - values * (s * s * s * jnp.mean(scaled * values, axis=-1, keepdims=True))
    return dv, jnp.sum(grad * values * s, axis=0, keepdims=True)


def rot(values, cosine, sine):
    front, back = values[:, :128], values[:, 128:]
    return jnp.concatenate([front * cosine - back * sine, back * cosine + front * sine], axis=-1)


def unrot(values, cosine, sine):
    return rot(values, cosine, -sine)


def mid_fn(u, hidden, g1, g2):
    hmid = hidden + u * inv_rms(u) * g1
    return [u, hmid], [hmid * inv_rms(hmid) * g2]


def ffn_out_fn(f, hmid, out_grad, g3):
    s = inv_rms(f)
    block = hmid + f * s * g3
    df, dg3 = rms_back(f, g3, s, out_grad)
    return [block, dg3], [df]


def ffn_in_fn(dbin, hmid, u, out_grad, g1, g2):
    dm, dg2 = rms_back(hmid, g2, inv_rms(hmid), dbin)
    dhmid = out_grad + dm
    du, dg1 = rms_back(u, g1, inv_rms(u), dhmid)
    return [dhmid, dg1, dg2], [du]


def last_fn(da, hidden, dhmid, block, g0):
    dh, dg0 = rms_back(hidden, g0, inv_rms(hidden), da)
    return [dg0], [dhmid + dh, block]


def dot(a, b, dims):
    return lax.dot_general(a, b, (dims, ((), ())), preferred_element_type=F32)


NN = ((1,), (0,))
NT = ((1,), (1,))
TN = ((0,), (0,))


def ffn_body(blocks, tokens, dense, gate, up, mixed, f):
    for k in range(32):
        for m in range(3):
            dense[m, pl.ds(ROWS * k, ROWS), :] = blocks[k, pl.ds(ROWS * m, ROWS), :]
    inner = math.sqrt(2.0 / math.pi)

    def body(i, carry):
        rows = pl.ds(pl.multiple_of(i * TOK, TOK), TOK)
        low = tokens[rows, :]
        g = dot(low, dense[0], NN)
        gate[rows, :] = g
        u = dot(low, dense[1], NN)
        up[rows, :] = u
        th = jnp.tanh(inner * (g + 0.044715 * g * g * g))
        z = (0.5 * g * (1.0 + th) * u).astype(BF)
        mixed[rows, :] = z
        f[rows, :] = dot(z, dense[2], NT).astype(BF)
        return carry

    lax.fori_loop(0, 2, body, 0)


def ffn_forward(blocks, tokens):
    vmem = pl.BlockSpec(memory_space=pltpu.VMEM)
    return pl.pallas_call(
        ffn_body,
        out_shape=[
            jax.ShapeDtypeStruct((3, D, HALF), BF),
            jax.ShapeDtypeStruct((512, HALF), F32),
            jax.ShapeDtypeStruct((512, HALF), F32),
            jax.ShapeDtypeStruct((512, HALF), BF),
            jax.ShapeDtypeStruct((512, D), BF),
        ],
        in_specs=[vmem] * 2,
        out_specs=[vmem] * 5,
        compiler_params=pltpu.CompilerParams(vmem_limit_bytes=48 * 1024 * 1024),
    )(blocks, tokens)


def project_body(got, hidden, w_qkv, woT, gains, normed, q, kv, tail):
    for k in range(32):
        z, x, c = k // 8, k // 2 % 4, k % 2
        here, rows = pl.ds(ROWS * k, ROWS), pl.ds(0, ROWS)
        w_qkv[here, :] = got[c, z, x, 0, rows, :]
        woT[here, :] = got[c, z, x, 1, rows, pl.ds(0, HD)]
        tail[here, :] = got[c, z, x, 1, rows, pl.ds(HD, 128)]
    turned = tail[...].astype(F32).T
    gains[...] = turned[:8]
    h = hidden[...]
    low = (h * inv_rms(h) * turned[0:1]).astype(BF)
    normed[...] = low
    out = dot(low, w_qkv[...], NN)
    q[...] = out[:, :HD]
    kv[...] = out[:, HD:].astype(BF)


def project(got, hidden):
    vmem = pl.BlockSpec(memory_space=pltpu.VMEM)
    shapes = [((D, 384), BF), ((D, HD), BF), ((8, D), F32), ((TOK, D), BF), ((TOK, HD), F32), ((TOK, 128), BF)]
    return pl.pallas_call(
        project_body,
        out_shape=[jax.ShapeDtypeStruct(s, t) for s, t in shapes],
        in_specs=[vmem] * 2,
        out_specs=[vmem] * len(shapes),
        scratch_shapes=[pltpu.VMEM((D, 128), BF)],
        compiler_params=pltpu.CompilerParams(vmem_limit_bytes=32 * 1024 * 1024),
    )(got, hidden)


def attention_body(kv, sort, q_raw, gq, gk, cosine, sine, seg_q, seg_k, woT, qr, kr, vb, k_own, probs, ob, u):
    sorted_kv = dot(kv[...], sort[...], NN)
    k_raw = sorted_kv[:, :HD]
    v = sorted_kv[:, HD:].astype(BF)
    vb[...] = v
    k_own[...] = k_raw[2 * TOK :]
    k = rot(k_raw * inv_rms(k_raw) * gk[...], cosine[...], sine[...]).astype(BF)
    kr[...] = k
    raw = q_raw[...]
    q = rot(raw * inv_rms(raw) * gq[...], cosine[pl.ds(2 * TOK, TOK), :], sine[pl.ds(2 * TOK, TOK), :]).astype(BF)
    qr[...] = q
    shape = (TOK, 3 * TOK)
    gap = lax.broadcasted_iota(jnp.int32, shape, 0) + 2 * TOK - lax.broadcasted_iota(jnp.int32, shape, 1)
    allowed = (seg_q[...] == seg_k[...]) & (gap >= 0) & (gap < WINDOW)
    scores = jnp.where(allowed, dot(q, k, NT) * (HD**-0.5), -1e30)
    exps = jnp.exp(scores - jnp.max(scores, axis=-1, keepdims=True))
    p = exps / jnp.sum(exps, axis=-1, keepdims=True)
    probs[...] = p
    o = dot(p.astype(BF), v, NN).astype(BF)
    ob[...] = o
    u[...] = dot(o, woT[...], NT).astype(BF)


def attention(*args):
    vmem = pl.BlockSpec(memory_space=pltpu.VMEM)
    wide = 3 * TOK
    shapes = [
        ((TOK, HD), BF),
        ((wide, HD), BF),
        ((wide, HD), BF),
        ((TOK, HD), F32),
        ((TOK, wide), F32),
        ((TOK, HD), BF),
        ((TOK, D), BF),
    ]
    return pl.pallas_call(
        attention_body,
        out_shape=[jax.ShapeDtypeStruct(s, t) for s, t in shapes],
        in_specs=[vmem] * len(args),
        out_specs=[vmem] * len(shapes),
        compiler_params=pltpu.CompilerParams(vmem_limit_bytes=32 * 1024 * 1024),
    )(*args)


def attention_back_body(*refs):
    du_all, woT, vb, probs, kr, qr, q_raw, gq, gk, cosine, sine, k_own, normed, ob = refs[:14]
    dkv_all, a_all, ob_all, dq_all, dgq, dgk = refs[14:20]
    part, got, dkvb, send_sem, recv_sem, local_sem = refs[20:]
    me = place()
    c, y, dp = me["c"], me["y"], lax.axis_index("dp")
    twin = {**me, "c": 1 - c}

    def along(d, t):
        at = (dp + d + 32) % 32
        return {"z": at // 8, "x": (at // 2) % 4, "c": at % 2, "y": (y + t + 4) % 4}

    offs = [(d, t) for d in range(3) for t in range(4)][1:]
    group = [decode(p, ("c", "y")) for p in range(1, 8)]
    places = [along(d, -t) for d, t in offs] + [moved(me, off, -1) for off in group]
    barrier = greet_all(places)
    pl.semaphore_wait(barrier, len(places))
    waits = []

    def to_twin(src, out, sem):
        remote(src, out.at[c], send_sem.at[sem], recv_sem.at[sem], twin).start()
        waits.append(remote(src, out.at[1 - c], send_sem.at[sem], recv_sem.at[sem], twin))
        own = pltpu.make_async_copy(src, out.at[c], local_sem.at[sem])
        own.start()
        waits.append(own)

    to_twin(normed, a_all, 0)
    to_twin(ob, ob_all, 1)
    scale = HD**-0.5
    dub = du_all[pl.ds(pl.multiple_of(c * TOK, TOK), TOK), :]
    dob = dot(dub, woT[...], NN).astype(BF)
    p = probs[...]
    dp_ = dot(dob, vb[...], NT)
    ds = (p * (dp_ - jnp.sum(p * dp_, axis=-1, keepdims=True))).astype(BF)
    part[:, pl.ds(0, HD)] = (dot(ds, qr[...], TN) * scale).astype(BF)
    part[:, pl.ds(HD, HD)] = dot(p.astype(BF), dob, TN).astype(BF)
    own = pltpu.make_async_copy(part.at[pl.ds(pl.multiple_of(2 * TOK + y * QTOK, QTOK), QTOK)], got.at[0, y], local_sem.at[2])
    own.start()
    halo_waits = []
    for i, (d, t) in enumerate(offs):
        target = along(-d, t)
        src = part.at[pl.ds(pl.multiple_of((2 - d) * TOK + target["y"] * QTOK, QTOK), QTOK)]
        sems = (send_sem.at[3 + i], recv_sem.at[3 + i])
        remote(src, got.at[d, y], *sems, target).start()
        halo_waits.append(remote(src, got.at[d, (y + 4 - t) % 4], *sems, target))
    raw = q_raw[...]
    dqr = dot(ds, kr[...], NN) * scale
    here = pl.ds(2 * TOK, TOK)
    dq, dg = rms_back(raw, gq[...], inv_rms(raw), unrot(dqr, cosine[here, :], sine[here, :]))
    dgq[...] = dg
    dq_all[c] = dq.astype(BF)
    remote(dq_all.at[c], dq_all.at[c], send_sem.at[2], recv_sem.at[2], twin).start()
    waits.append(remote(dq_all.at[c], dq_all.at[1 - c], send_sem.at[2], recv_sem.at[2], twin))
    own.wait()
    for w in halo_waits:
        w.wait()
    total = got[0, 0].astype(F32)
    for i in range(1, 12):
        total = total + got[i // 4, i % 4].astype(F32)
    k = k_own[pl.ds(pl.multiple_of(y * QTOK, QTOK), QTOK), :]
    rows = pl.ds(pl.multiple_of(2 * TOK + y * QTOK, QTOK), QTOK)
    dk, dg = rms_back(k, gk[...], inv_rms(k), unrot(total[:, :HD], cosine[rows, :], sine[rows, :]))
    dgk[...] = dg
    dkvb[:, pl.ds(0, HD)] = dk.astype(BF)
    dkvb[:, pl.ds(HD, HD)] = total[:, HD:].astype(BF)
    own = pltpu.make_async_copy(dkvb, dkv_all.at[c, y], local_sem.at[3])
    own.start()
    waits.append(own)
    for i, off in enumerate(group):
        target, source = moved(me, off, 1), moved(me, off, -1)
        sems = (send_sem.at[14 + i], recv_sem.at[14 + i])
        remote(dkvb, dkv_all.at[c, y], *sems, target).start()
        waits.append(remote(dkvb, dkv_all.at[source["c"], source["y"]], *sems, target))
    for w in waits:
        w.wait()


def attention_back(cid, *args):
    vmem = pl.BlockSpec(memory_space=pltpu.VMEM)
    shapes = [
        ((2, 4, QTOK, 512), BF),
        ((2, TOK, D), BF),
        ((2, TOK, HD), BF),
        ((2, TOK, HD), BF),
        ((1, HD), F32),
        ((1, HD), F32),
    ]
    return pl.pallas_call(
        attention_back_body,
        out_shape=[jax.ShapeDtypeStruct(s, t) for s, t in shapes],
        in_specs=[vmem] * len(args),
        out_specs=[vmem] * len(shapes),
        scratch_shapes=[
            pltpu.VMEM((3 * TOK, 512), BF),
            pltpu.VMEM((3, 4, QTOK, 512), BF),
            pltpu.VMEM((QTOK, 512), BF),
            pltpu.SemaphoreType.DMA((21,)),
            pltpu.SemaphoreType.DMA((21,)),
            pltpu.SemaphoreType.DMA((4,)),
        ],
        compiler_params=pltpu.CompilerParams(
            collective_id=cid, has_side_effects=True, vmem_limit_bytes=40 * 1024 * 1024
        ),
    )(*args)


def rope_tables():
    freqs = 10000.0 ** (-np.arange(128, dtype=np.float64) * 2.0 / 256)
    base = (np.arange(32, dtype=np.float64) - 2)[:, None] * 256 * freqs[None]
    step = np.arange(768, dtype=np.float64)[:, None] * freqs[None]
    return [t.astype(np.float32) for t in (np.cos(base), np.sin(base), np.cos(step), np.sin(step))]


def pack_body(gateup, downT, query, outputT, keyval, out, row):
    for m in range(3):
        row[:, pl.ds(0, FFT)] = gateup[m] if m < 2 else downT[...]
        row[:, pl.ds(FFT, FFP - FFT)] = jnp.zeros((ROWS, FFP - FFT), F32)
        for c in range(2):
            for x in range(4):
                out[8 * m + 2 * x + c] = row[:, pl.ds(HALF * c + BLK * x, BLK)].astype(BF)
    for x, half in enumerate((128, 128, 32, 32)):
        piece = (query[...], outputT[...], keyval[0], keyval[1])[x]
        row[:, pl.ds(0, 2 * half)] = piece
        for c in range(2):
            here = row[:, pl.ds(half * c, half)]
            out[24 + 2 * x + c, :, pl.ds(0, half)] = here.astype(BF)
            out[24 + 2 * x + c, :, pl.ds(half, BLK - half)] = jnp.zeros((ROWS, BLK - half), BF)


def to_columns(*args):
    vmem = pl.BlockSpec(memory_space=pltpu.VMEM)
    return pl.pallas_call(
        pack_body,
        out_shape=jax.ShapeDtypeStruct((32, ROWS, BLK), BF),
        in_specs=[vmem] * 5,
        out_specs=vmem,
        scratch_shapes=[pltpu.VMEM((ROWS, FFP), F32)],
        compiler_params=pltpu.CompilerParams(vmem_limit_bytes=32 * 1024 * 1024),
    )(*args)


def finish_body(*refs):
    o_got, w_got = refs[:2]
    weights, moms = refs[2:7], refs[7:12]
    new, nxt = refs[12:17], refs[17:22]
    row_o, row_w = refs[22:]

    def step(columns):
        return 0.15 * 0.2 * math.sqrt(max(D, columns))

    def update(i, m, width, columns):
        at = (m,) if m is not None else ()
        o, g = row_o[:, pl.ds(0, width)], row_w[:, pl.ds(0, width)]
        new[i][at + (slice(None), slice(None))] = weights[i][at + (slice(None), slice(None))] - step(columns) * o
        nxt[i][at + (slice(None), slice(None))] = 0.95 * moms[i][at + (slice(None), slice(None))] + g

    for m in range(3):
        for c in range(2):
            for x in range(4):
                here = pl.ds(HALF * c + BLK * x, BLK)
                row_o[:, here] = o_got[8 * m + 2 * x + c].astype(F32)
                row_w[:, here] = w_got[8 * m + 2 * x + c, :, pl.ds(0, BLK)].astype(F32)
        update(0 if m < 2 else 1, m if m < 2 else None, FFT, 6912)
    for x, half in enumerate((128, 128, 32, 32)):
        for c in range(2):
            here = pl.ds(half * c, half)
            row_o[:, here] = o_got[24 + 2 * x + c, :, pl.ds(0, half)].astype(F32)
            row_w[:, here] = w_got[24 + 2 * x + c, :, pl.ds(0, half)].astype(F32)
        update((2, 3, 4, 4)[x], (None, None, 0, 1)[x], 2 * half, 1024 if x < 2 else 256)


def finish(o_got, w_got, weights, moms):
    vmem = pl.BlockSpec(memory_space=pltpu.VMEM)
    out = pl.pallas_call(
        finish_body,
        out_shape=[jax.ShapeDtypeStruct(w.shape, F32) for w in weights] * 2,
        in_specs=[vmem] * 12,
        out_specs=[vmem] * 10,
        scratch_shapes=[pltpu.VMEM((ROWS, FFP), F32)] * 2,
        compiler_params=pltpu.CompilerParams(vmem_limit_bytes=32 * 1024 * 1024),
    )(o_got, w_got, *weights, *moms)
    return out[:5], out[5:]


def block_row(i, j):
    return 128 * (j * (j + 1) // 2 + i)


def chain_body(side, side_in, gram, mom, x, side_out, a, r, t, side_send, side_recv):
    me = place()
    places = side.places(me)
    barrier = greet_all(places)
    pl.semaphore_wait(barrier, len(places))
    side.start(me, side_in, side_out, side_send, side_recv)
    eye = lax.broadcasted_iota(jnp.int32, (128, 128), 0) == lax.broadcasted_iota(jnp.int32, (128, 128), 1)
    total = jnp.zeros((128, 128), F32)
    for i in range(D // 128):
        total = total + jnp.where(eye, gram[pl.ds(block_row(i, i), 128), :].astype(F32), 0.0)
    diag = jnp.sum(jnp.sum(total, axis=1, keepdims=True), axis=0, keepdims=True)
    inv = 1.0 / (jnp.sqrt(diag) + 1e-07)
    step = 384

    def by_rows(fn):
        def body(i, carry):
            fn(pl.ds(pl.multiple_of(i * step, step), step))
            return carry

        lax.fori_loop(0, D // step, body, 0)

    def poly(rows):
        low = a[rows, :]
        r[rows, :] = (COEF_TWO * low.astype(F32) + COEF_THREE * dot(low, a[...], NN)).astype(BF)

    def once(rows):
        low = a[rows, :]
        t[rows, :] = (COEF_ONE * low.astype(F32) + dot(low, r[...], NN)).astype(BF)

    def twice(rows):
        low = t[rows, :]
        a[rows, :] = (COEF_ONE * low.astype(F32) + dot(low, r[...], NN)).astype(BF)

    for j in range(D // 128):
        for i in range(j + 1):
            block = gram[pl.ds(block_row(i, j), 128), :].astype(F32) * (inv * inv)
            a[pl.ds(128 * i, 128), pl.ds(128 * j, 128)] = block.astype(BF)
            if i < j:
                a[pl.ds(128 * j, 128), pl.ds(128 * i, 128)] = block.T.astype(BF)
    x[...] = mom[...] * inv
    for i in range(3):
        by_rows(poly)
        x[...] = COEF_ONE * x[...] + dot(x[...].astype(BF), r[...], NN)
        if i < 2:
            by_rows(once)
            by_rows(twice)
    side.finish()


def orthogonal(gram, columns, side_in, cid):
    side = SideSwap()
    vmem = pl.BlockSpec(memory_space=pltpu.VMEM)
    hbm = pl.BlockSpec(memory_space=pl.ANY)
    return pl.pallas_call(
        functools.partial(chain_body, side),
        out_shape=[jax.ShapeDtypeStruct(columns.shape, F32), side.shape(side_in)],
        in_specs=[hbm, vmem, vmem],
        out_specs=[vmem, hbm],
        scratch_shapes=[pltpu.VMEM((D, D), BF)] * 3 + [pltpu.SemaphoreType.DMA((side.sems,))] * 2,
        compiler_params=pltpu.CompilerParams(
            collective_id=cid, has_side_effects=True, vmem_limit_bytes=48 * 1024 * 1024
        ),
    )(side_in, gram, columns)


def local(
    hidden_in,
    out_grad,
    segment_ids,
    w_query,
    w_keyval,
    w_output,
    w_gateup,
    w_down,
    norm_gains,
    qk_gains,
    mom_query,
    mom_keyval,
    mom_output,
    mom_gateup,
    mom_down,
    gain_moms,
    qk_moms,
):
    dp = lax.axis_index("dp")
    y = lax.axis_index("tensor")
    z, x, c = dp // 8, (dp // 2) % 4, dp % 2

    ffn_w = jnp.concatenate([w_gateup, w_down.T[None]], axis=0).astype(BF)
    ffn_w = jnp.pad(ffn_w, ((0, 0), (0, 0), (0, FFP - FFT))).reshape(3, ROWS, 2, HALF).transpose(2, 0, 1, 3)
    ffn_w = jnp.pad(ffn_w.reshape(2, 3 * ROWS, HALF), ((0, 0), (0, 4), (0, 0)))
    mom_downT, mom_outputT = mom_down.T, mom_output.T
    moms = to_columns(mom_gateup, mom_downT, mom_query, mom_outputT, mom_keyval)

    segs = jnp.pad(segment_ids.astype(F32).reshape(4, 64), ((0, ROWS - 4), (0, 0)))
    attn_w = jnp.stack(
        [
            jnp.concatenate([w_query, w_keyval[0], w_keyval[1]], axis=1),
            jnp.concatenate(
                [
                    w_output.T,
                    norm_gains.T,
                    jnp.broadcast_to(qk_gains.reshape(1, 4), (ROWS, 4)),
                    segs,
                    jnp.zeros((ROWS, 56), F32),
                ],
                axis=1,
            ),
        ]
    ).astype(BF)
    attn_w = jnp.pad(attn_w, ((0, 0), (0, 12), (0, 0)))
    attn_got = gather_plane(attn_w, 1)
    w_qkv, woT, gains, normed, q_raw, kv_piece = project(attn_got, hidden_in)
    g0, g1, g2, g3 = (gains[i : i + 1] for i in range(4))
    small = attn_got[:, :, :, 1, :4, 256:384].transpose(1, 2, 0, 3, 4).reshape(32, 4, 128)
    qk_mine = jnp.pad(small[:, 0, 4:8].reshape(32, 2, 2).transpose(1, 0, 2).reshape(2, 64), ((0, 14), (0, 64)))
    segs_all = small[:, :, 8:72].reshape(32, TOK).astype(jnp.int32)

    cos_b, sin_b, cos_s, sin_s = (jnp.asarray(t) for t in rope_tables())
    cb = lax.dynamic_slice_in_dim(cos_b, dp, 1, 0)
    sb = lax.dynamic_slice_in_dim(sin_b, dp, 1, 0)
    cosine = cb * cos_s - sb * sin_s
    sine = sb * cos_s + cb * sin_s

    kv_all, qk_all, ffn_near = halo([(kv_piece, "all"), (qk_mine, "near")], 1, 2, SideNear(), ffn_w)
    qk_full = qk_all[:, :2, :64].reshape(4, 2, 32, 2).transpose(1, 2, 0, 3).reshape(2, HD).astype(F32)
    gq, gk = qk_full[0:1], qk_full[1:2]
    order = np.arange(512)
    sort = np.zeros((512, 512), np.float32)
    sort[(order % 256) // 64 * 128 + order // 256 * 64 + order % 64, order] = 1.0
    first = jnp.maximum(dp - 2, 0)
    seg_rows = lax.dynamic_slice_in_dim(segs_all, first, 3, 0)
    seg_keys = jnp.where(
        dp >= 2, seg_rows, jnp.where(dp == 1, jnp.roll(seg_rows, 1, axis=0), jnp.roll(seg_rows, 2, axis=0))
    ).reshape(3 * TOK)
    seg_keys = jnp.where(jnp.arange(3 * TOK) >= (2 - dp) * TOK, seg_keys, -1)
    qr, kr, vb, k_own, probs, ob, u_part = attention(
        kv_all, jnp.asarray(sort, BF), q_raw, gq, gk, cosine, sine, segment_ids[:, None], seg_keys[None, :], woT
    )
    u_part = u_part.reshape(4, QTOK, D)
    hidden_q = lax.dynamic_slice_in_dim(hidden_in, y * QTOK, QTOK, 0)
    grad_q = lax.dynamic_slice_in_dim(out_grad, y * QTOK, QTOK, 0)
    u, hmid, bin_all, ffn_all = sum_then_gather(
        mid_fn, u_part, [hidden_q, g1, g2], [(QTOK, D)] * 2, 1, True, 3, SideGather(), ffn_near
    )

    bin_low = bin_all.reshape(512, D)
    dense, gate, up, mixed, f_part = ffn_forward(ffn_all.reshape(32, 112, HALF), bin_low)
    wg, wu, wdT = dense[0], dense[1], dense[2]
    inner = math.sqrt(2.0 / math.pi)
    th = jnp.tanh(inner * (gate + 0.044715 * gate * gate * gate))
    gelu = 0.5 * gate * (1.0 + th)
    gelu_d = 0.5 * (1.0 + th) + 0.5 * gate * (1.0 - th * th) * inner * (1.0 + 3 * 0.044715 * gate * gate)
    f_part = f_part.reshape(2, 4, QTOK, D)
    block, dg3, df_all, moms_all = sum_then_gather(
        ffn_out_fn, f_part, [hmid, grad_q, g3], [(QTOK, D), (1, D)], 1, True, 5, SideSwap(), moms
    )
    moms_cols = moms_all.reshape(D, BLK).T
    dfb = df_all.reshape(512, D)
    dz = dot(dfb, wdT, NN)
    dgate = (dz * up * gelu_d).astype(BF)
    dup = (dz * gelu).astype(BF)
    dbin_part = (dot(dgate, wg, NT) + dot(dup, wu, NT)).astype(BF).reshape(2, 4, QTOK, D)
    dhmid, dg1, dg2, du_all = sum_then_gather(
        ffn_in_fn,
        dbin_part,
        [hmid, u, grad_q, g1, g2],
        [(QTOK, D), (1, D), (1, D)],
        1,
        True,
        6,
    )

    dub_all = du_all.reshape(512, D)
    dkv_all, a_all, ob_all, dq_all, dgq, dgk = attention_back(
        7, dub_all, woT, vb, probs, kr, qr, q_raw, gq, gk, cosine, sine, k_own, normed, ob
    )
    dqb = lax.dynamic_slice_in_dim(dq_all, c, 1, 0)[0]
    dkv_all = dkv_all.reshape(512, 512)
    a_all, ob_all, dq_all = a_all.reshape(512, D), ob_all.reshape(512, HD), dq_all.reshape(512, HD)
    src, col = jnp.arange(512)[:, None], jnp.arange(128)[None, :]
    pick_y = (src == col // 64 * 256 + y * 64 + col % 64).astype(BF)
    col = col[:, :64]
    pick_c = (src == col // 32 * 256 + y * 64 + c * 32 + col % 32).astype(BF)
    dkv_mine = lax.dynamic_slice_in_dim(dkv_all, c * TOK, TOK, 0)
    dkv_y = dot(dkv_mine, pick_y, NN).astype(BF)
    dkv_cols = dot(dkv_all, pick_c, NN).astype(BF)
    da_part = (
        dot(
            jnp.concatenate([dqb, dkv_y], axis=1),
            w_qkv,
            NT,
        )
        .astype(BF)
        .reshape(4, QTOK, D)
    )
    dg0, last_in, last_out = sum_then_gather(
        last_fn, da_part, [hidden_q, dhmid, block, g0], [(1, D)], 2, False, 10
    )
    input_grad = last_in.reshape(TOK, D).astype(F32)
    block_out = last_out.reshape(TOK, D).astype(F32)

    gain_rows = jnp.concatenate(
        [dg0, dg1, dg2, dg3, jnp.concatenate([dgq, dgk, jnp.zeros((1, D - 2 * HD), F32)], axis=1)], axis=0
    ).astype(BF)

    ob_cols = lax.dynamic_slice_in_dim(ob_all, c * 128, 128, 1)
    dq_cols = lax.dynamic_slice_in_dim(dq_all, c * 128, 128, 1)
    d_gate = dot(dgate, bin_low, TN).astype(BF)
    d_up = dot(dup, bin_low, TN).astype(BF)
    d_down = dot(mixed, dfb, TN).astype(BF)
    d_q = dot(dq_cols, a_all, TN).astype(BF)
    d_kv = dot(dkv_cols, a_all, TN).astype(BF)
    d_o = dot(ob_cols, dub_all, TN).astype(BF)
    small = jnp.stack(
        [
            jnp.pad(d_q, ((0, BLK - 128), (0, 0))),
            jnp.pad(d_o, ((0, BLK - 128), (0, 0))),
            jnp.pad(d_kv[:32], ((0, BLK - 32), (0, 0))),
            jnp.concatenate([d_kv[32:], gain_rows, jnp.zeros((BLK - 37, D), BF)], axis=0),
        ]
    )
    wgrad = reduce_plane([d_gate.reshape(4, BLK, D), d_up.reshape(4, BLK, D), d_down.reshape(4, BLK, D), small], 11)

    kept = jnp.where((z == 3) & (x == 3), 32, BLK).reshape(1, 1)
    gram, gains_got, mom = gram_sum(kept, moms_cols, wgrad, wgrad[32:48].astype(BF), 13)
    gain_sum = jnp.sum(gains_got[:, :5].astype(F32), axis=0)
    gain_cols = jnp.concatenate(
        [
            gain_sum[:4].T.reshape(32, ROWS, 4),
            jnp.pad(
                gain_sum[4, : 2 * HD].reshape(2, 32, 4, 2)[:, :, y].transpose(1, 0, 2).reshape(32, 1, 4),
                ((0, 0), (0, ROWS - 1), (0, 0)),
            ),
        ],
        axis=2,
    )
    w_back = jnp.concatenate(
        [wgrad.astype(BF).T.reshape(32, ROWS, BLK), gain_cols.astype(BF), jnp.zeros((32, ROWS, 24), BF)], axis=2
    )
    ortho, w_got = orthogonal(gram.reshape(32 * PART, 128), mom, w_back, 12)
    gains_red = w_got[30, :, 224:228].T.astype(F32)
    qk_red = w_got[30, 0, 228:232].reshape(2, 2).astype(F32)
    o_back = ortho.astype(BF).T.reshape(32, ROWS, BLK)
    (o_got,) = exchange([(o_back, "a2a")], ("z", "x", "c"), 14)
    gain_rate = 2.0 / math.sqrt(8192)
    next_gain_moms = 0.9 * gain_moms + 0.1 * gains_red
    new_norm_gains = norm_gains - gain_rate * next_gain_moms
    next_qk_moms = 0.9 * qk_moms + 0.1 * qk_red
    new_qk_gains = qk_gains - gain_rate * next_qk_moms

    new, nxt = finish(
        o_got,
        w_got,
        [w_gateup, w_down.T, w_query, w_output.T, w_keyval],
        [mom_gateup, mom_downT, mom_query, mom_outputT, mom_keyval],
    )
    new_gateup, new_downT, new_query, new_outputT, new_keyval = new
    next_gateup, next_downT, next_query, next_outputT, next_keyval = nxt
    new_down, new_output, next_down, next_output = new_downT.T, new_outputT.T, next_downT.T, next_outputT.T
    return (
        block_out,
        input_grad,
        new_query,
        new_keyval,
        new_output,
        new_gateup,
        new_down,
        next_query,
        next_keyval,
        next_output,
        next_gateup,
        next_down,
        new_norm_gains,
        next_gain_moms,
        new_qk_gains,
        next_qk_moms,
    )


def solution(mesh):
    return jax.shard_map(
        local,
        mesh=mesh,
        in_specs=(
            P("dp", None),
            P("dp", None),
            P("dp"),
            P("dp", "tensor"),
            P(None, "dp", "tensor"),
            P("tensor", "dp"),
            P(None, "dp", "tensor"),
            P("tensor", "dp"),
            P(None, "dp"),
            P(None, ("dp", "tensor")),
            P("dp", "tensor"),
            P(None, "dp", "tensor"),
            P("tensor", "dp"),
            P(None, "dp", "tensor"),
            P("tensor", "dp"),
            P(None, "dp"),
            P(None, ("dp", "tensor")),
        ),
        out_specs=(
            P("dp", None),
            P("dp", None),
            P("dp", "tensor"),
            P(None, "dp", "tensor"),
            P("tensor", "dp"),
            P(None, "dp", "tensor"),
            P("tensor", "dp"),
            P("dp", "tensor"),
            P(None, "dp", "tensor"),
            P("tensor", "dp"),
            P(None, "dp", "tensor"),
            P("tensor", "dp"),
            P(None, "dp"),
            P(None, "dp"),
            P(None, ("dp", "tensor")),
            P(None, ("dp", "tensor")),
        ),
        check_vma=False,
    )
```

```python
import functools
import math

import jax
import jax.numpy as jnp
import numpy as np
from jax import lax
from jax.experimental import pallas as pl
from jax.experimental.pallas import tpu as pltpu
from jax.sharding import PartitionSpec as P

WINDOW = 512
EPSILON = 1e-06
COEF_ONE = 3.4445
COEF_TWO = -4.775
COEF_THREE = 2.0315

D = 1152
HD = 256
TOK = 256
QTOK = 64
ROWS = 36
FFT = 1728
FFP = 1792
HALF = 896
BLK = 224
PART = 192
BF = jnp.bfloat16
F32 = jnp.float32
MESH = pl.DeviceIdType.MESH

SIZES = {"z": 4, "x": 4, "c": 2, "y": 4}


def place():
    dp = lax.axis_index("dp")
    return {"z": dp // 8, "x": (dp // 2) % 4, "c": dp % 2, "y": lax.axis_index("tensor")}


def rank(at, axes):
    r = 0
    for a in axes:
        r = r * SIZES[a] + at[a]
    return r


def count(axes):
    return math.prod(SIZES[a] for a in axes)


def decode(p, axes):
    out = {}
    for a in reversed(axes):
        out[a] = p % SIZES[a]
        p = p // SIZES[a]
    return out


def moved(at, off, sign):
    return {a: (at[a] + (off[a] if sign > 0 else SIZES[a] - off[a])) % SIZES[a] if a in off else at[a] for a in at}


def device(at):
    return {"dp": at["z"] * 8 + at["x"] * 2 + at["c"], "tensor": at["y"]}


def slot(ref, mode, axes, target):
    if mode == "ag":
        return ref
    if mode == "a2a":
        return ref.at[rank(target, axes)]
    return ref.at[rank(target, mode[1])]


def exchange_body(axes, modes, subs, *refs):
    k = len(modes)
    n = count(axes)
    ins, outs = refs[:k], refs[k : 2 * k]
    send_sem, recv_sem, local_sem = refs[2 * k :]
    me = place()
    barrier = pltpu.get_barrier_semaphore()

    def greet(p, carry):
        pl.semaphore_signal(barrier, inc=1, device_id=device(moved(me, decode(p, axes), -1)), device_id_type=MESH)
        return carry

    def copies(p, arriving, items):
        off = decode(p, axes)
        target = moved(me, off, 1)
        place_of = moved(me, off, -1) if arriving else me
        return [
            pltpu.make_async_remote_copy(
                src_ref=slot(ins[i], modes[i], axes, target),
                dst_ref=outs[i].at[rank(place_of, subs[i])],
                send_sem=send_sem.at[i, p],
                recv_sem=recv_sem.at[i, p],
                device_id=device(target),
                device_id_type=MESH,
            )
            for i in items
        ]

    own = [
        pltpu.make_async_copy(slot(ins[i], modes[i], axes, me), outs[i].at[rank(me, subs[i])], local_sem.at[i])
        for i in range(k)
    ]
    lax.fori_loop(1, n, greet, 0)
    for copy in own:
        copy.start()
    pl.semaphore_wait(barrier, n - 1)
    if all(s == axes for s in subs):

        def launch(p, carry):
            for copy in copies(p, False, range(k)):
                copy.start()
            return carry

        def finish(p, carry):
            for copy in copies(p, True, range(k)):
                copy.wait()
            return carry

        lax.fori_loop(1, n, launch, 0)
        for copy in own:
            copy.wait()
        lax.fori_loop(1, n, finish, 0)
        return
    items = []
    for p in range(1, n):
        off = decode(p, axes)
        items.append((p, [i for i in range(k) if all(off[ax] == 0 for ax in axes if ax not in subs[i])]))
    for p, mine in items:
        for copy in copies(p, False, mine):
            copy.start()
    for copy in own:
        copy.wait()
    for p, mine in items:
        for copy in copies(p, True, mine):
            copy.wait()


def exchange(items, axes, cid):
    arrays = [i[0] for i in items]
    modes = [i[1] for i in items]
    subs = [i[2] if len(i) > 2 else axes for i in items]
    shapes = [
        (count(sub),) + (a.shape if m == "ag" else a.shape[1:]) for a, m, sub in zip(arrays, modes, subs)
    ]
    k, n = len(items), count(axes)
    vmem = pl.BlockSpec(memory_space=pltpu.VMEM)
    return pl.pallas_call(
        functools.partial(exchange_body, axes, modes, subs),
        out_shape=[jax.ShapeDtypeStruct(s, a.dtype) for s, a in zip(shapes, arrays)],
        in_specs=[vmem] * k,
        out_specs=[vmem] * k,
        scratch_shapes=[
            pltpu.SemaphoreType.DMA((k, n)),
            pltpu.SemaphoreType.DMA((k, n)),
            pltpu.SemaphoreType.DMA((k,)),
        ],
        compiler_params=pltpu.CompilerParams(
            collective_id=cid, has_side_effects=True, vmem_limit_bytes=32 * 1024 * 1024
        ),
    )(*arrays)


def virtual(me, p, q):
    c = me["c"]
    first = {"a": jnp.where(c == 0, me[p], me[q]), "b": jnp.where(c == 0, me[q], me[p])}

    def to(av, bv):
        return {**me, p: jnp.where(c == 0, av, bv), q: jnp.where(c == 0, bv, av)}

    return first["a"], first["b"], to


def remote(src, dst, send_sem, recv_sem, at):
    return pltpu.make_async_remote_copy(
        src_ref=src, dst_ref=dst, send_sem=send_sem, recv_sem=recv_sem, device_id=device(at), device_id_type=MESH
    )


def greet_all(places):
    barrier = pltpu.get_barrier_semaphore()
    for at in places:
        pl.semaphore_signal(barrier, inc=1, device_id=device(at), device_id_type=MESH)
    return barrier


def gather_body(block, out, send_sem, recv_sem, local_sem):
    me = place()
    a, b, to = virtual(me, "z", "x")
    twin = {**me, "c": 1 - me["c"]}
    a_next, a_last, a_far = (a + 1) % 4, (a + 3) % 4, (a + 2) % 4
    b_next, b_last = (b + 1) % 4, (b + 3) % 4
    barrier = greet_all([to(a_next, b), to(a_last, b), to(a, b_next), to(a, b_last)] + [twin])

    def spot(av, bv):
        at = to(av, bv)
        return out.at[me["c"], at["z"], at["x"]]

    here = spot(a, b)
    own = pltpu.make_async_copy(block, here, local_sem.at[0])
    own.start()
    pl.semaphore_wait(barrier, 5)

    def sent(src, dst_here, sem, at):
        remote(src, src, send_sem.at[sem], recv_sem.at[sem], at).start()
        return remote(src, dst_here, send_sem.at[sem], recv_sem.at[sem], at)

    own.wait()
    up, down = to(a_next, b), to(a_last, b)
    first = [sent(here, spot(a_last, b), 1, up), sent(here, spot(a_next, b), 2, down)]
    for w in first:
        w.wait()
    left, right, far = spot(a_last, b), spot(a_next, b), spot(a_far, b)
    for w in [sent(left.at[0], far.at[0], 3, up), sent(right.at[1], far.at[1], 4, down)]:
        w.wait()
    up2, down2 = to(a, b_next), to(a, b_last)
    waits = [
        (sent(spot(i, b), spot(i, b_last), 5 + 2 * i, up2), sent(spot(i, b), spot(i, b_next), 6 + 2 * i, down2))
        for i in range(4)
    ]
    late = []
    for i in range(4):
        w_last, w_next = waits[i]
        far = spot(i, (b + 2) % 4)
        if i < 2:
            w_last.wait()
            late += [sent(spot(i, b_last), far, 13 + i, up2), w_next]
        else:
            w_next.wait()
            late += [sent(spot(i, b_next), far, 13 + i, down2), w_last]
    for w in late:
        w.wait()
    remote(out.at[me["c"]], out.at[me["c"]], send_sem.at[0], recv_sem.at[0], twin).start()
    remote(out.at[me["c"]], out.at[1 - me["c"]], send_sem.at[0], recv_sem.at[0], twin).wait()


def gather_plane(block, cid):
    vmem = pl.BlockSpec(memory_space=pltpu.VMEM)
    return pl.pallas_call(
        gather_body,
        out_shape=jax.ShapeDtypeStruct((2, 4, 4) + block.shape, block.dtype),
        in_specs=[vmem],
        out_specs=vmem,
        scratch_shapes=[
            pltpu.SemaphoreType.DMA((17,)),
            pltpu.SemaphoreType.DMA((17,)),
            pltpu.SemaphoreType.DMA((1,)),
        ],
        compiler_params=pltpu.CompilerParams(
            collective_id=cid, has_side_effects=True, vmem_limit_bytes=32 * 1024 * 1024
        ),
    )(block)


class SideNear:
    sems = 7

    def shape(self, ffn):
        return jax.ShapeDtypeStruct((4, 2) + ffn.shape[1:], ffn.dtype)

    def places(self, me):
        a, b, to = virtual(me, "z", "x")
        return [to((a + 1) % 4, b), to((a + 3) % 4, b), {**me, "c": 1 - me["c"]}]

    def start(self, me, ffn, near, send_sem, recv_sem):
        a, b, to = virtual(me, "z", "x")
        c = me["c"]
        twin = {**me, "c": 1 - c}
        a_next, a_last, a_far = (a + 1) % 4, (a + 3) % 4, (a + 2) % 4
        up, down = to(a_next, b), to(a_last, b)

        def sent(src, dst_here, sem, at):
            remote(src, src, send_sem.at[sem], recv_sem.at[sem], at).start()
            return remote(src, dst_here, send_sem.at[sem], recv_sem.at[sem], at)

        keep = pltpu.make_async_copy(ffn.at[c], near.at[a, c], recv_sem.at[1])
        keep.start()
        remote(ffn.at[1 - c], near.at[b, c], send_sem.at[0], recv_sem.at[0], twin).start()
        keep.wait()
        remote(ffn.at[1 - c], near.at[a, 1 - c], send_sem.at[0], recv_sem.at[0], twin).wait()
        first = [sent(near.at[a], near.at[a_last], 2, up), sent(near.at[a], near.at[a_next], 3, down)]

        def middle():
            for w in first:
                w.wait()
            self.late = [
                sent(near.at[a_last, 0], near.at[a_far, 0], 4, up),
                sent(near.at[a_next, 1], near.at[a_far, 1], 5, down),
            ]

        self.middle = middle

    def finish(self):
        for w in self.late:
            w.wait()


class SideGather:
    sems = 16

    def shape(self, near):
        return jax.ShapeDtypeStruct((4, 4) + near.shape[1:], near.dtype)

    def places(self, me):
        a, b, to = virtual(me, "z", "x")
        return [to(a, (b + 1) % 4), to(a, (b + 3) % 4)]

    def start(self, me, near, out, send_sem, recv_sem):
        a, b, to = virtual(me, "z", "x")
        b_next, b_last = (b + 1) % 4, (b + 3) % 4
        up, down = to(a, b_next), to(a, b_last)

        def spot(av, bv):
            at = to(av, bv)
            return out.at[at["z"], at["x"]]

        def sent(src, dst, dst_here, sem, at):
            remote(src, dst, send_sem.at[sem], recv_sem.at[sem], at).start()
            return remote(src, dst_here, send_sem.at[sem], recv_sem.at[sem], at)

        self.waits = []
        for i in range(4):
            self.waits.append(
                (
                    sent(near.at[i], spot(i, b), spot(i, b_last), 2 * i, up),
                    sent(near.at[i], spot(i, b), spot(i, b_next), 2 * i + 1, down),
                )
            )
        self.late = []
        for i in range(4):
            copy = pltpu.make_async_copy(near.at[i], spot(i, b), recv_sem.at[12 + i])
            copy.start()
            self.late.append(copy)

        def middle():
            for i in range(4):
                w_last, w_next = self.waits[i]
                far = spot(i, (b + 2) % 4)
                if i < 2:
                    w_last.wait()
                    src = spot(i, b_last)
                    self.late += [sent(src, src, far, 8 + i, up), w_next]
                else:
                    w_next.wait()
                    src = spot(i, b_next)
                    self.late += [sent(src, src, far, 8 + i, down), w_last]

        self.middle = middle

    def finish(self):
        for w in self.late:
            w.wait()


class SideSwap:
    sems = 33
    axes = ("z", "x", "c")

    def shape(self, parts):
        return jax.ShapeDtypeStruct(parts.shape, parts.dtype)

    def places(self, me):
        return [moved(me, decode(p, self.axes), -1) for p in range(1, 32)]

    def start(self, me, parts, out, send_sem, recv_sem):
        def copies(p, arriving):
            off = decode(p, self.axes)
            target = moved(me, off, 1)
            spot = moved(me, off, -1) if arriving else me
            return remote(
                parts.at[rank(target, self.axes)],
                out.at[rank(spot, self.axes)],
                send_sem.at[p],
                recv_sem.at[p],
                target,
            )

        def launch(p, carry):
            copies(p, False).start()
            return carry

        def finish(p, carry):
            copies(p, True).wait()
            return carry

        lax.fori_loop(1, 32, launch, 0)
        mine = rank(me, self.axes)
        copy = pltpu.make_async_copy(parts.at[mine], out.at[mine], recv_sem.at[32])
        copy.start()
        copy.wait()
        self.finish = lambda: lax.fori_loop(1, 32, finish, 0)
        self.middle = lambda: None


def reduce_body(by0, by1, by2, by3, total, p, r1, r2, q, r3, r4, send_sem, recv_sem, local_sem):
    me = place()
    a, b, to = virtual(me, "z", "x")
    a_next, a_last, a_far = (a + 1) % 4, (a + 3) % 4, (a + 2) % 4
    b_next, b_last, b_far = (b + 1) % 4, (b + 3) % 4, (b + 2) % 4
    up, down = to(a_next, b), to(a_last, b)
    up2, down2 = to(a, b_next), to(a, b_last)
    barrier = greet_all([up, down, up2, down2])

    def at(ref, av, bv):
        w = to(av, bv)
        return ref.at[w["z"], w["x"]]

    loads = [pltpu.make_async_copy(by, p.at[i], local_sem.at[i]) for i, by in enumerate((by0, by1, by2, by3))]
    for load in loads:
        load.start()
    pl.semaphore_wait(barrier, 4)
    for load in loads:
        load.wait()
    first = []
    for i in range(4):
        first.append(remote(at(p, a_far, i), r1.at[i], send_sem.at[i], recv_sem.at[i], up if i < 2 else down))
        first[-1].start()
    second = []

    def onward(i, way, src):
        sem = 4 + 2 * i + way
        copy = remote(src, r2.at[way, i], send_sem.at[sem], recv_sem.at[sem], down if way else up)
        copy.start()
        second.append(copy)

    for i in range(4):
        onward(i, 1 if i < 2 else 0, at(p, a_last if i < 2 else a_next, i))
    for i in range(4):
        first[i].wait()
        dest = at(p, a_next if i < 2 else a_last, i)
        dest[...] = (dest[...].astype(F32) + r1[i].astype(F32)).astype(BF)
        onward(i, 0 if i < 2 else 1, dest)
    for copy in second:
        copy.wait()
    for i in range(4):
        q[i] = (at(p, a, i)[...].astype(F32) + r2[0, i].astype(F32) + r2[1, i].astype(F32)).astype(BF)
    lo, hi = pl.ds(0, BLK // 2), pl.ds(BLK // 2, BLK // 2)
    one = remote(q.at[b_far, lo], r3.at[0], send_sem.at[12], recv_sem.at[12], up2)
    two = remote(q.at[b_far, hi], r3.at[1], send_sem.at[13], recv_sem.at[13], down2)
    one.start()
    two.start()
    three = remote(q.at[b_next, hi], r4.at[0, hi], send_sem.at[14], recv_sem.at[14], up2)
    four = remote(q.at[b_last, lo], r4.at[1, lo], send_sem.at[15], recv_sem.at[15], down2)
    three.start()
    four.start()
    one.wait()
    dest = q.at[b_next, lo]
    dest[...] = (dest[...].astype(F32) + r3[0].astype(F32)).astype(BF)
    five = remote(q.at[b_next, lo], r4.at[0, lo], send_sem.at[16], recv_sem.at[16], up2)
    five.start()
    two.wait()
    dest = q.at[b_last, hi]
    dest[...] = (dest[...].astype(F32) + r3[1].astype(F32)).astype(BF)
    six = remote(q.at[b_last, hi], r4.at[1, hi], send_sem.at[17], recv_sem.at[17], down2)
    six.start()
    for copy in (three, four, five, six):
        copy.wait()
    total[...] = q[b].astype(F32) + r4[0].astype(F32) + r4[1].astype(F32)


def reduce_plane(parts, cid):
    block = parts[0].shape[1:]
    return pl.pallas_call(
        reduce_body,
        out_shape=jax.ShapeDtypeStruct(block, F32),
        in_specs=[pl.BlockSpec(memory_space=pl.ANY)] * 4,
        out_specs=pl.BlockSpec(memory_space=pltpu.VMEM),
        scratch_shapes=[
            pltpu.VMEM((4, 4) + block, BF),
            pltpu.VMEM((4,) + block, BF),
            pltpu.VMEM((2, 4) + block, BF),
            pltpu.VMEM((4,) + block, BF),
            pltpu.VMEM((2, BLK // 2, D), BF),
            pltpu.VMEM((2,) + block, BF),
            pltpu.SemaphoreType.DMA((18,)),
            pltpu.SemaphoreType.DMA((18,)),
            pltpu.SemaphoreType.DMA((4,)),
        ],
        compiler_params=pltpu.CompilerParams(
            collective_id=cid, has_side_effects=True, vmem_limit_bytes=48 * 1024 * 1024
        ),
    )(*parts)


def gram_body(kept, moms, grad, extra, gram, extras, mom, flat, parts, p, got, mine, bx, send_sem, recv_sem, local_sem):
    me = place()
    c, z = me["c"], me["z"]
    axes = ("x", "y")
    twin = {**me, "c": 1 - c}
    barrier = pltpu.get_barrier_semaphore()
    for i in range(1, 16):
        pl.semaphore_signal(barrier, inc=1, device_id=device(moved(me, decode(i, axes), -1)), device_id_type=MESH)
    for i in range(4):
        pl.semaphore_signal(barrier, inc=1, device_id=device({**twin, "y": (me["y"] + i) % 4}), device_id_type=MESH)
    new = 0.95 * moms[...].astype(F32) + grad[...]
    new = jnp.where(lax.broadcasted_iota(jnp.int32, (BLK, 1), 0) < kept[...], new, 0.0)
    mom[...] = new
    flat[...] = new.astype(BF)
    start = 0
    for j in range(D // 128):
        tall = 128 * (j + 1)
        value = dot(flat[:, pl.ds(0, tall)], flat[:, pl.ds(128 * j, 128)], TN).astype(BF)
        while tall:
            part, row = divmod(start, PART)
            size = min(tall, PART - row)
            done = 128 * (j + 1) - tall
            parts[part // 16, part % 16, pl.ds(row, size), :] = value[done : done + size]
            start, tall = start + size, tall - size
    for part in range(start // PART, 32):
        row = start % PART if part == start // PART else 0
        parts[part // 16, part % 16, pl.ds(row, PART - row), :] = jnp.zeros((PART - row, 128), BF)
    load = pltpu.make_async_copy(parts.at[c], p, local_sem.at[0])
    load.start()
    keep = pltpu.make_async_copy(extra, extras.at[rank(me, ("c", "y"))], local_sem.at[1])
    keep.start()
    pl.semaphore_wait(barrier, 19)
    swap = remote(parts.at[1 - c], got, send_sem.at[0, 0], recv_sem.at[0, 0], twin)
    swap.start()
    extra_waits = []
    for i in range(1, 8):
        off = decode(i, ("c", "y"))
        target, source = moved(me, off, 1), moved(me, off, -1)
        sems = (send_sem.at[3, i], recv_sem.at[3, i])
        remote(extra, extras.at[rank(me, ("c", "y"))], *sems, target).start()
        extra_waits.append(remote(extra, extras.at[rank(source, ("c", "y"))], *sems, target))
    load.wait()
    swap.wait()
    for i in range(16):
        p[i] = (p[i].astype(F32) + got[i].astype(F32)).astype(BF)
    waits = []
    for i in range(1, 16):
        off = decode(i, axes)
        target, source = moved(me, off, 1), moved(me, off, -1)
        sems = (send_sem.at[1, i], recv_sem.at[1, i])
        remote(p.at[rank(target, axes)], mine.at[rank(me, axes)], *sems, target).start()
        waits.append(remote(p.at[rank(target, axes)], mine.at[rank(source, axes)], *sems, target))
    own = pltpu.make_async_copy(p.at[rank(me, axes)], mine.at[rank(me, axes)], local_sem.at[0])
    own.start()
    own.wait()
    for w in waits:
        w.wait()
    sums = []
    for i in range(4):
        part = mine[4 * i].astype(F32)
        for j in range(1, 4):
            part = part + mine[4 * i + j].astype(F32)
        sums.append(part)
    whole = sums[0] + sums[1] + sums[2] + sums[3]
    for i in range(4):
        bx[i] = jnp.where(z < 3, whole, sums[i]).astype(BF)
    waits = []
    spot = gram.at[c]
    for i in range(1, 16):
        off = decode(i, axes)
        target, source = moved(me, off, 1), moved(me, off, -1)
        sems = (send_sem.at[2, i], recv_sem.at[2, i])
        remote(bx.at[target["x"]], spot.at[rank(me, axes)], *sems, target).start()
        waits.append(remote(bx.at[target["x"]], spot.at[rank(source, axes)], *sems, target))
    own = pltpu.make_async_copy(bx.at[me["x"]], spot.at[rank(me, axes)], local_sem.at[0])
    own.start()
    own.wait()
    for w in waits:
        w.wait()
    remote(gram.at[c], gram.at[c], send_sem.at[2, 0], recv_sem.at[2, 0], twin).start()
    remote(gram.at[c], gram.at[1 - c], send_sem.at[2, 0], recv_sem.at[2, 0], twin).wait()
    keep.wait()
    for w in extra_waits:
        w.wait()


def gram_sum(kept, moms, grad, extra, cid):
    vmem = pl.BlockSpec(memory_space=pltpu.VMEM)
    half = (16, PART, 128)
    return pl.pallas_call(
        gram_body,
        out_shape=[
            jax.ShapeDtypeStruct((2,) + half, BF),
            jax.ShapeDtypeStruct((8,) + extra.shape, extra.dtype),
            jax.ShapeDtypeStruct(grad.shape, F32),
        ],
        in_specs=[vmem] * 4,
        out_specs=[vmem] * 3,
        scratch_shapes=[
            pltpu.VMEM(moms.shape, BF),
            pltpu.VMEM((2,) + half, BF),
            pltpu.VMEM(half, BF),
            pltpu.VMEM(half, BF),
            pltpu.VMEM(half, BF),
            pltpu.VMEM((4,) + half[1:], BF),
            pltpu.SemaphoreType.DMA((4, 16)),
            pltpu.SemaphoreType.DMA((4, 16)),
            pltpu.SemaphoreType.DMA((2,)),
        ],
        compiler_params=pltpu.CompilerParams(
            collective_id=cid, has_side_effects=True, vmem_limit_bytes=48 * 1024 * 1024
        ),
    )(kept, moms, grad, extra)


def halo_body(sign, kinds, side, *refs):
    k = len(kinds)
    side_in, ins, outs, side_out = refs[0], refs[1 : 1 + k], refs[1 + k : 1 + 2 * k], refs[1 + 2 * k]
    send_sem, recv_sem, local_sem, side_send, side_recv = refs[2 + 2 * k :]
    me = place()
    dp = lax.axis_index("dp")
    y = lax.axis_index("tensor")
    barrier = pltpu.get_barrier_semaphore()
    offs = [(d, t) for d in range(3) for t in range(4)]

    def dev(d, t, way):
        shift = d if way > 0 else 32 - d
        return {"dp": (dp + shift) % 32, "tensor": (y + (t if way > 0 else 4 - t)) % 4}

    for d, t in offs[1:]:
        back = dev(d, t, -1) if sign > 0 else {"dp": (dp + d) % 32, "tensor": (y + 4 - t) % 4}
        pl.semaphore_signal(barrier, inc=1, device_id=back, device_id_type=MESH)
    more = side.places(me)
    greet_all(more)
    own = []
    copies = []
    for i, kind in enumerate(kinds):
        for p, (d, t) in enumerate(offs):
            if kind == "near" and d > 0:
                continue
            ty = (y + t) % 4
            sy = (y + 4 - t) % 4
            src = ins[i].at[pl.ds(pl.multiple_of((2 - d) * TOK + ty * QTOK, QTOK), QTOK)] if kind == "split" else ins[i]
            tdp = (dp + d) % 32 if sign > 0 else (dp + 32 - d) % 32
            if kind == "near":
                to, frm = outs[i].at[y], outs[i].at[sy]
            elif kind == "all":
                rows = pl.ds((2 - d) * TOK, TOK)
                to, frm = (outs[i].at[rows, pl.ds(pl.multiple_of(at * 128, 128), 128)] for at in (y, sy))
            else:
                to, frm = outs[i].at[d, y], outs[i].at[d, sy]
            if p == 0:
                own.append(pltpu.make_async_copy(src, to, local_sem.at[i]))
                continue
            args = dict(send_sem=send_sem.at[i, p], recv_sem=recv_sem.at[i, p], device_id={"dp": tdp, "tensor": ty}, device_id_type=MESH)
            copies.append(
                (
                    pltpu.make_async_remote_copy(src_ref=src, dst_ref=to, **args),
                    pltpu.make_async_remote_copy(src_ref=src, dst_ref=frm, **args),
                )
            )
    for copy in own:
        copy.start()
    pl.semaphore_wait(barrier, len(offs) - 1 + len(more))
    for out_copy, _ in copies:
        out_copy.start()
    side.start(me, side_in, side_out, side_send, side_recv)
    for copy in own:
        copy.wait()
    side.middle()
    for _, in_copy in copies:
        in_copy.wait()
    side.finish()


def halo(items, sign, cid, side, side_in):
    arrays = [a for a, _ in items]
    kinds = [m for _, m in items]
    shapes = []
    for a, m in items:
        shapes.append({"near": (4,) + a.shape, "all": (3 * TOK, 512), "split": (3, 4, QTOK, 512)}[m])
    k = len(items)
    return pl.pallas_call(
        functools.partial(halo_body, sign, kinds, side),
        out_shape=[jax.ShapeDtypeStruct(s, a.dtype) for s, a in zip(shapes, arrays)] + [side.shape(side_in)],
        in_specs=[pl.BlockSpec(memory_space=pl.ANY)] + [pl.BlockSpec(memory_space=pltpu.VMEM)] * k,
        out_specs=[pl.BlockSpec(memory_space=pltpu.VMEM)] * k + [pl.BlockSpec(memory_space=pl.ANY)],
        scratch_shapes=[
            pltpu.SemaphoreType.DMA((k, 12)),
            pltpu.SemaphoreType.DMA((k, 12)),
            pltpu.SemaphoreType.DMA((k,)),
            pltpu.SemaphoreType.DMA((side.sems,)),
            pltpu.SemaphoreType.DMA((side.sems,)),
        ],
        compiler_params=pltpu.CompilerParams(collective_id=cid, has_side_effects=True),
    )(side_in, *arrays)


def sum_body(fn, both, spread, side, n_extra, n_local, n_ag, *refs):
    if side is not None:
        side_in, side_out, side_send, side_recv = refs[0], refs[1 + 1 + n_extra + n_local + n_ag], refs[-2], refs[-1]
        refs = refs[1 : 2 + n_extra + n_local + n_ag] + refs[3 + n_extra + n_local + n_ag : -2]
    parts = refs[0]
    extras = refs[1 : 1 + n_extra]
    locals_ = refs[1 + n_extra : 1 + n_extra + n_local]
    gathers = refs[1 + n_extra + n_local : 1 + n_extra + n_local + n_ag]
    pre, recv, agbuf, send_sem, recv_sem, local_sem = refs[1 + n_extra + n_local + n_ag :]
    me = place()
    c, y = me["c"], me["y"]
    twin = {**me, "c": 1 - c}
    near = [(moved(me, {"y": i}, 1), moved(me, {"y": i}, -1)) for i in range(1, 4)]
    use_twin = both or spread
    places = [source for _, source in near] + ([twin] if use_twin else [])
    if side is not None:
        places += side.places(me)
    barrier = greet_all(places)
    pl.semaphore_wait(barrier, len(places))
    if both:
        swap = remote(parts.at[1 - c], pre, send_sem.at[0], recv_sem.at[0], twin)
        swap.start()
        if side is not None:
            side.start(me, side_in, side_out, side_send, side_recv)
        swap.wait()
        for i in range(4):
            pre[i] = (pre[i].astype(F32) + parts[c, i].astype(F32)).astype(BF)
        mine = pre
    else:
        mine = parts
    waits = []
    for i, (target, source) in enumerate(near):
        sems = (send_sem.at[1 + i], recv_sem.at[1 + i])
        remote(mine.at[target["y"]], recv.at[i], *sems, target).start()
        waits.append(remote(mine.at[target["y"]], recv.at[i], *sems, target))
    if side is not None and not both:
        side.start(me, side_in, side_out, side_send, side_recv)
    total = mine[y].astype(F32)
    for i in range(3):
        waits[i].wait()
        total = total + recv[i].astype(F32)
    local_vals, ag_vals = fn(total, *[e[...] for e in extras])
    for i, value in enumerate(ag_vals):
        agbuf[i] = value.astype(BF)
    waits, own = [], []
    for j in range(n_ag):
        out = gathers[j].at[c] if spread else gathers[j]
        for i, (target, source) in enumerate(near):
            sems = (send_sem.at[4 + 3 * j + i], recv_sem.at[4 + 3 * j + i])
            remote(agbuf.at[j], out.at[y], *sems, target).start()
            waits.append(remote(agbuf.at[j], out.at[source["y"]], *sems, target))
        own.append(pltpu.make_async_copy(agbuf.at[j], out.at[y], local_sem.at[j]))
        own[-1].start()
    for ref, value in zip(locals_, local_vals):
        ref[...] = value
    if side is not None:
        side.middle()
    for copy in own + waits:
        copy.wait()
    if spread:
        for j in range(n_ag):
            g = gathers[j]
            sems = (send_sem.at[4 + 3 * n_ag + j], recv_sem.at[4 + 3 * n_ag + j])
            remote(g.at[c], g.at[c], *sems, twin).start()
            remote(g.at[c], g.at[1 - c], *sems, twin).wait()
    if side is not None:
        side.finish()


def sum_then_gather(fn, parts, extras, local_shapes, n_ag, spread, cid, side=None, side_in=None):
    both = parts.ndim == 4
    rows = parts.shape[-2:]
    vmem = pl.BlockSpec(memory_space=pltpu.VMEM)
    gathered = ((2, 4) if spread else (4,)) + rows
    n_sem = 4 + 4 * n_ag
    hbm = pl.BlockSpec(memory_space=pl.ANY)
    more = side is not None
    return pl.pallas_call(
        functools.partial(sum_body, fn, both, spread, side, len(extras), len(local_shapes), n_ag),
        out_shape=[jax.ShapeDtypeStruct(s, F32) for s in local_shapes]
        + [jax.ShapeDtypeStruct(gathered, BF)] * n_ag
        + ([side.shape(side_in)] if more else []),
        in_specs=[hbm] * more + [vmem] * (1 + len(extras)),
        out_specs=[vmem] * (len(local_shapes) + n_ag) + [hbm] * more,
        scratch_shapes=[
            pltpu.VMEM((4,) + rows, BF),
            pltpu.VMEM((3,) + rows, BF),
            pltpu.VMEM((n_ag,) + rows, BF),
            pltpu.SemaphoreType.DMA((n_sem,)),
            pltpu.SemaphoreType.DMA((n_sem,)),
            pltpu.SemaphoreType.DMA((n_ag,)),
        ]
        + ([pltpu.SemaphoreType.DMA((side.sems,))] * 2 if more else []),
        compiler_params=pltpu.CompilerParams(
            collective_id=cid, has_side_effects=True, vmem_limit_bytes=32 * 1024 * 1024
        ),
    )(*([side_in] if more else []), parts, *extras)


def inv_rms(values):
    return lax.rsqrt(jnp.mean(values * values, axis=-1, keepdims=True) + EPSILON)


def rms_back(values, gain, s, grad):
    scaled = gain * grad
    dv = s * scaled - values * (s * s * s * jnp.mean(scaled * values, axis=-1, keepdims=True))
    return dv, jnp.sum(grad * values * s, axis=0, keepdims=True)


def rot(values, cosine, sine):
    front, back = values[:, :128], values[:, 128:]
    return jnp.concatenate([front * cosine - back * sine, back * cosine + front * sine], axis=-1)


def unrot(values, cosine, sine):
    return rot(values, cosine, -sine)


def mid_fn(u, hidden, g1, g2):
    hmid = hidden + u * inv_rms(u) * g1
    return [u, hmid], [hmid * inv_rms(hmid) * g2]


def ffn_out_fn(f, hmid, out_grad, g3):
    s = inv_rms(f)
    block = hmid + f * s * g3
    df, dg3 = rms_back(f, g3, s, out_grad)
    return [block, dg3], [df]


def ffn_in_fn(dbin, hmid, u, out_grad, g1, g2):
    dm, dg2 = rms_back(hmid, g2, inv_rms(hmid), dbin)
    dhmid = out_grad + dm
    du, dg1 = rms_back(u, g1, inv_rms(u), dhmid)
    return [dhmid, dg1, dg2], [du]


def last_fn(da, hidden, dhmid, block, g0):
    dh, dg0 = rms_back(hidden, g0, inv_rms(hidden), da)
    return [dg0], [dhmid + dh, block]


def dot(a, b, dims):
    return lax.dot_general(a, b, (dims, ((), ())), preferred_element_type=F32)


NN = ((1,), (0,))
NT = ((1,), (1,))
TN = ((0,), (0,))


def ffn_body(blocks, tokens, dense, gate, up, mixed, f):
    for k in range(32):
        for m in range(3):
            dense[m, pl.ds(ROWS * k, ROWS), :] = blocks[k, pl.ds(ROWS * m, ROWS), :]
    inner = math.sqrt(2.0 / math.pi)

    def body(i, carry):
        rows = pl.ds(pl.multiple_of(i * TOK, TOK), TOK)
        low = tokens[rows, :]
        g = dot(low, dense[0], NN)
        gate[rows, :] = g
        u = dot(low, dense[1], NN)
        up[rows, :] = u
        th = jnp.tanh(inner * (g + 0.044715 * g * g * g))
        z = (0.5 * g * (1.0 + th) * u).astype(BF)
        mixed[rows, :] = z
        f[rows, :] = dot(z, dense[2], NT).astype(BF)
        return carry

    lax.fori_loop(0, 2, body, 0)


def ffn_forward(blocks, tokens):
    vmem = pl.BlockSpec(memory_space=pltpu.VMEM)
    return pl.pallas_call(
        ffn_body,
        out_shape=[
            jax.ShapeDtypeStruct((3, D, HALF), BF),
            jax.ShapeDtypeStruct((512, HALF), F32),
            jax.ShapeDtypeStruct((512, HALF), F32),
            jax.ShapeDtypeStruct((512, HALF), BF),
            jax.ShapeDtypeStruct((512, D), BF),
        ],
        in_specs=[vmem] * 2,
        out_specs=[vmem] * 5,
        compiler_params=pltpu.CompilerParams(vmem_limit_bytes=48 * 1024 * 1024),
    )(blocks, tokens)


def project_body(got, hidden, w_qkv, woT, gains, normed, q, kv, tail):
    for k in range(32):
        z, x, c = k // 8, k // 2 % 4, k % 2
        here, rows = pl.ds(ROWS * k, ROWS), pl.ds(0, ROWS)
        w_qkv[here, :] = got[c, z, x, 0, rows, :]
        woT[here, :] = got[c, z, x, 1, rows, pl.ds(0, HD)]
        tail[here, :] = got[c, z, x, 1, rows, pl.ds(HD, 128)]
    turned = tail[...].astype(F32).T
    gains[...] = turned[:8]
    h = hidden[...]
    low = (h * inv_rms(h) * turned[0:1]).astype(BF)
    normed[...] = low
    out = dot(low, w_qkv[...], NN)
    q[...] = out[:, :HD]
    kv[...] = out[:, HD:].astype(BF)


def project(got, hidden):
    vmem = pl.BlockSpec(memory_space=pltpu.VMEM)
    shapes = [((D, 384), BF), ((D, HD), BF), ((8, D), F32), ((TOK, D), BF), ((TOK, HD), F32), ((TOK, 128), BF)]
    return pl.pallas_call(
        project_body,
        out_shape=[jax.ShapeDtypeStruct(s, t) for s, t in shapes],
        in_specs=[vmem] * 2,
        out_specs=[vmem] * len(shapes),
        scratch_shapes=[pltpu.VMEM((D, 128), BF)],
        compiler_params=pltpu.CompilerParams(vmem_limit_bytes=32 * 1024 * 1024),
    )(got, hidden)


def attention_body(kv, sort, q_raw, gq, gk, cosine, sine, seg_q, seg_k, woT, qr, kr, vb, k_own, probs, ob, u):
    sorted_kv = dot(kv[...], sort[...], NN)
    k_raw = sorted_kv[:, :HD]
    v = sorted_kv[:, HD:].astype(BF)
    vb[...] = v
    k_own[...] = k_raw[2 * TOK :]
    k = rot(k_raw * inv_rms(k_raw) * gk[...], cosine[...], sine[...]).astype(BF)
    kr[...] = k
    raw = q_raw[...]
    q = rot(raw * inv_rms(raw) * gq[...], cosine[pl.ds(2 * TOK, TOK), :], sine[pl.ds(2 * TOK, TOK), :]).astype(BF)
    qr[...] = q
    shape = (TOK, 3 * TOK)
    gap = lax.broadcasted_iota(jnp.int32, shape, 0) + 2 * TOK - lax.broadcasted_iota(jnp.int32, shape, 1)
    allowed = (seg_q[...] == seg_k[...]) & (gap >= 0) & (gap < WINDOW)
    scores = jnp.where(allowed, dot(q, k, NT) * (HD**-0.5), -1e30)
    exps = jnp.exp(scores - jnp.max(scores, axis=-1, keepdims=True))
    p = exps / jnp.sum(exps, axis=-1, keepdims=True)
    probs[...] = p
    o = dot(p.astype(BF), v, NN).astype(BF)
    ob[...] = o
    u[...] = dot(o, woT[...], NT).astype(BF)


def attention(*args):
    vmem = pl.BlockSpec(memory_space=pltpu.VMEM)
    wide = 3 * TOK
    shapes = [
        ((TOK, HD), BF),
        ((wide, HD), BF),
        ((wide, HD), BF),
        ((TOK, HD), F32),
        ((TOK, wide), F32),
        ((TOK, HD), BF),
        ((TOK, D), BF),
    ]
    return pl.pallas_call(
        attention_body,
        out_shape=[jax.ShapeDtypeStruct(s, t) for s, t in shapes],
        in_specs=[vmem] * len(args),
        out_specs=[vmem] * len(shapes),
        compiler_params=pltpu.CompilerParams(vmem_limit_bytes=32 * 1024 * 1024),
    )(*args)


def attention_back_body(*refs):
    du_all, woT, vb, probs, kr, qr, q_raw, gq, gk, cosine, sine, k_own, normed, ob = refs[:14]
    dkv_all, a_all, ob_all, dq_all, dgq, dgk = refs[14:20]
    part, got, dkvb, send_sem, recv_sem, local_sem = refs[20:]
    me = place()
    c, y, dp = me["c"], me["y"], lax.axis_index("dp")
    twin = {**me, "c": 1 - c}

    def along(d, t):
        at = (dp + d + 32) % 32
        return {"z": at // 8, "x": (at // 2) % 4, "c": at % 2, "y": (y + t + 4) % 4}

    offs = [(d, t) for d in range(3) for t in range(4)][1:]
    group = [decode(p, ("c", "y")) for p in range(1, 8)]
    places = [along(d, -t) for d, t in offs] + [moved(me, off, -1) for off in group]
    barrier = greet_all(places)
    pl.semaphore_wait(barrier, len(places))
    waits = []

    def to_twin(src, out, sem):
        remote(src, out.at[c], send_sem.at[sem], recv_sem.at[sem], twin).start()
        waits.append(remote(src, out.at[1 - c], send_sem.at[sem], recv_sem.at[sem], twin))
        own = pltpu.make_async_copy(src, out.at[c], local_sem.at[sem])
        own.start()
        waits.append(own)

    to_twin(normed, a_all, 0)
    to_twin(ob, ob_all, 1)
    scale = HD**-0.5
    dub = du_all[pl.ds(pl.multiple_of(c * TOK, TOK), TOK), :]
    dob = dot(dub, woT[...], NN).astype(BF)
    p = probs[...]
    dp_ = dot(dob, vb[...], NT)
    ds = (p * (dp_ - jnp.sum(p * dp_, axis=-1, keepdims=True))).astype(BF)
    part[:, pl.ds(0, HD)] = (dot(ds, qr[...], TN) * scale).astype(BF)
    part[:, pl.ds(HD, HD)] = dot(p.astype(BF), dob, TN).astype(BF)
    own = pltpu.make_async_copy(part.at[pl.ds(pl.multiple_of(2 * TOK + y * QTOK, QTOK), QTOK)], got.at[0, y], local_sem.at[2])
    own.start()
    halo_waits = []
    for i, (d, t) in enumerate(offs):
        target = along(-d, t)
        src = part.at[pl.ds(pl.multiple_of((2 - d) * TOK + target["y"] * QTOK, QTOK), QTOK)]
        sems = (send_sem.at[3 + i], recv_sem.at[3 + i])
        remote(src, got.at[d, y], *sems, target).start()
        halo_waits.append(remote(src, got.at[d, (y + 4 - t) % 4], *sems, target))
    raw = q_raw[...]
    dqr = dot(ds, kr[...], NN) * scale
    here = pl.ds(2 * TOK, TOK)
    dq, dg = rms_back(raw, gq[...], inv_rms(raw), unrot(dqr, cosine[here, :], sine[here, :]))
    dgq[...] = dg
    dq_all[c] = dq.astype(BF)
    remote(dq_all.at[c], dq_all.at[c], send_sem.at[2], recv_sem.at[2], twin).start()
    waits.append(remote(dq_all.at[c], dq_all.at[1 - c], send_sem.at[2], recv_sem.at[2], twin))
    own.wait()
    for w in halo_waits:
        w.wait()
    total = got[0, 0].astype(F32)
    for i in range(1, 12):
        total = total + got[i // 4, i % 4].astype(F32)
    k = k_own[pl.ds(pl.multiple_of(y * QTOK, QTOK), QTOK), :]
    rows = pl.ds(pl.multiple_of(2 * TOK + y * QTOK, QTOK), QTOK)
    dk, dg = rms_back(k, gk[...], inv_rms(k), unrot(total[:, :HD], cosine[rows, :], sine[rows, :]))
    dgk[...] = dg
    dkvb[:, pl.ds(0, HD)] = dk.astype(BF)
    dkvb[:, pl.ds(HD, HD)] = total[:, HD:].astype(BF)
    own = pltpu.make_async_copy(dkvb, dkv_all.at[c, y], local_sem.at[3])
    own.start()
    waits.append(own)
    for i, off in enumerate(group):
        target, source = moved(me, off, 1), moved(me, off, -1)
        sems = (send_sem.at[14 + i], recv_sem.at[14 + i])
        remote(dkvb, dkv_all.at[c, y], *sems, target).start()
        waits.append(remote(dkvb, dkv_all.at[source["c"], source["y"]], *sems, target))
    for w in waits:
        w.wait()


def attention_back(cid, *args):
    vmem = pl.BlockSpec(memory_space=pltpu.VMEM)
    shapes = [
        ((2, 4, QTOK, 512), BF),
        ((2, TOK, D), BF),
        ((2, TOK, HD), BF),
        ((2, TOK, HD), BF),
        ((1, HD), F32),
        ((1, HD), F32),
    ]
    return pl.pallas_call(
        attention_back_body,
        out_shape=[jax.ShapeDtypeStruct(s, t) for s, t in shapes],
        in_specs=[vmem] * len(args),
        out_specs=[vmem] * len(shapes),
        scratch_shapes=[
            pltpu.VMEM((3 * TOK, 512), BF),
            pltpu.VMEM((3, 4, QTOK, 512), BF),
            pltpu.VMEM((QTOK, 512), BF),
            pltpu.SemaphoreType.DMA((21,)),
            pltpu.SemaphoreType.DMA((21,)),
            pltpu.SemaphoreType.DMA((4,)),
        ],
        compiler_params=pltpu.CompilerParams(
            collective_id=cid, has_side_effects=True, vmem_limit_bytes=40 * 1024 * 1024
        ),
    )(*args)


def ffn_back_body(grads, gate, up, dense, dgate, dup, part):
    inner = math.sqrt(2.0 / math.pi)

    def body(i, carry):
        rows = pl.ds(pl.multiple_of(i * TOK, TOK), TOK)
        dz = dot(grads[rows, :], dense[2], NN)
        g = gate[rows, :]
        th = jnp.tanh(inner * (g + 0.044715 * g * g * g))
        slope = 0.5 * (1.0 + th) + 0.5 * g * (1.0 - th * th) * inner * (1.0 + 3 * 0.044715 * g * g)
        dg = (dz * up[rows, :] * slope).astype(BF)
        du = (dz * (0.5 * g * (1.0 + th))).astype(BF)
        dgate[rows, :] = dg
        dup[rows, :] = du
        part[rows, :] = (dot(dg, dense[0], NT) + dot(du, dense[1], NT)).astype(BF)
        return carry

    lax.fori_loop(0, 2, body, 0)


def ffn_backward(*args):
    vmem = pl.BlockSpec(memory_space=pltpu.VMEM)
    shapes = [(512, HALF), (512, HALF), (512, D)]
    return pl.pallas_call(
        ffn_back_body,
        out_shape=[jax.ShapeDtypeStruct(s, BF) for s in shapes],
        in_specs=[vmem] * 4,
        out_specs=[vmem] * 3,
        compiler_params=pltpu.CompilerParams(vmem_limit_bytes=48 * 1024 * 1024),
    )(*args)


def rope_tables():
    freqs = 10000.0 ** (-np.arange(128, dtype=np.float64) * 2.0 / 256)
    base = (np.arange(32, dtype=np.float64) - 2)[:, None] * 256 * freqs[None]
    step = np.arange(768, dtype=np.float64)[:, None] * freqs[None]
    return [t.astype(np.float32) for t in (np.cos(base), np.sin(base), np.cos(step), np.sin(step))]


def pack_body(gateup, downT, query, outputT, keyval, out, row):
    for m in range(3):
        row[:, pl.ds(0, FFT)] = gateup[m] if m < 2 else downT[...]
        row[:, pl.ds(FFT, FFP - FFT)] = jnp.zeros((ROWS, FFP - FFT), F32)
        for c in range(2):
            for x in range(4):
                out[8 * m + 2 * x + c] = row[:, pl.ds(HALF * c + BLK * x, BLK)].astype(BF)
    for x, half in enumerate((128, 128, 32, 32)):
        piece = (query[...], outputT[...], keyval[0], keyval[1])[x]
        row[:, pl.ds(0, 2 * half)] = piece
        for c in range(2):
            here = row[:, pl.ds(half * c, half)]
            out[24 + 2 * x + c, :, pl.ds(0, half)] = here.astype(BF)
            out[24 + 2 * x + c, :, pl.ds(half, BLK - half)] = jnp.zeros((ROWS, BLK - half), BF)


def to_columns(*args):
    vmem = pl.BlockSpec(memory_space=pltpu.VMEM)
    return pl.pallas_call(
        pack_body,
        out_shape=jax.ShapeDtypeStruct((32, ROWS, BLK), BF),
        in_specs=[vmem] * 5,
        out_specs=vmem,
        scratch_shapes=[pltpu.VMEM((ROWS, FFP), F32)],
        compiler_params=pltpu.CompilerParams(vmem_limit_bytes=32 * 1024 * 1024),
    )(*args)


def finish_body(*refs):
    o_got, w_got = refs[:2]
    weights, moms = refs[2:7], refs[7:12]
    new, nxt = refs[12:17], refs[17:22]
    row_o, row_w = refs[22:]

    def step(columns):
        return 0.15 * 0.2 * math.sqrt(max(D, columns))

    def update(i, m, width, columns):
        at = (m,) if m is not None else ()
        o, g = row_o[:, pl.ds(0, width)], row_w[:, pl.ds(0, width)]
        new[i][at + (slice(None), slice(None))] = weights[i][at + (slice(None), slice(None))] - step(columns) * o
        nxt[i][at + (slice(None), slice(None))] = 0.95 * moms[i][at + (slice(None), slice(None))] + g

    for m in range(3):
        for c in range(2):
            for x in range(4):
                here = pl.ds(HALF * c + BLK * x, BLK)
                row_o[:, here] = o_got[8 * m + 2 * x + c].astype(F32)
                row_w[:, here] = w_got[8 * m + 2 * x + c, :, pl.ds(0, BLK)].astype(F32)
        update(0 if m < 2 else 1, m if m < 2 else None, FFT, 6912)
    for x, half in enumerate((128, 128, 32, 32)):
        for c in range(2):
            here = pl.ds(half * c, half)
            row_o[:, here] = o_got[24 + 2 * x + c, :, pl.ds(0, half)].astype(F32)
            row_w[:, here] = w_got[24 + 2 * x + c, :, pl.ds(0, half)].astype(F32)
        update((2, 3, 4, 4)[x], (None, None, 0, 1)[x], 2 * half, 1024 if x < 2 else 256)


def finish(o_got, w_got, weights, moms):
    vmem = pl.BlockSpec(memory_space=pltpu.VMEM)
    out = pl.pallas_call(
        finish_body,
        out_shape=[jax.ShapeDtypeStruct(w.shape, F32) for w in weights] * 2,
        in_specs=[vmem] * 12,
        out_specs=[vmem] * 10,
        scratch_shapes=[pltpu.VMEM((ROWS, FFP), F32)] * 2,
        compiler_params=pltpu.CompilerParams(vmem_limit_bytes=32 * 1024 * 1024),
    )(o_got, w_got, *weights, *moms)
    return out[:5], out[5:]


def block_row(i, j):
    return 128 * (j * (j + 1) // 2 + i)


def chain_body(side, side_in, gram, mom, x, side_out, a, r, t, side_send, side_recv):
    me = place()
    places = side.places(me)
    barrier = greet_all(places)
    pl.semaphore_wait(barrier, len(places))
    side.start(me, side_in, side_out, side_send, side_recv)
    eye = lax.broadcasted_iota(jnp.int32, (128, 128), 0) == lax.broadcasted_iota(jnp.int32, (128, 128), 1)
    total = jnp.zeros((128, 128), F32)
    for i in range(D // 128):
        total = total + jnp.where(eye, gram[pl.ds(block_row(i, i), 128), :].astype(F32), 0.0)
    diag = jnp.sum(jnp.sum(total, axis=1, keepdims=True), axis=0, keepdims=True)
    inv = 1.0 / (jnp.sqrt(diag) + 1e-07)
    step = 384

    def by_rows(fn):
        def body(i, carry):
            fn(pl.ds(pl.multiple_of(i * step, step), step))
            return carry

        lax.fori_loop(0, D // step, body, 0)

    def poly(rows):
        low = a[rows, :]
        r[rows, :] = (COEF_TWO * low.astype(F32) + COEF_THREE * dot(low, a[...], NN)).astype(BF)

    def once(rows):
        low = a[rows, :]
        t[rows, :] = (COEF_ONE * low.astype(F32) + dot(low, r[...], NN)).astype(BF)

    def twice(rows):
        low = t[rows, :]
        a[rows, :] = (COEF_ONE * low.astype(F32) + dot(low, r[...], NN)).astype(BF)

    for j in range(D // 128):
        for i in range(j + 1):
            block = gram[pl.ds(block_row(i, j), 128), :].astype(F32) * (inv * inv)
            a[pl.ds(128 * i, 128), pl.ds(128 * j, 128)] = block.astype(BF)
            if i < j:
                a[pl.ds(128 * j, 128), pl.ds(128 * i, 128)] = block.T.astype(BF)
    x[...] = mom[...] * inv
    for i in range(3):
        by_rows(poly)
        x[...] = COEF_ONE * x[...] + dot(x[...].astype(BF), r[...], NN)
        if i < 2:
            by_rows(once)
            by_rows(twice)
    side.finish()


def orthogonal(gram, columns, side_in, cid):
    side = SideSwap()
    vmem = pl.BlockSpec(memory_space=pltpu.VMEM)
    hbm = pl.BlockSpec(memory_space=pl.ANY)
    return pl.pallas_call(
        functools.partial(chain_body, side),
        out_shape=[jax.ShapeDtypeStruct(columns.shape, F32), side.shape(side_in)],
        in_specs=[hbm, vmem, vmem],
        out_specs=[vmem, hbm],
        scratch_shapes=[pltpu.VMEM((D, D), BF)] * 3 + [pltpu.SemaphoreType.DMA((side.sems,))] * 2,
        compiler_params=pltpu.CompilerParams(
            collective_id=cid, has_side_effects=True, vmem_limit_bytes=48 * 1024 * 1024
        ),
    )(side_in, gram, columns)


def local(
    hidden_in,
    out_grad,
    segment_ids,
    w_query,
    w_keyval,
    w_output,
    w_gateup,
    w_down,
    norm_gains,
    qk_gains,
    mom_query,
    mom_keyval,
    mom_output,
    mom_gateup,
    mom_down,
    gain_moms,
    qk_moms,
):
    dp = lax.axis_index("dp")
    y = lax.axis_index("tensor")
    z, x, c = dp // 8, (dp // 2) % 4, dp % 2

    ffn_w = jnp.concatenate([w_gateup, w_down.T[None]], axis=0).astype(BF)
    ffn_w = jnp.pad(ffn_w, ((0, 0), (0, 0), (0, FFP - FFT))).reshape(3, ROWS, 2, HALF).transpose(2, 0, 1, 3)
    ffn_w = jnp.pad(ffn_w.reshape(2, 3 * ROWS, HALF), ((0, 0), (0, 4), (0, 0)))
    mom_downT, mom_outputT = mom_down.T, mom_output.T
    moms = to_columns(mom_gateup, mom_downT, mom_query, mom_outputT, mom_keyval)

    segs = jnp.pad(segment_ids.astype(F32).reshape(4, 64), ((0, ROWS - 4), (0, 0)))
    attn_w = jnp.stack(
        [
            jnp.concatenate([w_query, w_keyval[0], w_keyval[1]], axis=1),
            jnp.concatenate(
                [
                    w_output.T,
                    norm_gains.T,
                    jnp.broadcast_to(qk_gains.reshape(1, 4), (ROWS, 4)),
                    segs,
                    jnp.zeros((ROWS, 56), F32),
                ],
                axis=1,
            ),
        ]
    ).astype(BF)
    attn_w = jnp.pad(attn_w, ((0, 0), (0, 12), (0, 0)))
    attn_got = gather_plane(attn_w, 1)
    w_qkv, woT, gains, normed, q_raw, kv_piece = project(attn_got, hidden_in)
    g0, g1, g2, g3 = (gains[i : i + 1] for i in range(4))
    small = attn_got[:, :, :, 1, :4, 256:384].transpose(1, 2, 0, 3, 4).reshape(32, 4, 128)
    qk_mine = jnp.pad(small[:, 0, 4:8].reshape(32, 2, 2).transpose(1, 0, 2).reshape(2, 64), ((0, 14), (0, 64)))
    segs_all = small[:, :, 8:72].reshape(32, TOK).astype(jnp.int32)

    cos_b, sin_b, cos_s, sin_s = (jnp.asarray(t) for t in rope_tables())
    cb = lax.dynamic_slice_in_dim(cos_b, dp, 1, 0)
    sb = lax.dynamic_slice_in_dim(sin_b, dp, 1, 0)
    cosine = cb * cos_s - sb * sin_s
    sine = sb * cos_s + cb * sin_s

    kv_all, qk_all, ffn_near = halo([(kv_piece, "all"), (qk_mine, "near")], 1, 2, SideNear(), ffn_w)
    qk_full = qk_all[:, :2, :64].reshape(4, 2, 32, 2).transpose(1, 2, 0, 3).reshape(2, HD).astype(F32)
    gq, gk = qk_full[0:1], qk_full[1:2]
    order = np.arange(512)
    sort = np.zeros((512, 512), np.float32)
    sort[(order % 256) // 64 * 128 + order // 256 * 64 + order % 64, order] = 1.0
    first = jnp.maximum(dp - 2, 0)
    seg_rows = lax.dynamic_slice_in_dim(segs_all, first, 3, 0)
    seg_keys = jnp.where(
        dp >= 2, seg_rows, jnp.where(dp == 1, jnp.roll(seg_rows, 1, axis=0), jnp.roll(seg_rows, 2, axis=0))
    ).reshape(3 * TOK)
    seg_keys = jnp.where(jnp.arange(3 * TOK) >= (2 - dp) * TOK, seg_keys, -1)
    qr, kr, vb, k_own, probs, ob, u_part = attention(
        kv_all, jnp.asarray(sort, BF), q_raw, gq, gk, cosine, sine, segment_ids[:, None], seg_keys[None, :], woT
    )
    u_part = u_part.reshape(4, QTOK, D)
    hidden_q = lax.dynamic_slice_in_dim(hidden_in, y * QTOK, QTOK, 0)
    grad_q = lax.dynamic_slice_in_dim(out_grad, y * QTOK, QTOK, 0)
    u, hmid, bin_all, ffn_all = sum_then_gather(
        mid_fn, u_part, [hidden_q, g1, g2], [(QTOK, D)] * 2, 1, True, 3, SideGather(), ffn_near
    )

    bin_low = bin_all.reshape(512, D)
    dense, gate, up, mixed, f_part = ffn_forward(ffn_all.reshape(32, 112, HALF), bin_low)
    f_part = f_part.reshape(2, 4, QTOK, D)
    block, dg3, df_all, moms_all = sum_then_gather(
        ffn_out_fn, f_part, [hmid, grad_q, g3], [(QTOK, D), (1, D)], 1, True, 5, SideSwap(), moms
    )
    moms_cols = moms_all.reshape(D, BLK).T
    dfb = df_all.reshape(512, D)
    dgate, dup, dbin_part = ffn_backward(dfb, gate, up, dense)
    dbin_part = dbin_part.reshape(2, 4, QTOK, D)
    dhmid, dg1, dg2, du_all = sum_then_gather(
        ffn_in_fn,
        dbin_part,
        [hmid, u, grad_q, g1, g2],
        [(QTOK, D), (1, D), (1, D)],
        1,
        True,
        6,
    )

    dub_all = du_all.reshape(512, D)
    dkv_all, a_all, ob_all, dq_all, dgq, dgk = attention_back(
        7, dub_all, woT, vb, probs, kr, qr, q_raw, gq, gk, cosine, sine, k_own, normed, ob
    )
    dqb = lax.dynamic_slice_in_dim(dq_all, c, 1, 0)[0]
    dkv_all = dkv_all.reshape(512, 512)
    a_all, ob_all, dq_all = a_all.reshape(512, D), ob_all.reshape(512, HD), dq_all.reshape(512, HD)
    src, col = jnp.arange(512)[:, None], jnp.arange(128)[None, :]
    pick_y = (src == col // 64 * 256 + y * 64 + col % 64).astype(BF)
    col = col[:, :64]
    pick_c = (src == col // 32 * 256 + y * 64 + c * 32 + col % 32).astype(BF)
    dkv_mine = lax.dynamic_slice_in_dim(dkv_all, c * TOK, TOK, 0)
    dkv_y = dot(dkv_mine, pick_y, NN).astype(BF)
    dkv_cols = dot(dkv_all, pick_c, NN).astype(BF)
    da_part = (
        dot(
            jnp.concatenate([dqb, dkv_y], axis=1),
            w_qkv,
            NT,
        )
        .astype(BF)
        .reshape(4, QTOK, D)
    )
    dg0, last_in, last_out = sum_then_gather(
        last_fn, da_part, [hidden_q, dhmid, block, g0], [(1, D)], 2, False, 10
    )
    input_grad = last_in.reshape(TOK, D).astype(F32)
    block_out = last_out.reshape(TOK, D).astype(F32)

    gain_rows = jnp.concatenate(
        [dg0, dg1, dg2, dg3, jnp.concatenate([dgq, dgk, jnp.zeros((1, D - 2 * HD), F32)], axis=1)], axis=0
    ).astype(BF)

    ob_cols = lax.dynamic_slice_in_dim(ob_all, c * 128, 128, 1)
    dq_cols = lax.dynamic_slice_in_dim(dq_all, c * 128, 128, 1)
    d_gate = dot(dgate, bin_low, TN).astype(BF)
    d_up = dot(dup, bin_low, TN).astype(BF)
    d_down = dot(mixed, dfb, TN).astype(BF)
    d_q = dot(dq_cols, a_all, TN).astype(BF)
    d_kv = dot(dkv_cols, a_all, TN).astype(BF)
    d_o = dot(ob_cols, dub_all, TN).astype(BF)
    small = jnp.stack(
        [
            jnp.pad(d_q, ((0, BLK - 128), (0, 0))),
            jnp.pad(d_o, ((0, BLK - 128), (0, 0))),
            jnp.pad(d_kv[:32], ((0, BLK - 32), (0, 0))),
            jnp.concatenate([d_kv[32:], gain_rows, jnp.zeros((BLK - 37, D), BF)], axis=0),
        ]
    )
    wgrad = reduce_plane([d_gate.reshape(4, BLK, D), d_up.reshape(4, BLK, D), d_down.reshape(4, BLK, D), small], 11)

    kept = jnp.where((z == 3) & (x == 3), 32, BLK).reshape(1, 1)
    gram, gains_got, mom = gram_sum(kept, moms_cols, wgrad, wgrad[32:48].astype(BF), 13)
    gain_sum = jnp.sum(gains_got[:, :5].astype(F32), axis=0)
    gain_cols = jnp.concatenate(
        [
            gain_sum[:4].T.reshape(32, ROWS, 4),
            jnp.pad(
                gain_sum[4, : 2 * HD].reshape(2, 32, 4, 2)[:, :, y].transpose(1, 0, 2).reshape(32, 1, 4),
                ((0, 0), (0, ROWS - 1), (0, 0)),
            ),
        ],
        axis=2,
    )
    w_back = jnp.concatenate(
        [wgrad.astype(BF).T.reshape(32, ROWS, BLK), gain_cols.astype(BF), jnp.zeros((32, ROWS, 24), BF)], axis=2
    )
    ortho, w_got = orthogonal(gram.reshape(32 * PART, 128), mom, w_back, 12)
    gains_red = w_got[30, :, 224:228].T.astype(F32)
    qk_red = w_got[30, 0, 228:232].reshape(2, 2).astype(F32)
    o_back = ortho.astype(BF).T.reshape(32, ROWS, BLK)
    (o_got,) = exchange([(o_back, "a2a")], ("z", "x", "c"), 14)
    gain_rate = 2.0 / math.sqrt(8192)
    next_gain_moms = 0.9 * gain_moms + 0.1 * gains_red
    new_norm_gains = norm_gains - gain_rate * next_gain_moms
    next_qk_moms = 0.9 * qk_moms + 0.1 * qk_red
    new_qk_gains = qk_gains - gain_rate * next_qk_moms

    new, nxt = finish(
        o_got,
        w_got,
        [w_gateup, w_down.T, w_query, w_output.T, w_keyval],
        [mom_gateup, mom_downT, mom_query, mom_outputT, mom_keyval],
    )
    new_gateup, new_downT, new_query, new_outputT, new_keyval = new
    next_gateup, next_downT, next_query, next_outputT, next_keyval = nxt
    new_down, new_output, next_down, next_output = new_downT.T, new_outputT.T, next_downT.T, next_outputT.T
    return (
        block_out,
        input_grad,
        new_query,
        new_keyval,
        new_output,
        new_gateup,
        new_down,
        next_query,
        next_keyval,
        next_output,
        next_gateup,
        next_down,
        new_norm_gains,
        next_gain_moms,
        new_qk_gains,
        next_qk_moms,
    )


def solution(mesh):
    return jax.shard_map(
        local,
        mesh=mesh,
        in_specs=(
            P("dp", None),
            P("dp", None),
            P("dp"),
            P("dp", "tensor"),
            P(None, "dp", "tensor"),
            P("tensor", "dp"),
            P(None, "dp", "tensor"),
            P("tensor", "dp"),
            P(None, "dp"),
            P(None, ("dp", "tensor")),
            P("dp", "tensor"),
            P(None, "dp", "tensor"),
            P("tensor", "dp"),
            P(None, "dp", "tensor"),
            P("tensor", "dp"),
            P(None, "dp"),
            P(None, ("dp", "tensor")),
        ),
        out_specs=(
            P("dp", None),
            P("dp", None),
            P("dp", "tensor"),
            P(None, "dp", "tensor"),
            P("tensor", "dp"),
            P(None, "dp", "tensor"),
            P("tensor", "dp"),
            P("dp", "tensor"),
            P(None, "dp", "tensor"),
            P("tensor", "dp"),
            P(None, "dp", "tensor"),
            P("tensor", "dp"),
            P(None, "dp"),
            P(None, "dp"),
            P(None, ("dp", "tensor")),
            P(None, ("dp", "tensor")),
        ),
        check_vma=False,
    )
```

```python
import functools
import math

import jax
import jax.numpy as jnp
import numpy as np
from jax import lax
from jax.experimental import pallas as pl
from jax.experimental.pallas import tpu as pltpu
from jax.sharding import PartitionSpec as P

WINDOW = 512
EPSILON = 1e-06
COEF_ONE = 3.4445
COEF_TWO = -4.775
COEF_THREE = 2.0315

D = 1152
HD = 256
TOK = 256
QTOK = 64
ROWS = 36
FFT = 1728
FFP = 1792
HALF = 896
BLK = 224
PART = 192
BF = jnp.bfloat16
F32 = jnp.float32
MESH = pl.DeviceIdType.MESH

SIZES = {"z": 4, "x": 4, "c": 2, "y": 4}


def place():
    dp = lax.axis_index("dp")
    return {"z": dp // 8, "x": (dp // 2) % 4, "c": dp % 2, "y": lax.axis_index("tensor")}


def rank(at, axes):
    r = 0
    for a in axes:
        r = r * SIZES[a] + at[a]
    return r


def count(axes):
    return math.prod(SIZES[a] for a in axes)


def decode(p, axes):
    out = {}
    for a in reversed(axes):
        out[a] = p % SIZES[a]
        p = p // SIZES[a]
    return out


def moved(at, off, sign):
    return {a: (at[a] + (off[a] if sign > 0 else SIZES[a] - off[a])) % SIZES[a] if a in off else at[a] for a in at}


def device(at):
    return {"dp": at["z"] * 8 + at["x"] * 2 + at["c"], "tensor": at["y"]}


def slot(ref, mode, axes, target):
    if mode == "ag":
        return ref
    if mode == "a2a":
        return ref.at[rank(target, axes)]
    return ref.at[rank(target, mode[1])]


def exchange_body(axes, modes, subs, *refs):
    k = len(modes)
    n = count(axes)
    ins, outs = refs[:k], refs[k : 2 * k]
    send_sem, recv_sem, local_sem = refs[2 * k :]
    me = place()
    barrier = pltpu.get_barrier_semaphore()

    def greet(p, carry):
        pl.semaphore_signal(barrier, inc=1, device_id=device(moved(me, decode(p, axes), -1)), device_id_type=MESH)
        return carry

    def copies(p, arriving, items):
        off = decode(p, axes)
        target = moved(me, off, 1)
        place_of = moved(me, off, -1) if arriving else me
        return [
            pltpu.make_async_remote_copy(
                src_ref=slot(ins[i], modes[i], axes, target),
                dst_ref=outs[i].at[rank(place_of, subs[i])],
                send_sem=send_sem.at[i, p],
                recv_sem=recv_sem.at[i, p],
                device_id=device(target),
                device_id_type=MESH,
            )
            for i in items
        ]

    own = [
        pltpu.make_async_copy(slot(ins[i], modes[i], axes, me), outs[i].at[rank(me, subs[i])], local_sem.at[i])
        for i in range(k)
    ]
    lax.fori_loop(1, n, greet, 0)
    for copy in own:
        copy.start()
    pl.semaphore_wait(barrier, n - 1)
    if all(s == axes for s in subs):

        def launch(p, carry):
            for copy in copies(p, False, range(k)):
                copy.start()
            return carry

        def finish(p, carry):
            for copy in copies(p, True, range(k)):
                copy.wait()
            return carry

        lax.fori_loop(1, n, launch, 0)
        for copy in own:
            copy.wait()
        lax.fori_loop(1, n, finish, 0)
        return
    items = []
    for p in range(1, n):
        off = decode(p, axes)
        items.append((p, [i for i in range(k) if all(off[ax] == 0 for ax in axes if ax not in subs[i])]))
    for p, mine in items:
        for copy in copies(p, False, mine):
            copy.start()
    for copy in own:
        copy.wait()
    for p, mine in items:
        for copy in copies(p, True, mine):
            copy.wait()


def exchange(items, axes, cid):
    arrays = [i[0] for i in items]
    modes = [i[1] for i in items]
    subs = [i[2] if len(i) > 2 else axes for i in items]
    shapes = [
        (count(sub),) + (a.shape if m == "ag" else a.shape[1:]) for a, m, sub in zip(arrays, modes, subs)
    ]
    k, n = len(items), count(axes)
    vmem = pl.BlockSpec(memory_space=pltpu.VMEM)
    return pl.pallas_call(
        functools.partial(exchange_body, axes, modes, subs),
        out_shape=[jax.ShapeDtypeStruct(s, a.dtype) for s, a in zip(shapes, arrays)],
        in_specs=[vmem] * k,
        out_specs=[vmem] * k,
        scratch_shapes=[
            pltpu.SemaphoreType.DMA((k, n)),
            pltpu.SemaphoreType.DMA((k, n)),
            pltpu.SemaphoreType.DMA((k,)),
        ],
        compiler_params=pltpu.CompilerParams(
            collective_id=cid, has_side_effects=True, vmem_limit_bytes=32 * 1024 * 1024
        ),
    )(*arrays)


def virtual(me, p, q):
    c = me["c"]
    first = {"a": jnp.where(c == 0, me[p], me[q]), "b": jnp.where(c == 0, me[q], me[p])}

    def to(av, bv):
        return {**me, p: jnp.where(c == 0, av, bv), q: jnp.where(c == 0, bv, av)}

    return first["a"], first["b"], to


def remote(src, dst, send_sem, recv_sem, at):
    return pltpu.make_async_remote_copy(
        src_ref=src, dst_ref=dst, send_sem=send_sem, recv_sem=recv_sem, device_id=device(at), device_id_type=MESH
    )


def greet_all(places):
    barrier = pltpu.get_barrier_semaphore()
    for at in places:
        pl.semaphore_signal(barrier, inc=1, device_id=device(at), device_id_type=MESH)
    return barrier


def gather_body(block, out, send_sem, recv_sem, local_sem):
    me = place()
    a, b, to = virtual(me, "z", "x")
    twin = {**me, "c": 1 - me["c"]}
    a_next, a_last, a_far = (a + 1) % 4, (a + 3) % 4, (a + 2) % 4
    b_next, b_last = (b + 1) % 4, (b + 3) % 4
    barrier = greet_all([to(a_next, b), to(a_last, b), to(a, b_next), to(a, b_last), to(a_far, b), twin])

    def spot(av, bv):
        at = to(av, bv)
        return out.at[me["c"], at["z"], at["x"]]

    here = spot(a, b)
    own = pltpu.make_async_copy(block, here, local_sem.at[0])
    own.start()
    pl.semaphore_wait(barrier, 6)

    def sent(src, dst_here, sem, at):
        remote(src, src, send_sem.at[sem], recv_sem.at[sem], at).start()
        return remote(src, dst_here, send_sem.at[sem], recv_sem.at[sem], at)

    own.wait()
    up, down = to(a_next, b), to(a_last, b)
    first = [
        sent(here, spot(a_last, b), 1, up),
        sent(here, spot(a_next, b), 2, down),
        sent(here, spot(a_far, b), 3, to(a_far, b)),
    ]
    for w in first:
        w.wait()
    up2, down2 = to(a, b_next), to(a, b_last)
    waits = [
        (sent(spot(i, b), spot(i, b_last), 5 + 2 * i, up2), sent(spot(i, b), spot(i, b_next), 6 + 2 * i, down2))
        for i in range(4)
    ]
    late = []
    for i in range(4):
        w_last, w_next = waits[i]
        far = spot(i, (b + 2) % 4)
        if i < 2:
            w_last.wait()
            late += [sent(spot(i, b_last), far, 13 + i, up2), w_next]
        else:
            w_next.wait()
            late += [sent(spot(i, b_next), far, 13 + i, down2), w_last]
    for w in late:
        w.wait()
    remote(out.at[me["c"]], out.at[me["c"]], send_sem.at[0], recv_sem.at[0], twin).start()
    remote(out.at[me["c"]], out.at[1 - me["c"]], send_sem.at[0], recv_sem.at[0], twin).wait()


def gather_plane(block, cid):
    vmem = pl.BlockSpec(memory_space=pltpu.VMEM)
    return pl.pallas_call(
        gather_body,
        out_shape=jax.ShapeDtypeStruct((2, 4, 4) + block.shape, block.dtype),
        in_specs=[vmem],
        out_specs=vmem,
        scratch_shapes=[
            pltpu.SemaphoreType.DMA((17,)),
            pltpu.SemaphoreType.DMA((17,)),
            pltpu.SemaphoreType.DMA((1,)),
        ],
        compiler_params=pltpu.CompilerParams(
            collective_id=cid, has_side_effects=True, vmem_limit_bytes=32 * 1024 * 1024
        ),
    )(block)


class SideNear:
    sems = 7

    def shape(self, ffn):
        return jax.ShapeDtypeStruct((4, 2) + ffn.shape[1:], ffn.dtype)

    def places(self, me):
        a, b, to = virtual(me, "z", "x")
        return [to((a + 1) % 4, b), to((a + 3) % 4, b), {**me, "c": 1 - me["c"]}]

    def start(self, me, ffn, near, send_sem, recv_sem):
        a, b, to = virtual(me, "z", "x")
        c = me["c"]
        twin = {**me, "c": 1 - c}
        a_next, a_last, a_far = (a + 1) % 4, (a + 3) % 4, (a + 2) % 4
        up, down = to(a_next, b), to(a_last, b)

        def sent(src, dst_here, sem, at):
            remote(src, src, send_sem.at[sem], recv_sem.at[sem], at).start()
            return remote(src, dst_here, send_sem.at[sem], recv_sem.at[sem], at)

        keep = pltpu.make_async_copy(ffn.at[c], near.at[a, c], recv_sem.at[1])
        keep.start()
        remote(ffn.at[1 - c], near.at[b, c], send_sem.at[0], recv_sem.at[0], twin).start()
        keep.wait()
        remote(ffn.at[1 - c], near.at[a, 1 - c], send_sem.at[0], recv_sem.at[0], twin).wait()
        first = [sent(near.at[a], near.at[a_last], 2, up), sent(near.at[a], near.at[a_next], 3, down)]

        def middle():
            for w in first:
                w.wait()
            self.late = [
                sent(near.at[a_last, 0], near.at[a_far, 0], 4, up),
                sent(near.at[a_next, 1], near.at[a_far, 1], 5, down),
            ]

        self.middle = middle

    def finish(self):
        for w in self.late:
            w.wait()


class SideGather:
    sems = 16

    def shape(self, near):
        return jax.ShapeDtypeStruct((4, 4) + near.shape[1:], near.dtype)

    def places(self, me):
        a, b, to = virtual(me, "z", "x")
        return [to(a, (b + 1) % 4), to(a, (b + 3) % 4)]

    def start(self, me, near, out, send_sem, recv_sem):
        a, b, to = virtual(me, "z", "x")
        b_next, b_last = (b + 1) % 4, (b + 3) % 4
        up, down = to(a, b_next), to(a, b_last)

        def spot(av, bv):
            at = to(av, bv)
            return out.at[at["z"], at["x"]]

        def sent(src, dst, dst_here, sem, at):
            remote(src, dst, send_sem.at[sem], recv_sem.at[sem], at).start()
            return remote(src, dst_here, send_sem.at[sem], recv_sem.at[sem], at)

        self.waits = []
        for i in range(4):
            self.waits.append(
                (
                    sent(near.at[i], spot(i, b), spot(i, b_last), 2 * i, up),
                    sent(near.at[i], spot(i, b), spot(i, b_next), 2 * i + 1, down),
                )
            )
        self.late = []
        for i in range(4):
            copy = pltpu.make_async_copy(near.at[i], spot(i, b), recv_sem.at[12 + i])
            copy.start()
            self.late.append(copy)

        def middle():
            for i in range(4):
                w_last, w_next = self.waits[i]
                far = spot(i, (b + 2) % 4)
                if i < 2:
                    w_last.wait()
                    src = spot(i, b_last)
                    self.late += [sent(src, src, far, 8 + i, up), w_next]
                else:
                    w_next.wait()
                    src = spot(i, b_next)
                    self.late += [sent(src, src, far, 8 + i, down), w_last]

        self.middle = middle

    def finish(self):
        for w in self.late:
            w.wait()


class SideSwap:
    sems = 33
    axes = ("z", "x", "c")

    def shape(self, parts):
        return jax.ShapeDtypeStruct(parts.shape, parts.dtype)

    def places(self, me):
        return [moved(me, decode(p, self.axes), -1) for p in range(1, 32)]

    def start(self, me, parts, out, send_sem, recv_sem):
        def copies(p, arriving):
            off = decode(p, self.axes)
            target = moved(me, off, 1)
            spot = moved(me, off, -1) if arriving else me
            return remote(
                parts.at[rank(target, self.axes)],
                out.at[rank(spot, self.axes)],
                send_sem.at[p],
                recv_sem.at[p],
                target,
            )

        def launch(p, carry):
            copies(p, False).start()
            return carry

        def finish(p, carry):
            copies(p, True).wait()
            return carry

        lax.fori_loop(1, 32, launch, 0)
        mine = rank(me, self.axes)
        copy = pltpu.make_async_copy(parts.at[mine], out.at[mine], recv_sem.at[32])
        copy.start()
        copy.wait()
        self.finish = lambda: lax.fori_loop(1, 32, finish, 0)
        self.middle = lambda: None


def reduce_body(by0, by1, by2, by3, total, p, r1, r2, q, r3, r4, send_sem, recv_sem, local_sem):
    me = place()
    a, b, to = virtual(me, "z", "x")
    a_next, a_last, a_far = (a + 1) % 4, (a + 3) % 4, (a + 2) % 4
    b_next, b_last, b_far = (b + 1) % 4, (b + 3) % 4, (b + 2) % 4
    up, down = to(a_next, b), to(a_last, b)
    up2, down2 = to(a, b_next), to(a, b_last)
    barrier = greet_all([up, down, up2, down2])

    def at(ref, av, bv):
        w = to(av, bv)
        return ref.at[w["z"], w["x"]]

    loads = [pltpu.make_async_copy(by, p.at[i], local_sem.at[i]) for i, by in enumerate((by0, by1, by2, by3))]
    for load in loads:
        load.start()
    pl.semaphore_wait(barrier, 4)
    for load in loads:
        load.wait()
    first = []
    for i in range(4):
        first.append(remote(at(p, a_far, i), r1.at[i], send_sem.at[i], recv_sem.at[i], up if i < 2 else down))
        first[-1].start()
    second = []

    def onward(i, way, src):
        sem = 4 + 2 * i + way
        copy = remote(src, r2.at[way, i], send_sem.at[sem], recv_sem.at[sem], down if way else up)
        copy.start()
        second.append(copy)

    for i in range(4):
        onward(i, 1 if i < 2 else 0, at(p, a_last if i < 2 else a_next, i))
    for i in range(4):
        first[i].wait()
        dest = at(p, a_next if i < 2 else a_last, i)
        dest[...] = (dest[...].astype(F32) + r1[i].astype(F32)).astype(BF)
        onward(i, 0 if i < 2 else 1, dest)
    for copy in second:
        copy.wait()
    for i in range(4):
        q[i] = (at(p, a, i)[...].astype(F32) + r2[0, i].astype(F32) + r2[1, i].astype(F32)).astype(BF)
    lo, hi = pl.ds(0, BLK // 2), pl.ds(BLK // 2, BLK // 2)
    one = remote(q.at[b_far, lo], r3.at[0], send_sem.at[12], recv_sem.at[12], up2)
    two = remote(q.at[b_far, hi], r3.at[1], send_sem.at[13], recv_sem.at[13], down2)
    one.start()
    two.start()
    three = remote(q.at[b_next, hi], r4.at[0, hi], send_sem.at[14], recv_sem.at[14], up2)
    four = remote(q.at[b_last, lo], r4.at[1, lo], send_sem.at[15], recv_sem.at[15], down2)
    three.start()
    four.start()
    one.wait()
    dest = q.at[b_next, lo]
    dest[...] = (dest[...].astype(F32) + r3[0].astype(F32)).astype(BF)
    five = remote(q.at[b_next, lo], r4.at[0, lo], send_sem.at[16], recv_sem.at[16], up2)
    five.start()
    two.wait()
    dest = q.at[b_last, hi]
    dest[...] = (dest[...].astype(F32) + r3[1].astype(F32)).astype(BF)
    six = remote(q.at[b_last, hi], r4.at[1, hi], send_sem.at[17], recv_sem.at[17], down2)
    six.start()
    for copy in (three, four, five, six):
        copy.wait()
    total[...] = q[b].astype(F32) + r4[0].astype(F32) + r4[1].astype(F32)


def reduce_plane(parts, cid):
    block = parts[0].shape[1:]
    return pl.pallas_call(
        reduce_body,
        out_shape=jax.ShapeDtypeStruct(block, F32),
        in_specs=[pl.BlockSpec(memory_space=pl.ANY)] * 4,
        out_specs=pl.BlockSpec(memory_space=pltpu.VMEM),
        scratch_shapes=[
            pltpu.VMEM((4, 4) + block, BF),
            pltpu.VMEM((4,) + block, BF),
            pltpu.VMEM((2, 4) + block, BF),
            pltpu.VMEM((4,) + block, BF),
            pltpu.VMEM((2, BLK // 2, D), BF),
            pltpu.VMEM((2,) + block, BF),
            pltpu.SemaphoreType.DMA((18,)),
            pltpu.SemaphoreType.DMA((18,)),
            pltpu.SemaphoreType.DMA((4,)),
        ],
        compiler_params=pltpu.CompilerParams(
            collective_id=cid, has_side_effects=True, vmem_limit_bytes=48 * 1024 * 1024
        ),
    )(*parts)


def gram_body(kept, moms, grad, extra, gram, extras, mom, flat, parts, p, got, mine, bx, send_sem, recv_sem, local_sem):
    me = place()
    c, z = me["c"], me["z"]
    axes = ("x", "y")
    twin = {**me, "c": 1 - c}
    barrier = pltpu.get_barrier_semaphore()
    for i in range(1, 16):
        pl.semaphore_signal(barrier, inc=1, device_id=device(moved(me, decode(i, axes), -1)), device_id_type=MESH)
    for i in range(4):
        pl.semaphore_signal(barrier, inc=1, device_id=device({**twin, "y": (me["y"] + i) % 4}), device_id_type=MESH)
    new = 0.95 * moms[...].astype(F32) + grad[...]
    new = jnp.where(lax.broadcasted_iota(jnp.int32, (BLK, 1), 0) < kept[...], new, 0.0)
    mom[...] = new
    flat[...] = new.astype(BF)
    start = 0
    for j in range(D // 128):
        tall = 128 * (j + 1)
        value = dot(flat[:, pl.ds(0, tall)], flat[:, pl.ds(128 * j, 128)], TN).astype(BF)
        while tall:
            part, row = divmod(start, PART)
            size = min(tall, PART - row)
            done = 128 * (j + 1) - tall
            parts[part // 16, part % 16, pl.ds(row, size), :] = value[done : done + size]
            start, tall = start + size, tall - size
    for part in range(start // PART, 32):
        row = start % PART if part == start // PART else 0
        parts[part // 16, part % 16, pl.ds(row, PART - row), :] = jnp.zeros((PART - row, 128), BF)
    load = pltpu.make_async_copy(parts.at[c], p, local_sem.at[0])
    load.start()
    keep = pltpu.make_async_copy(extra, extras.at[rank(me, ("c", "y"))], local_sem.at[1])
    keep.start()
    pl.semaphore_wait(barrier, 19)
    swap = remote(parts.at[1 - c], got, send_sem.at[0, 0], recv_sem.at[0, 0], twin)
    swap.start()
    extra_waits = []
    for i in range(1, 8):
        off = decode(i, ("c", "y"))
        target, source = moved(me, off, 1), moved(me, off, -1)
        sems = (send_sem.at[3, i], recv_sem.at[3, i])
        remote(extra, extras.at[rank(me, ("c", "y"))], *sems, target).start()
        extra_waits.append(remote(extra, extras.at[rank(source, ("c", "y"))], *sems, target))
    load.wait()
    swap.wait()
    for i in range(16):
        p[i] = (p[i].astype(F32) + got[i].astype(F32)).astype(BF)
    waits = []
    for i in range(1, 16):
        off = decode(i, axes)
        target, source = moved(me, off, 1), moved(me, off, -1)
        sems = (send_sem.at[1, i], recv_sem.at[1, i])
        remote(p.at[rank(target, axes)], mine.at[rank(me, axes)], *sems, target).start()
        waits.append(remote(p.at[rank(target, axes)], mine.at[rank(source, axes)], *sems, target))
    own = pltpu.make_async_copy(p.at[rank(me, axes)], mine.at[rank(me, axes)], local_sem.at[0])
    own.start()
    own.wait()
    for w in waits:
        w.wait()
    sums = []
    for i in range(4):
        part = mine[4 * i].astype(F32)
        for j in range(1, 4):
            part = part + mine[4 * i + j].astype(F32)
        sums.append(part)
    whole = sums[0] + sums[1] + sums[2] + sums[3]
    for i in range(4):
        bx[i] = jnp.where(z < 3, whole, sums[i]).astype(BF)
    waits = []
    spot = gram.at[c]
    for i in range(1, 16):
        off = decode(i, axes)
        target, source = moved(me, off, 1), moved(me, off, -1)
        sems = (send_sem.at[2, i], recv_sem.at[2, i])
        remote(bx.at[target["x"]], spot.at[rank(me, axes)], *sems, target).start()
        waits.append(remote(bx.at[target["x"]], spot.at[rank(source, axes)], *sems, target))
    own = pltpu.make_async_copy(bx.at[me["x"]], spot.at[rank(me, axes)], local_sem.at[0])
    own.start()
    own.wait()
    for w in waits:
        w.wait()
    remote(gram.at[c], gram.at[c], send_sem.at[2, 0], recv_sem.at[2, 0], twin).start()
    remote(gram.at[c], gram.at[1 - c], send_sem.at[2, 0], recv_sem.at[2, 0], twin).wait()
    keep.wait()
    for w in extra_waits:
        w.wait()


def gram_sum(kept, moms, grad, extra, cid):
    vmem = pl.BlockSpec(memory_space=pltpu.VMEM)
    half = (16, PART, 128)
    return pl.pallas_call(
        gram_body,
        out_shape=[
            jax.ShapeDtypeStruct((2,) + half, BF),
            jax.ShapeDtypeStruct((8,) + extra.shape, extra.dtype),
            jax.ShapeDtypeStruct(grad.shape, F32),
        ],
        in_specs=[vmem] * 4,
        out_specs=[vmem] * 3,
        scratch_shapes=[
            pltpu.VMEM(moms.shape, BF),
            pltpu.VMEM((2,) + half, BF),
            pltpu.VMEM(half, BF),
            pltpu.VMEM(half, BF),
            pltpu.VMEM(half, BF),
            pltpu.VMEM((4,) + half[1:], BF),
            pltpu.SemaphoreType.DMA((4, 16)),
            pltpu.SemaphoreType.DMA((4, 16)),
            pltpu.SemaphoreType.DMA((2,)),
        ],
        compiler_params=pltpu.CompilerParams(
            collective_id=cid, has_side_effects=True, vmem_limit_bytes=48 * 1024 * 1024
        ),
    )(kept, moms, grad, extra)


def halo_body(sign, kinds, side, *refs):
    k = len(kinds)
    side_in, ins, outs, side_out = refs[0], refs[1 : 1 + k], refs[1 + k : 1 + 2 * k], refs[1 + 2 * k]
    send_sem, recv_sem, local_sem, side_send, side_recv = refs[2 + 2 * k :]
    me = place()
    dp = lax.axis_index("dp")
    y = lax.axis_index("tensor")
    barrier = pltpu.get_barrier_semaphore()
    offs = [(d, t) for d in range(3) for t in range(4)]

    def dev(d, t, way):
        shift = d if way > 0 else 32 - d
        return {"dp": (dp + shift) % 32, "tensor": (y + (t if way > 0 else 4 - t)) % 4}

    for d, t in offs[1:]:
        back = dev(d, t, -1) if sign > 0 else {"dp": (dp + d) % 32, "tensor": (y + 4 - t) % 4}
        pl.semaphore_signal(barrier, inc=1, device_id=back, device_id_type=MESH)
    more = side.places(me)
    greet_all(more)
    own = []
    copies = []
    for i, kind in enumerate(kinds):
        for p, (d, t) in enumerate(offs):
            if kind == "near" and d > 0:
                continue
            ty = (y + t) % 4
            sy = (y + 4 - t) % 4
            src = ins[i].at[pl.ds(pl.multiple_of((2 - d) * TOK + ty * QTOK, QTOK), QTOK)] if kind == "split" else ins[i]
            tdp = (dp + d) % 32 if sign > 0 else (dp + 32 - d) % 32
            if kind == "near":
                to, frm = outs[i].at[y], outs[i].at[sy]
            elif kind == "all":
                rows = pl.ds((2 - d) * TOK, TOK)
                to, frm = (outs[i].at[rows, pl.ds(pl.multiple_of(at * 128, 128), 128)] for at in (y, sy))
            else:
                to, frm = outs[i].at[d, y], outs[i].at[d, sy]
            if p == 0:
                own.append(pltpu.make_async_copy(src, to, local_sem.at[i]))
                continue
            args = dict(send_sem=send_sem.at[i, p], recv_sem=recv_sem.at[i, p], device_id={"dp": tdp, "tensor": ty}, device_id_type=MESH)
            copies.append(
                (
                    pltpu.make_async_remote_copy(src_ref=src, dst_ref=to, **args),
                    pltpu.make_async_remote_copy(src_ref=src, dst_ref=frm, **args),
                )
            )
    for copy in own:
        copy.start()
    pl.semaphore_wait(barrier, len(offs) - 1 + len(more))
    for out_copy, _ in copies:
        out_copy.start()
    side.start(me, side_in, side_out, side_send, side_recv)
    for copy in own:
        copy.wait()
    side.middle()
    for _, in_copy in copies:
        in_copy.wait()
    side.finish()


def halo(items, sign, cid, side, side_in):
    arrays = [a for a, _ in items]
    kinds = [m for _, m in items]
    shapes = []
    for a, m in items:
        shapes.append({"near": (4,) + a.shape, "all": (3 * TOK, 512), "split": (3, 4, QTOK, 512)}[m])
    k = len(items)
    return pl.pallas_call(
        functools.partial(halo_body, sign, kinds, side),
        out_shape=[jax.ShapeDtypeStruct(s, a.dtype) for s, a in zip(shapes, arrays)] + [side.shape(side_in)],
        in_specs=[pl.BlockSpec(memory_space=pl.ANY)] + [pl.BlockSpec(memory_space=pltpu.VMEM)] * k,
        out_specs=[pl.BlockSpec(memory_space=pltpu.VMEM)] * k + [pl.BlockSpec(memory_space=pl.ANY)],
        scratch_shapes=[
            pltpu.SemaphoreType.DMA((k, 12)),
            pltpu.SemaphoreType.DMA((k, 12)),
            pltpu.SemaphoreType.DMA((k,)),
            pltpu.SemaphoreType.DMA((side.sems,)),
            pltpu.SemaphoreType.DMA((side.sems,)),
        ],
        compiler_params=pltpu.CompilerParams(collective_id=cid, has_side_effects=True),
    )(side_in, *arrays)


def sum_body(fn, both, spread, side, n_extra, n_local, n_ag, *refs):
    if side is not None:
        side_in, side_out, side_send, side_recv = refs[0], refs[1 + 1 + n_extra + n_local + n_ag], refs[-2], refs[-1]
        refs = refs[1 : 2 + n_extra + n_local + n_ag] + refs[3 + n_extra + n_local + n_ag : -2]
    parts = refs[0]
    extras = refs[1 : 1 + n_extra]
    locals_ = refs[1 + n_extra : 1 + n_extra + n_local]
    gathers = refs[1 + n_extra + n_local : 1 + n_extra + n_local + n_ag]
    pre, recv, agbuf, send_sem, recv_sem, local_sem = refs[1 + n_extra + n_local + n_ag :]
    me = place()
    c, y = me["c"], me["y"]
    twin = {**me, "c": 1 - c}
    near = [(moved(me, {"y": i}, 1), moved(me, {"y": i}, -1)) for i in range(1, 4)]
    use_twin = both or spread
    places = [source for _, source in near] + ([twin] if use_twin else [])
    if side is not None:
        places += side.places(me)
    barrier = greet_all(places)
    pl.semaphore_wait(barrier, len(places))
    if both:
        swap = remote(parts.at[1 - c], pre, send_sem.at[0], recv_sem.at[0], twin)
        swap.start()
        if side is not None:
            side.start(me, side_in, side_out, side_send, side_recv)
        swap.wait()
        for i in range(4):
            pre[i] = (pre[i].astype(F32) + parts[c, i].astype(F32)).astype(BF)
        mine = pre
    else:
        mine = parts
    waits = []
    for i, (target, source) in enumerate(near):
        sems = (send_sem.at[1 + i], recv_sem.at[1 + i])
        remote(mine.at[target["y"]], recv.at[i], *sems, target).start()
        waits.append(remote(mine.at[target["y"]], recv.at[i], *sems, target))
    if side is not None and not both:
        side.start(me, side_in, side_out, side_send, side_recv)
    total = mine[y].astype(F32)
    for i in range(3):
        waits[i].wait()
        total = total + recv[i].astype(F32)
    local_vals, ag_vals = fn(total, *[e[...] for e in extras])
    for i, value in enumerate(ag_vals):
        agbuf[i] = value.astype(BF)
    waits, own = [], []
    for j in range(n_ag):
        out = gathers[j].at[c] if spread else gathers[j]
        for i, (target, source) in enumerate(near):
            sems = (send_sem.at[4 + 3 * j + i], recv_sem.at[4 + 3 * j + i])
            remote(agbuf.at[j], out.at[y], *sems, target).start()
            waits.append(remote(agbuf.at[j], out.at[source["y"]], *sems, target))
        own.append(pltpu.make_async_copy(agbuf.at[j], out.at[y], local_sem.at[j]))
        own[-1].start()
    for ref, value in zip(locals_, local_vals):
        ref[...] = value
    if side is not None:
        side.middle()
    for copy in own + waits:
        copy.wait()
    if spread:
        for j in range(n_ag):
            g = gathers[j]
            sems = (send_sem.at[4 + 3 * n_ag + j], recv_sem.at[4 + 3 * n_ag + j])
            remote(g.at[c], g.at[c], *sems, twin).start()
            remote(g.at[c], g.at[1 - c], *sems, twin).wait()
    if side is not None:
        side.finish()


def sum_then_gather(fn, parts, extras, local_shapes, n_ag, spread, cid, side=None, side_in=None):
    both = parts.ndim == 4
    rows = parts.shape[-2:]
    vmem = pl.BlockSpec(memory_space=pltpu.VMEM)
    gathered = ((2, 4) if spread else (4,)) + rows
    n_sem = 4 + 4 * n_ag
    hbm = pl.BlockSpec(memory_space=pl.ANY)
    more = side is not None
    return pl.pallas_call(
        functools.partial(sum_body, fn, both, spread, side, len(extras), len(local_shapes), n_ag),
        out_shape=[jax.ShapeDtypeStruct(s, F32) for s in local_shapes]
        + [jax.ShapeDtypeStruct(gathered, BF)] * n_ag
        + ([side.shape(side_in)] if more else []),
        in_specs=[hbm] * more + [vmem] * (1 + len(extras)),
        out_specs=[vmem] * (len(local_shapes) + n_ag) + [hbm] * more,
        scratch_shapes=[
            pltpu.VMEM((4,) + rows, BF),
            pltpu.VMEM((3,) + rows, BF),
            pltpu.VMEM((n_ag,) + rows, BF),
            pltpu.SemaphoreType.DMA((n_sem,)),
            pltpu.SemaphoreType.DMA((n_sem,)),
            pltpu.SemaphoreType.DMA((n_ag,)),
        ]
        + ([pltpu.SemaphoreType.DMA((side.sems,))] * 2 if more else []),
        compiler_params=pltpu.CompilerParams(
            collective_id=cid, has_side_effects=True, vmem_limit_bytes=32 * 1024 * 1024
        ),
    )(*([side_in] if more else []), parts, *extras)


def inv_rms(values):
    return lax.rsqrt(jnp.mean(values * values, axis=-1, keepdims=True) + EPSILON)


def rms_back(values, gain, s, grad):
    scaled = gain * grad
    dv = s * scaled - values * (s * s * s * jnp.mean(scaled * values, axis=-1, keepdims=True))
    return dv, jnp.sum(grad * values * s, axis=0, keepdims=True)


def rot(values, cosine, sine):
    front, back = values[:, :128], values[:, 128:]
    return jnp.concatenate([front * cosine - back * sine, back * cosine + front * sine], axis=-1)


def unrot(values, cosine, sine):
    return rot(values, cosine, -sine)


def mid_fn(u, hidden, g1, g2):
    hmid = hidden + u * inv_rms(u) * g1
    return [u, hmid], [hmid * inv_rms(hmid) * g2]


def ffn_out_fn(f, hmid, out_grad, g3):
    s = inv_rms(f)
    block = hmid + f * s * g3
    df, dg3 = rms_back(f, g3, s, out_grad)
    return [block, dg3], [df]


def ffn_in_fn(dbin, hmid, u, out_grad, g1, g2):
    dm, dg2 = rms_back(hmid, g2, inv_rms(hmid), dbin)
    dhmid = out_grad + dm
    du, dg1 = rms_back(u, g1, inv_rms(u), dhmid)
    return [dhmid, dg1, dg2], [du]


def last_fn(da, hidden, dhmid, block, g0):
    dh, dg0 = rms_back(hidden, g0, inv_rms(hidden), da)
    return [dg0], [dhmid + dh, block]


def dot(a, b, dims):
    return lax.dot_general(a, b, (dims, ((), ())), preferred_element_type=F32)


NN = ((1,), (0,))
NT = ((1,), (1,))
TN = ((0,), (0,))


def ffn_body(blocks, tokens, dense, gate, up, mixed, f):
    for k in range(32):
        for m in range(3):
            dense[m, pl.ds(ROWS * k, ROWS), :] = blocks[k, pl.ds(ROWS * m, ROWS), :]
    inner = math.sqrt(2.0 / math.pi)

    def body(i, carry):
        rows = pl.ds(pl.multiple_of(i * TOK, TOK), TOK)
        low = tokens[rows, :]
        g = dot(low, dense[0], NN)
        gate[rows, :] = g
        u = dot(low, dense[1], NN)
        up[rows, :] = u
        th = jnp.tanh(inner * (g + 0.044715 * g * g * g))
        z = (0.5 * g * (1.0 + th) * u).astype(BF)
        mixed[rows, :] = z
        f[rows, :] = dot(z, dense[2], NT).astype(BF)
        return carry

    lax.fori_loop(0, 2, body, 0)


def ffn_forward(blocks, tokens):
    vmem = pl.BlockSpec(memory_space=pltpu.VMEM)
    return pl.pallas_call(
        ffn_body,
        out_shape=[
            jax.ShapeDtypeStruct((3, D, HALF), BF),
            jax.ShapeDtypeStruct((512, HALF), F32),
            jax.ShapeDtypeStruct((512, HALF), F32),
            jax.ShapeDtypeStruct((512, HALF), BF),
            jax.ShapeDtypeStruct((512, D), BF),
        ],
        in_specs=[vmem] * 2,
        out_specs=[vmem] * 5,
        compiler_params=pltpu.CompilerParams(vmem_limit_bytes=48 * 1024 * 1024),
    )(blocks, tokens)


def project_body(got, hidden, w_qkv, woT, gains, normed, q, kv, tail):
    for k in range(32):
        z, x, c = k // 8, k // 2 % 4, k % 2
        here, rows = pl.ds(ROWS * k, ROWS), pl.ds(0, ROWS)
        w_qkv[here, :] = got[c, z, x, 0, rows, :]
        woT[here, :] = got[c, z, x, 1, rows, pl.ds(0, HD)]
        tail[here, :] = got[c, z, x, 1, rows, pl.ds(HD, 128)]
    turned = tail[...].astype(F32).T
    gains[...] = turned[:8]
    h = hidden[...]
    low = (h * inv_rms(h) * turned[0:1]).astype(BF)
    normed[...] = low
    out = dot(low, w_qkv[...], NN)
    q[...] = out[:, :HD]
    kv[...] = out[:, HD:].astype(BF)


def project(got, hidden):
    vmem = pl.BlockSpec(memory_space=pltpu.VMEM)
    shapes = [((D, 384), BF), ((D, HD), BF), ((8, D), F32), ((TOK, D), BF), ((TOK, HD), F32), ((TOK, 128), BF)]
    return pl.pallas_call(
        project_body,
        out_shape=[jax.ShapeDtypeStruct(s, t) for s, t in shapes],
        in_specs=[vmem] * 2,
        out_specs=[vmem] * len(shapes),
        scratch_shapes=[pltpu.VMEM((D, 128), BF)],
        compiler_params=pltpu.CompilerParams(vmem_limit_bytes=32 * 1024 * 1024),
    )(got, hidden)


def attention_body(kv, sort, q_raw, gq, gk, cosine, sine, seg_q, seg_k, woT, qr, kr, vb, k_own, probs, ob, u):
    sorted_kv = dot(kv[...], sort[...], NN)
    k_raw = sorted_kv[:, :HD]
    v = sorted_kv[:, HD:].astype(BF)
    vb[...] = v
    k_own[...] = k_raw[2 * TOK :]
    k = rot(k_raw * inv_rms(k_raw) * gk[...], cosine[...], sine[...]).astype(BF)
    kr[...] = k
    raw = q_raw[...]
    q = rot(raw * inv_rms(raw) * gq[...], cosine[pl.ds(2 * TOK, TOK), :], sine[pl.ds(2 * TOK, TOK), :]).astype(BF)
    qr[...] = q
    shape = (TOK, 3 * TOK)
    gap = lax.broadcasted_iota(jnp.int32, shape, 0) + 2 * TOK - lax.broadcasted_iota(jnp.int32, shape, 1)
    allowed = (seg_q[...] == seg_k[...]) & (gap >= 0) & (gap < WINDOW)
    scores = jnp.where(allowed, dot(q, k, NT) * (HD**-0.5), -1e30)
    exps = jnp.exp(scores - jnp.max(scores, axis=-1, keepdims=True))
    p = exps / jnp.sum(exps, axis=-1, keepdims=True)
    probs[...] = p
    o = dot(p.astype(BF), v, NN).astype(BF)
    ob[...] = o
    u[...] = dot(o, woT[...], NT).astype(BF)


def attention(*args):
    vmem = pl.BlockSpec(memory_space=pltpu.VMEM)
    wide = 3 * TOK
    shapes = [
        ((TOK, HD), BF),
        ((wide, HD), BF),
        ((wide, HD), BF),
        ((TOK, HD), F32),
        ((TOK, wide), F32),
        ((TOK, HD), BF),
        ((TOK, D), BF),
    ]
    return pl.pallas_call(
        attention_body,
        out_shape=[jax.ShapeDtypeStruct(s, t) for s, t in shapes],
        in_specs=[vmem] * len(args),
        out_specs=[vmem] * len(shapes),
        compiler_params=pltpu.CompilerParams(vmem_limit_bytes=32 * 1024 * 1024),
    )(*args)


def attention_back_body(*refs):
    du_all, woT, vb, probs, kr, qr, q_raw, gq, gk, cosine, sine, k_own, normed, ob = refs[:14]
    dkv_all, a_all, ob_all, dq_all, dgq, dgk = refs[14:20]
    part, got, dkvb, send_sem, recv_sem, local_sem = refs[20:]
    me = place()
    c, y, dp = me["c"], me["y"], lax.axis_index("dp")
    twin = {**me, "c": 1 - c}

    def along(d, t):
        at = (dp + d + 32) % 32
        return {"z": at // 8, "x": (at // 2) % 4, "c": at % 2, "y": (y + t + 4) % 4}

    offs = [(d, t) for d in range(3) for t in range(4)][1:]
    group = [decode(p, ("c", "y")) for p in range(1, 8)]
    places = [along(d, -t) for d, t in offs] + [moved(me, off, -1) for off in group]
    barrier = greet_all(places)
    pl.semaphore_wait(barrier, len(places))
    waits = []

    def to_twin(src, out, sem):
        remote(src, out.at[c], send_sem.at[sem], recv_sem.at[sem], twin).start()
        waits.append(remote(src, out.at[1 - c], send_sem.at[sem], recv_sem.at[sem], twin))
        own = pltpu.make_async_copy(src, out.at[c], local_sem.at[sem])
        own.start()
        waits.append(own)

    to_twin(normed, a_all, 0)
    to_twin(ob, ob_all, 1)
    scale = HD**-0.5
    dub = du_all[pl.ds(pl.multiple_of(c * TOK, TOK), TOK), :]
    dob = dot(dub, woT[...], NN).astype(BF)
    p = probs[...]
    dp_ = dot(dob, vb[...], NT)
    ds = (p * (dp_ - jnp.sum(p * dp_, axis=-1, keepdims=True))).astype(BF)
    part[:, pl.ds(0, HD)] = (dot(ds, qr[...], TN) * scale).astype(BF)
    part[:, pl.ds(HD, HD)] = dot(p.astype(BF), dob, TN).astype(BF)
    own = pltpu.make_async_copy(part.at[pl.ds(pl.multiple_of(2 * TOK + y * QTOK, QTOK), QTOK)], got.at[0, y], local_sem.at[2])
    own.start()
    halo_waits = []
    for i, (d, t) in enumerate(offs):
        target = along(-d, t)
        src = part.at[pl.ds(pl.multiple_of((2 - d) * TOK + target["y"] * QTOK, QTOK), QTOK)]
        sems = (send_sem.at[3 + i], recv_sem.at[3 + i])
        remote(src, got.at[d, y], *sems, target).start()
        halo_waits.append(remote(src, got.at[d, (y + 4 - t) % 4], *sems, target))
    raw = q_raw[...]
    dqr = dot(ds, kr[...], NN) * scale
    here = pl.ds(2 * TOK, TOK)
    dq, dg = rms_back(raw, gq[...], inv_rms(raw), unrot(dqr, cosine[here, :], sine[here, :]))
    dgq[...] = dg
    dq_all[c] = dq.astype(BF)
    remote(dq_all.at[c], dq_all.at[c], send_sem.at[2], recv_sem.at[2], twin).start()
    waits.append(remote(dq_all.at[c], dq_all.at[1 - c], send_sem.at[2], recv_sem.at[2], twin))
    own.wait()
    for w in halo_waits:
        w.wait()
    total = got[0, 0].astype(F32)
    for i in range(1, 12):
        total = total + got[i // 4, i % 4].astype(F32)
    k = k_own[pl.ds(pl.multiple_of(y * QTOK, QTOK), QTOK), :]
    rows = pl.ds(pl.multiple_of(2 * TOK + y * QTOK, QTOK), QTOK)
    dk, dg = rms_back(k, gk[...], inv_rms(k), unrot(total[:, :HD], cosine[rows, :], sine[rows, :]))
    dgk[...] = dg
    dkvb[:, pl.ds(0, HD)] = dk.astype(BF)
    dkvb[:, pl.ds(HD, HD)] = total[:, HD:].astype(BF)
    own = pltpu.make_async_copy(dkvb, dkv_all.at[c, y], local_sem.at[3])
    own.start()
    waits.append(own)
    for i, off in enumerate(group):
        target, source = moved(me, off, 1), moved(me, off, -1)
        sems = (send_sem.at[14 + i], recv_sem.at[14 + i])
        remote(dkvb, dkv_all.at[c, y], *sems, target).start()
        waits.append(remote(dkvb, dkv_all.at[source["c"], source["y"]], *sems, target))
    for w in waits:
        w.wait()


def attention_back(cid, *args):
    vmem = pl.BlockSpec(memory_space=pltpu.VMEM)
    shapes = [
        ((2, 4, QTOK, 512), BF),
        ((2, TOK, D), BF),
        ((2, TOK, HD), BF),
        ((2, TOK, HD), BF),
        ((1, HD), F32),
        ((1, HD), F32),
    ]
    return pl.pallas_call(
        attention_back_body,
        out_shape=[jax.ShapeDtypeStruct(s, t) for s, t in shapes],
        in_specs=[vmem] * len(args),
        out_specs=[vmem] * len(shapes),
        scratch_shapes=[
            pltpu.VMEM((3 * TOK, 512), BF),
            pltpu.VMEM((3, 4, QTOK, 512), BF),
            pltpu.VMEM((QTOK, 512), BF),
            pltpu.SemaphoreType.DMA((21,)),
            pltpu.SemaphoreType.DMA((21,)),
            pltpu.SemaphoreType.DMA((4,)),
        ],
        compiler_params=pltpu.CompilerParams(
            collective_id=cid, has_side_effects=True, vmem_limit_bytes=40 * 1024 * 1024
        ),
    )(*args)


def ffn_back_body(grads, gate, up, dense, dgate, dup, part):
    inner = math.sqrt(2.0 / math.pi)

    def body(i, carry):
        rows = pl.ds(pl.multiple_of(i * TOK, TOK), TOK)
        dz = dot(grads[rows, :], dense[2], NN)
        g = gate[rows, :]
        th = jnp.tanh(inner * (g + 0.044715 * g * g * g))
        slope = 0.5 * (1.0 + th) + 0.5 * g * (1.0 - th * th) * inner * (1.0 + 3 * 0.044715 * g * g)
        dg = (dz * up[rows, :] * slope).astype(BF)
        du = (dz * (0.5 * g * (1.0 + th))).astype(BF)
        dgate[rows, :] = dg
        dup[rows, :] = du
        part[rows, :] = (dot(dg, dense[0], NT) + dot(du, dense[1], NT)).astype(BF)
        return carry

    lax.fori_loop(0, 2, body, 0)


def ffn_backward(*args):
    vmem = pl.BlockSpec(memory_space=pltpu.VMEM)
    shapes = [(512, HALF), (512, HALF), (512, D)]
    return pl.pallas_call(
        ffn_back_body,
        out_shape=[jax.ShapeDtypeStruct(s, BF) for s in shapes],
        in_specs=[vmem] * 4,
        out_specs=[vmem] * 3,
        compiler_params=pltpu.CompilerParams(vmem_limit_bytes=48 * 1024 * 1024),
    )(*args)


def rope_tables():
    freqs = 10000.0 ** (-np.arange(128, dtype=np.float64) * 2.0 / 256)
    base = (np.arange(32, dtype=np.float64) - 2)[:, None] * 256 * freqs[None]
    step = np.arange(768, dtype=np.float64)[:, None] * freqs[None]
    return [t.astype(np.float32) for t in (np.cos(base), np.sin(base), np.cos(step), np.sin(step))]


def pack_body(gateup, downT, query, outputT, keyval, out, row):
    for m in range(3):
        row[:, pl.ds(0, FFT)] = gateup[m] if m < 2 else downT[...]
        row[:, pl.ds(FFT, FFP - FFT)] = jnp.zeros((ROWS, FFP - FFT), F32)
        for c in range(2):
            for x in range(4):
                out[8 * m + 2 * x + c] = row[:, pl.ds(HALF * c + BLK * x, BLK)].astype(BF)
    for x, half in enumerate((128, 128, 32, 32)):
        piece = (query[...], outputT[...], keyval[0], keyval[1])[x]
        row[:, pl.ds(0, 2 * half)] = piece
        for c in range(2):
            here = row[:, pl.ds(half * c, half)]
            out[24 + 2 * x + c, :, pl.ds(0, half)] = here.astype(BF)
            out[24 + 2 * x + c, :, pl.ds(half, BLK - half)] = jnp.zeros((ROWS, BLK - half), BF)


def to_columns(*args):
    vmem = pl.BlockSpec(memory_space=pltpu.VMEM)
    return pl.pallas_call(
        pack_body,
        out_shape=jax.ShapeDtypeStruct((32, ROWS, BLK), BF),
        in_specs=[vmem] * 5,
        out_specs=vmem,
        scratch_shapes=[pltpu.VMEM((ROWS, FFP), F32)],
        compiler_params=pltpu.CompilerParams(vmem_limit_bytes=32 * 1024 * 1024),
    )(*args)


def finish_body(*refs):
    o_got, w_got = refs[:2]
    weights, moms = refs[2:7], refs[7:12]
    new, nxt = refs[12:17], refs[17:22]
    row_o, row_w = refs[22:]

    def step(columns):
        return 0.15 * 0.2 * math.sqrt(max(D, columns))

    def update(i, m, width, columns):
        at = (m,) if m is not None else ()
        o, g = row_o[:, pl.ds(0, width)], row_w[:, pl.ds(0, width)]
        new[i][at + (slice(None), slice(None))] = weights[i][at + (slice(None), slice(None))] - step(columns) * o
        nxt[i][at + (slice(None), slice(None))] = 0.95 * moms[i][at + (slice(None), slice(None))] + g

    for m in range(3):
        for c in range(2):
            for x in range(4):
                here = pl.ds(HALF * c + BLK * x, BLK)
                row_o[:, here] = o_got[8 * m + 2 * x + c].astype(F32)
                row_w[:, here] = w_got[8 * m + 2 * x + c, :, pl.ds(0, BLK)].astype(F32)
        update(0 if m < 2 else 1, m if m < 2 else None, FFT, 6912)
    for x, half in enumerate((128, 128, 32, 32)):
        for c in range(2):
            here = pl.ds(half * c, half)
            row_o[:, here] = o_got[24 + 2 * x + c, :, pl.ds(0, half)].astype(F32)
            row_w[:, here] = w_got[24 + 2 * x + c, :, pl.ds(0, half)].astype(F32)
        update((2, 3, 4, 4)[x], (None, None, 0, 1)[x], 2 * half, 1024 if x < 2 else 256)


def finish(o_got, w_got, weights, moms):
    vmem = pl.BlockSpec(memory_space=pltpu.VMEM)
    out = pl.pallas_call(
        finish_body,
        out_shape=[jax.ShapeDtypeStruct(w.shape, F32) for w in weights] * 2,
        in_specs=[vmem] * 12,
        out_specs=[vmem] * 10,
        scratch_shapes=[pltpu.VMEM((ROWS, FFP), F32)] * 2,
        compiler_params=pltpu.CompilerParams(vmem_limit_bytes=32 * 1024 * 1024),
    )(o_got, w_got, *weights, *moms)
    return out[:5], out[5:]


def block_row(i, j):
    return 128 * (j * (j + 1) // 2 + i)


def chain_body(side, side_in, gram, mom, x, side_out, a, r, t, side_send, side_recv):
    me = place()
    places = side.places(me)
    barrier = greet_all(places)
    pl.semaphore_wait(barrier, len(places))
    side.start(me, side_in, side_out, side_send, side_recv)
    eye = lax.broadcasted_iota(jnp.int32, (128, 128), 0) == lax.broadcasted_iota(jnp.int32, (128, 128), 1)
    total = jnp.zeros((128, 128), F32)
    for i in range(D // 128):
        total = total + jnp.where(eye, gram[pl.ds(block_row(i, i), 128), :].astype(F32), 0.0)
    diag = jnp.sum(jnp.sum(total, axis=1, keepdims=True), axis=0, keepdims=True)
    inv = 1.0 / (jnp.sqrt(diag) + 1e-07)
    step = 384

    def by_rows(fn):
        def body(i, carry):
            fn(pl.ds(pl.multiple_of(i * step, step), step))
            return carry

        lax.fori_loop(0, D // step, body, 0)

    def poly(rows):
        low = a[rows, :]
        r[rows, :] = (COEF_TWO * low.astype(F32) + COEF_THREE * dot(low, a[...], NN)).astype(BF)

    def once(rows):
        low = a[rows, :]
        t[rows, :] = (COEF_ONE * low.astype(F32) + dot(low, r[...], NN)).astype(BF)

    def twice(rows):
        low = t[rows, :]
        a[rows, :] = (COEF_ONE * low.astype(F32) + dot(low, r[...], NN)).astype(BF)

    for j in range(D // 128):
        for i in range(j + 1):
            block = gram[pl.ds(block_row(i, j), 128), :].astype(F32) * (inv * inv)
            a[pl.ds(128 * i, 128), pl.ds(128 * j, 128)] = block.astype(BF)
            if i < j:
                a[pl.ds(128 * j, 128), pl.ds(128 * i, 128)] = block.T.astype(BF)
    x[...] = mom[...] * inv
    for i in range(3):
        by_rows(poly)
        x[...] = COEF_ONE * x[...] + dot(x[...].astype(BF), r[...], NN)
        if i < 2:
            by_rows(once)
            by_rows(twice)
    side.finish()


def orthogonal(gram, columns, side_in, cid):
    side = SideSwap()
    vmem = pl.BlockSpec(memory_space=pltpu.VMEM)
    hbm = pl.BlockSpec(memory_space=pl.ANY)
    return pl.pallas_call(
        functools.partial(chain_body, side),
        out_shape=[jax.ShapeDtypeStruct(columns.shape, F32), side.shape(side_in)],
        in_specs=[hbm, vmem, vmem],
        out_specs=[vmem, hbm],
        scratch_shapes=[pltpu.VMEM((D, D), BF)] * 3 + [pltpu.SemaphoreType.DMA((side.sems,))] * 2,
        compiler_params=pltpu.CompilerParams(
            collective_id=cid, has_side_effects=True, vmem_limit_bytes=48 * 1024 * 1024
        ),
    )(side_in, gram, columns)


def local(
    hidden_in,
    out_grad,
    segment_ids,
    w_query,
    w_keyval,
    w_output,
    w_gateup,
    w_down,
    norm_gains,
    qk_gains,
    mom_query,
    mom_keyval,
    mom_output,
    mom_gateup,
    mom_down,
    gain_moms,
    qk_moms,
):
    dp = lax.axis_index("dp")
    y = lax.axis_index("tensor")
    z, x, c = dp // 8, (dp // 2) % 4, dp % 2

    ffn_w = jnp.concatenate([w_gateup, w_down.T[None]], axis=0).astype(BF)
    ffn_w = jnp.pad(ffn_w, ((0, 0), (0, 0), (0, FFP - FFT))).reshape(3, ROWS, 2, HALF).transpose(2, 0, 1, 3)
    ffn_w = jnp.pad(ffn_w.reshape(2, 3 * ROWS, HALF), ((0, 0), (0, 4), (0, 0)))
    mom_downT, mom_outputT = mom_down.T, mom_output.T
    moms = to_columns(mom_gateup, mom_downT, mom_query, mom_outputT, mom_keyval)

    segs = jnp.pad(segment_ids.astype(F32).reshape(4, 64), ((0, ROWS - 4), (0, 0)))
    attn_w = jnp.stack(
        [
            jnp.concatenate([w_query, w_keyval[0], w_keyval[1]], axis=1),
            jnp.concatenate(
                [
                    w_output.T,
                    norm_gains.T,
                    jnp.broadcast_to(qk_gains.reshape(1, 4), (ROWS, 4)),
                    segs,
                    jnp.zeros((ROWS, 56), F32),
                ],
                axis=1,
            ),
        ]
    ).astype(BF)
    attn_w = jnp.pad(attn_w, ((0, 0), (0, 12), (0, 0)))
    attn_got = gather_plane(attn_w, 1)
    w_qkv, woT, gains, normed, q_raw, kv_piece = project(attn_got, hidden_in)
    g0, g1, g2, g3 = (gains[i : i + 1] for i in range(4))
    small = attn_got[:, :, :, 1, :4, 256:384].transpose(1, 2, 0, 3, 4).reshape(32, 4, 128)
    qk_mine = jnp.pad(small[:, 0, 4:8].reshape(32, 2, 2).transpose(1, 0, 2).reshape(2, 64), ((0, 14), (0, 64)))
    segs_all = small[:, :, 8:72].reshape(32, TOK).astype(jnp.int32)

    cos_b, sin_b, cos_s, sin_s = (jnp.asarray(t) for t in rope_tables())
    cb = lax.dynamic_slice_in_dim(cos_b, dp, 1, 0)
    sb = lax.dynamic_slice_in_dim(sin_b, dp, 1, 0)
    cosine = cb * cos_s - sb * sin_s
    sine = sb * cos_s + cb * sin_s

    kv_all, qk_all, ffn_near = halo([(kv_piece, "all"), (qk_mine, "near")], 1, 2, SideNear(), ffn_w)
    qk_full = qk_all[:, :2, :64].reshape(4, 2, 32, 2).transpose(1, 2, 0, 3).reshape(2, HD).astype(F32)
    gq, gk = qk_full[0:1], qk_full[1:2]
    order = np.arange(512)
    sort = np.zeros((512, 512), np.float32)
    sort[(order % 256) // 64 * 128 + order // 256 * 64 + order % 64, order] = 1.0
    first = jnp.maximum(dp - 2, 0)
    seg_rows = lax.dynamic_slice_in_dim(segs_all, first, 3, 0)
    seg_keys = jnp.where(
        dp >= 2, seg_rows, jnp.where(dp == 1, jnp.roll(seg_rows, 1, axis=0), jnp.roll(seg_rows, 2, axis=0))
    ).reshape(3 * TOK)
    seg_keys = jnp.where(jnp.arange(3 * TOK) >= (2 - dp) * TOK, seg_keys, -1)
    qr, kr, vb, k_own, probs, ob, u_part = attention(
        kv_all, jnp.asarray(sort, BF), q_raw, gq, gk, cosine, sine, segment_ids[:, None], seg_keys[None, :], woT
    )
    u_part = u_part.reshape(4, QTOK, D)
    hidden_q = lax.dynamic_slice_in_dim(hidden_in, y * QTOK, QTOK, 0)
    grad_q = lax.dynamic_slice_in_dim(out_grad, y * QTOK, QTOK, 0)
    u, hmid, bin_all, ffn_all = sum_then_gather(
        mid_fn, u_part, [hidden_q, g1, g2], [(QTOK, D)] * 2, 1, True, 3, SideGather(), ffn_near
    )

    bin_low = bin_all.reshape(512, D)
    dense, gate, up, mixed, f_part = ffn_forward(ffn_all.reshape(32, 112, HALF), bin_low)
    f_part = f_part.reshape(2, 4, QTOK, D)
    block, dg3, df_all, moms_all = sum_then_gather(
        ffn_out_fn, f_part, [hmid, grad_q, g3], [(QTOK, D), (1, D)], 1, True, 5, SideSwap(), moms
    )
    moms_cols = moms_all.reshape(D, BLK).T
    dfb = df_all.reshape(512, D)
    dgate, dup, dbin_part = ffn_backward(dfb, gate, up, dense)
    dbin_part = dbin_part.reshape(2, 4, QTOK, D)
    dhmid, dg1, dg2, du_all = sum_then_gather(
        ffn_in_fn,
        dbin_part,
        [hmid, u, grad_q, g1, g2],
        [(QTOK, D), (1, D), (1, D)],
        1,
        True,
        6,
    )

    dub_all = du_all.reshape(512, D)
    dkv_all, a_all, ob_all, dq_all, dgq, dgk = attention_back(
        7, dub_all, woT, vb, probs, kr, qr, q_raw, gq, gk, cosine, sine, k_own, normed, ob
    )
    dqb = lax.dynamic_slice_in_dim(dq_all, c, 1, 0)[0]
    dkv_all = dkv_all.reshape(512, 512)
    a_all, ob_all, dq_all = a_all.reshape(512, D), ob_all.reshape(512, HD), dq_all.reshape(512, HD)
    src, col = jnp.arange(512)[:, None], jnp.arange(128)[None, :]
    pick_y = (src == col // 64 * 256 + y * 64 + col % 64).astype(BF)
    col = col[:, :64]
    pick_c = (src == col // 32 * 256 + y * 64 + c * 32 + col % 32).astype(BF)
    dkv_mine = lax.dynamic_slice_in_dim(dkv_all, c * TOK, TOK, 0)
    dkv_y = dot(dkv_mine, pick_y, NN).astype(BF)
    dkv_cols = dot(dkv_all, pick_c, NN).astype(BF)
    da_part = (
        dot(
            jnp.concatenate([dqb, dkv_y], axis=1),
            w_qkv,
            NT,
        )
        .astype(BF)
        .reshape(4, QTOK, D)
    )
    dg0, last_in, last_out = sum_then_gather(
        last_fn, da_part, [hidden_q, dhmid, block, g0], [(1, D)], 2, False, 10
    )
    input_grad = last_in.reshape(TOK, D).astype(F32)
    block_out = last_out.reshape(TOK, D).astype(F32)

    gain_rows = jnp.concatenate(
        [dg0, dg1, dg2, dg3, jnp.concatenate([dgq, dgk, jnp.zeros((1, D - 2 * HD), F32)], axis=1)], axis=0
    ).astype(BF)

    ob_cols = lax.dynamic_slice_in_dim(ob_all, c * 128, 128, 1)
    dq_cols = lax.dynamic_slice_in_dim(dq_all, c * 128, 128, 1)
    d_gate = dot(dgate, bin_low, TN).astype(BF)
    d_up = dot(dup, bin_low, TN).astype(BF)
    d_down = dot(mixed, dfb, TN).astype(BF)
    d_q = dot(dq_cols, a_all, TN).astype(BF)
    d_kv = dot(dkv_cols, a_all, TN).astype(BF)
    d_o = dot(ob_cols, dub_all, TN).astype(BF)
    small = jnp.stack(
        [
            jnp.pad(d_q, ((0, BLK - 128), (0, 0))),
            jnp.pad(d_o, ((0, BLK - 128), (0, 0))),
            jnp.pad(d_kv[:32], ((0, BLK - 32), (0, 0))),
            jnp.concatenate([d_kv[32:], gain_rows, jnp.zeros((BLK - 37, D), BF)], axis=0),
        ]
    )
    wgrad = reduce_plane([d_gate.reshape(4, BLK, D), d_up.reshape(4, BLK, D), d_down.reshape(4, BLK, D), small], 11)

    kept = jnp.where((z == 3) & (x == 3), 32, BLK).reshape(1, 1)
    gram, gains_got, mom = gram_sum(kept, moms_cols, wgrad, wgrad[32:48].astype(BF), 13)
    gain_sum = jnp.sum(gains_got[:, :5].astype(F32), axis=0)
    gain_cols = jnp.concatenate(
        [
            gain_sum[:4].T.reshape(32, ROWS, 4),
            jnp.pad(
                gain_sum[4, : 2 * HD].reshape(2, 32, 4, 2)[:, :, y].transpose(1, 0, 2).reshape(32, 1, 4),
                ((0, 0), (0, ROWS - 1), (0, 0)),
            ),
        ],
        axis=2,
    )
    w_back = jnp.concatenate(
        [wgrad.astype(BF).T.reshape(32, ROWS, BLK), gain_cols.astype(BF), jnp.zeros((32, ROWS, 24), BF)], axis=2
    )
    ortho, w_got = orthogonal(gram.reshape(32 * PART, 128), mom, w_back, 12)
    gains_red = w_got[30, :, 224:228].T.astype(F32)
    qk_red = w_got[30, 0, 228:232].reshape(2, 2).astype(F32)
    o_back = ortho.astype(BF).T.reshape(32, ROWS, BLK)
    (o_got,) = exchange([(o_back, "a2a")], ("z", "x", "c"), 14)
    gain_rate = 2.0 / math.sqrt(8192)
    next_gain_moms = 0.9 * gain_moms + 0.1 * gains_red
    new_norm_gains = norm_gains - gain_rate * next_gain_moms
    next_qk_moms = 0.9 * qk_moms + 0.1 * qk_red
    new_qk_gains = qk_gains - gain_rate * next_qk_moms

    new, nxt = finish(
        o_got,
        w_got,
        [w_gateup, w_down.T, w_query, w_output.T, w_keyval],
        [mom_gateup, mom_downT, mom_query, mom_outputT, mom_keyval],
    )
    new_gateup, new_downT, new_query, new_outputT, new_keyval = new
    next_gateup, next_downT, next_query, next_outputT, next_keyval = nxt
    new_down, new_output, next_down, next_output = new_downT.T, new_outputT.T, next_downT.T, next_outputT.T
    return (
        block_out,
        input_grad,
        new_query,
        new_keyval,
        new_output,
        new_gateup,
        new_down,
        next_query,
        next_keyval,
        next_output,
        next_gateup,
        next_down,
        new_norm_gains,
        next_gain_moms,
        new_qk_gains,
        next_qk_moms,
    )


def solution(mesh):
    return jax.shard_map(
        local,
        mesh=mesh,
        in_specs=(
            P("dp", None),
            P("dp", None),
            P("dp"),
            P("dp", "tensor"),
            P(None, "dp", "tensor"),
            P("tensor", "dp"),
            P(None, "dp", "tensor"),
            P("tensor", "dp"),
            P(None, "dp"),
            P(None, ("dp", "tensor")),
            P("dp", "tensor"),
            P(None, "dp", "tensor"),
            P("tensor", "dp"),
            P(None, "dp", "tensor"),
            P("tensor", "dp"),
            P(None, "dp"),
            P(None, ("dp", "tensor")),
        ),
        out_specs=(
            P("dp", None),
            P("dp", None),
            P("dp", "tensor"),
            P(None, "dp", "tensor"),
            P("tensor", "dp"),
            P(None, "dp", "tensor"),
            P("tensor", "dp"),
            P("dp", "tensor"),
            P(None, "dp", "tensor"),
            P("tensor", "dp"),
            P(None, "dp", "tensor"),
            P("tensor", "dp"),
            P(None, "dp"),
            P(None, "dp"),
            P(None, ("dp", "tensor")),
            P(None, ("dp", "tensor")),
        ),
        check_vma=False,
    )
```
